32 devices in a mesh: head: 4 (over x, core), track: 8 (over z, y).
Axes of the slice: x: 2, y: 2, z: 4, core: 2. Of those that a mesh axis runs over, the one named last changes fastest.
Arguments:
- potential: float32 [256, 1024, 128], P('head', 'track'), may hold values from -6 to 6
- source: float32 [256, 1024, 128], P('head', 'track'), may hold values from -6 to 6
- depth_kernel: float32 [3, 128], replicated, may hold values from -0.5 to 0.5
- magnet: float32 [3, 8, 16384], P(None, 'track', 'head'), may hold values from -0.8 to 0.8
- footprint: int32 [8, 16384], P('track', 'head'), may hold values from 0 to 65535, as said below
- temp_index: int32 [8, 16384], P('track', 'head'), may hold values from 0 to 127
- temp_profile: float32 [128], replicated, may hold values from 0.3 to 1.4
- self_tiles: float32 [8, 128, 128, 128], P('track', 'head'), may hold values from -0.5 to 0.5
- next_tiles: float32 [8, 128, 128, 128], P('track', 'head'), may hold values from -0.5 to 0.5
Outputs:
- relaxed: float32 [256, 1024, 128], P('head', 'track')
- magnet_out: float32 [3, 8, 16384], P(None, 'track', 'head')
The draws below stay inside these ranges and needn't reach their ends.
Inputs may be any that keep to these rules, and one draw needn't show every extreme that they name: Within the 4096 grains of one device (an aligned block of a track tile), no more than 1024 have footprint cells in any one pole block of 8192 cells; in every draw one pole block, the same for every device, takes exactly 1024 grains of every device.
All inputs are finite; a program needn't handle non-finite values.
Results may differ from the reference program's by a relative error of at most 0.0001.
Values sent between devices are 32-bit elements; how exact they have to be, the bound alone decides.
No kernel may reach another device: no remote copies, remote signals or barrier semaphores. Data moves between devices by JAX's collectives and lax.ppermute only.
A program may use at most 320 MiB of HBM per device.

```python
import jax
import jax.numpy as jnp
from jax import lax

HX = 64
HY = 128
HZ = 128
GRAIN_DEV = 4096
TILE = 128
NTEMP = 128
NX = 256
NY = 1024
GRAINS_TRACK = 16384
TILES_TRACK = 128
SURFACE_ALL = 65536
CAP = 1024
N_HEAD = 4
N_TRACK = 8


def draw_footprint(key, part):
    blocks = N_TRACK * N_HEAD
    key_hot, key_perm, key_step, key_cell = jax.random.split(key, 4)
    hot = jax.random.randint(key_hot, (), 0, N_TRACK, dtype=jnp.int32)
    perm_keys = jax.random.split(key_perm, blocks)
    orders = jax.vmap(lambda sub: jax.random.permutation(sub, GRAIN_DEV))(perm_keys).astype(jnp.int32)
    ranks = jnp.argsort(orders, axis=1, stable=True).astype(jnp.int32)
    rest = ranks - CAP
    step_add = jax.random.randint(key_step, (blocks, GRAIN_DEV), 0, 2, dtype=jnp.int32)
    other = (rest + step_add) % (N_TRACK - 1)
    other = other + (other >= hot).astype(jnp.int32)
    owner = jnp.where(ranks < CAP, hot, other)
    offset = jax.random.randint(key_cell, (blocks, GRAIN_DEV), 0, HX * HY, dtype=jnp.int32)
    cells = owner * (HX * HY) + offset
    return cells.reshape(N_TRACK, N_HEAD * GRAIN_DEV).astype(jnp.int32)


def plant(array, key, least, high):
    dims = array.shape
    index_at = [jax.random.randint(jax.random.fold_in(key, axis), (), 0, dims[axis]) for axis in range(len(dims))]
    array = array.at[tuple(index_at)].set(least)
    longest = dims.index(max(dims))
    index_at[longest] = (index_at[longest] + 1) % dims[longest]
    return array.at[tuple(index_at)].set(high)


def block_levels(rng, extent, cuts, smallest, high):
    level = 1.0
    for dim, blocks in cuts:
        heights = jax.random.uniform(jax.random.fold_in(jax.random.fold_in(rng, 6), dim), (blocks,), jnp.float32, smallest / len(cuts), high / len(cuts))
        level = level * jnp.repeat(jnp.exp(heights), extent[dim] // blocks).reshape((-1,) + (1,) * (len(extent) - 1 - dim))
    return level


def bell_draw(stream_key, dims, spread, limit, shards=(), kind=jnp.bfloat16):
    drawn = jax.random.normal(stream_key, dims, jnp.float32) * spread
    if len(shards) > 0:
        drawn = block_levels(stream_key, dims, shards, -0.22, 0.18) * drawn
    return jnp.clip(drawn, min=-limit, max=limit).astype(kind)


def setup_inputs(seed: int = 0) -> dict:
    key_list = jax.random.split(jax.random.key(seed), 10)
    potential = bell_draw(key_list[0], (NX, NY, HZ), 1.0, 6.0, ((0, 4), (1, 8)), jnp.float32)
    source = bell_draw(key_list[1], (NX, NY, HZ), 1.0, 6.0, ((0, 4), (1, 8)), jnp.float32)
    depth_kernel = bell_draw(key_list[2], (3, HZ), HZ ** -0.5, 0.5, (), jnp.float32)
    magnet = jnp.clip(jax.random.uniform(key_list[3], (3, N_TRACK, GRAINS_TRACK), jnp.float32, -0.8, 0.8) * block_levels(key_list[3], (3, N_TRACK, GRAINS_TRACK), ((1, 8), (2, 4)), -0.4, 0.0), -0.8, 0.8)
    footprint = draw_footprint(jax.random.fold_in(key_list[9], 71), 0)
    temp_index = plant(jax.random.randint(key_list[5], (N_TRACK, GRAINS_TRACK), 0, NTEMP), jax.random.fold_in(key_list[5], 1), 0, NTEMP - 1).astype(jnp.int32)
    temp_profile = jnp.clip(jax.random.uniform(key_list[6], (NTEMP,), jnp.float32, 0.3, 1.4), 0.3, 1.4)
    self_tiles = bell_draw(key_list[7], (N_TRACK, TILES_TRACK, TILE, TILE), TILE ** -0.5, 0.5, ((0, 8), (1, 4)), jnp.float32)
    next_tiles = bell_draw(key_list[8], (N_TRACK, TILES_TRACK, TILE, TILE), TILE ** -0.5, 0.5, ((0, 8), (1, 4)), jnp.float32)
    return dict(potential=potential, source=source, depth_kernel=depth_kernel, magnet=magnet, footprint=footprint, temp_index=temp_index, temp_profile=temp_profile, self_tiles=self_tiles, next_tiles=next_tiles)


HIGH = lax.Precision.HIGHEST


def relax_sweep(padded, source):
    center = padded[1:-1, 1:-1]
    deep = jnp.pad(center, ((0, 0), (0, 0), (1, 1)))
    others = [padded[2:, 1:-1], padded[:-2, 1:-1], padded[1:-1, 2:], padded[1:-1, :-2], deep[:, :, 2:], deep[:, :, :-2]]
    numer = source
    denom = jnp.ones_like(center)
    for other in others:
        differ = other - center
        perm = 1.0 + 4.0 / (1.0 + 4.0 * differ * differ)
        numer = numer + perm * differ
        denom = denom + perm
    return center + 0.8 * numer / denom


def cross_comp(a_vec, b_vec):
    return jnp.stack([a_vec[1] * b_vec[2] - a_vec[2] * b_vec[1], a_vec[2] * b_vec[0] - a_vec[0] * b_vec[2], a_vec[0] * b_vec[1] - a_vec[1] * b_vec[0]])


def llb_section(state, field, target):
    sq_norm = jnp.sum(state * state, axis=0)
    total = field + 0.5 * (1.0 - sq_norm / target) * state
    turn = cross_comp(state, total)
    damp = cross_comp(state, turn)
    along = jnp.sum(state * total, axis=0)
    return state + 0.1 * (-turn - 0.5 * damp + 0.3 * along * state)


def reference(potential, source, depth_kernel, magnet, footprint, temp_index, temp_profile, self_tiles, next_tiles):
    n_head = NX // HX
    n_track = NY // HY
    relaxed = potential
    for sweep_idx in range(2):
        padded = jnp.pad(relaxed, ((1, 1), (1, 1), (0, 0)))
        relaxed = relax_sweep(padded, source)
    surface = jnp.einsum('kz,xyz->kxy', depth_kernel, relaxed, precision=HIGH)
    table = surface.reshape(3, n_head, HX, n_track, HY).transpose(0, 1, 3, 2, 4).reshape(3, n_head, SURFACE_ALL)
    row_block = (jnp.arange(GRAINS_TRACK, dtype=jnp.int32) // GRAIN_DEV).astype(jnp.int32)
    row_block = jnp.broadcast_to(row_block[None, :], footprint.shape)
    applied = table[:, row_block, footprint]
    temp = temp_profile[temp_index]
    target = 0.05 + jnp.maximum(1.0 - temp, 0.0)
    state = magnet
    for section in range(2):
        tiles = state.reshape(3, n_track, TILES_TRACK, TILE)
        padded = jnp.pad(tiles, ((0, 0), (0, 0), (1, 1), (0, 0)))
        ex = jnp.einsum('tkij,ctkj->ctki', self_tiles, padded[:, :, 1:-1], precision=HIGH)
        ex = ex + jnp.einsum('tkij,ctkj->ctki', next_tiles, padded[:, :, :-2], precision=HIGH)
        ex = ex + jnp.einsum('tkji,ctkj->ctki', next_tiles, padded[:, :, 2:], precision=HIGH)
        ex = ex.reshape(3, n_track, GRAINS_TRACK)
        state = llb_section(state, applied + ex, target)
    return relaxed, state
```

```python
import math

import jax
import jax.numpy as jnp
from jax import lax
from jax.experimental import pallas as pl
from jax.experimental.pallas import tpu as pltpu
from jax.sharding import PartitionSpec as P

F32 = jnp.float32
BF16 = jnp.bfloat16
STRIP = 16
UNIT = 4
TOP = 8
LANES = 128
NT = (((1,), (1,)), ((), ()))
VM = pl.BlockSpec(memory_space=pltpu.VMEM)
SM = pl.BlockSpec(memory_space=pltpu.SMEM)
ANY = pl.BlockSpec(memory_space=pl.ANY)


def mm(a, b):
    return jnp.dot(a, b, preferred_element_type=F32)


def mm_nt(a, b):
    return lax.dot_general(a, b, NT, preferred_element_type=F32)


def split(v):
    hi = v.astype(BF16)
    return hi, (v - hi.astype(F32)).astype(BF16)


def cost(flops, moved):
    return pl.CostEstimate(flops=flops, bytes_accessed=moved, transcendentals=0)


def rcp(v):
    return pl.reciprocal(v, approx=True)


def flux(d):
    mu = 1.0 + rcp(0.25 + d * d)
    return mu * d, mu


def z_flux(c):
    lane = lax.broadcasted_iota(jnp.int32, c.shape, c.ndim - 1)
    n = c.shape[-1]
    zl = jnp.where(lane == 0, 0.0, pltpu.roll(c, 1, c.ndim - 1))
    zr = jnp.where(lane == n - 1, 0.0, pltpu.roll(c, n - 1, c.ndim - 1))
    fl, ml = flux(zl - c)
    fr, mr = flux(zr - c)
    return fl + fr, ml + mr


def both(v):
    hi = v.astype(jnp.bfloat16).astype(jnp.float32)
    return jnp.concatenate([hi, v - hi], axis=0).astype(jnp.bfloat16)


def finish(c, numer, denom):
    return c + 0.8 * (numer * rcp(denom))


def relax_call(nx, ny, nz):
    chunk = UNIT
    rows = ny + 2 * TOP

    def kernel(flags, p_hbm, s_hbm, hlo, hhi, tlo, thi, own_lo, own_hi, kern, o_hbm, table,
               pe, q, sb, ob, fx1, mx1, fx2, mx2, fy1, my1, fy2, my2, psem, ssem, osem):
        n_chunk = nx // chunk

        def pcopy(c):
            return pltpu.make_async_copy(p_hbm.at[pl.ds(c * chunk, chunk)],
                                         pe.at[pl.ds(2 + c * chunk, chunk), pl.ds(TOP, ny)], psem.at[c])

        def scopy(c):
            return pltpu.make_async_copy(s_hbm.at[pl.ds(c * chunk, chunk)],
                                         sb.at[pl.ds(1 + c * chunk, chunk)], ssem.at[c])

        def ocopy(c):
            return pltpu.make_async_copy(ob.at[pl.ds(c * chunk + UNIT, chunk)],
                                         o_hbm.at[pl.ds(c * chunk, chunk)], osem.at[c])

        for c in range(n_chunk):
            pcopy(c).start()
            scopy(c).start()

        has = [flags[n] > 0 for n in range(4)]

        def keep(flag, v):
            return jnp.where(flag, v, 0.0)

        main = pl.ds(TOP, ny)
        for at, ref, first in ((0, hlo, 0), (1, hlo, ny), (nx + 2, hhi, 0), (nx + 3, hhi, ny)):
            pe[at, main, :] = keep(has[0 if at < 2 else 1], ref[pl.ds(first, ny), :])
        sb[0, :, :] = hlo[pl.ds(2 * ny, ny), :]
        sb[nx + 1, :, :] = hhi[pl.ds(2 * ny, ny), :]
        pe2 = pe.reshape((nx + 4) * rows, nz)
        q2 = q.reshape((nx + 2) * rows, nz)
        for side, (ref, own, row) in enumerate(((tlo, own_lo, TOP - 1), (thi, own_hi, TOP + ny))):
            flag = has[2 + side]
            c = keep(flag, ref[pl.ds(0, nx), :])
            far = keep(flag, ref[pl.ds(nx, nx), :])
            src = ref[pl.ds(2 * nx, nx), :]
            near = own[pl.ds(0, nx), :]
            corners = keep(flag, ref[pl.ds(3 * nx, 8), :])
            below = keep(has[0], corners[0:1])
            above = keep(has[1], corners[1:2])
            ix = lax.broadcasted_iota(jnp.int32, c.shape, 0)
            xl = jnp.where(ix == 0, below, pltpu.roll(c, 1, 0))
            xr = jnp.where(ix == nx - 1, above, pltpu.roll(c, nx - 1, 0))
            numer, denom = z_flux(c)
            numer = numer + src
            denom = denom + 1.0
            for other in (far, near, xl, xr):
                f, mu = flux(other - c)
                numer = numer + f
                denom = denom + mu
            pe2[pl.ds(2 * rows + row, nx, stride=rows), :] = c
            pe2[pl.ds(rows + row, 1), :] = below
            pe2[pl.ds((nx + 2) * rows + row, 1), :] = above
            q2[pl.ds(rows + row, nx, stride=rows), :] = keep(flag, finish(c, numer, denom))

        def sweep(a, x, planes, fx, mx, fy, my, src, store):
            for u in range(planes):
                f, mu = flux(a[x + u, pl.ds(1, TOP), :] - a[x + u, pl.ds(0, TOP), :])
                fy[u, pl.ds(0, TOP), :] = f
                my[u, pl.ds(0, TOP), :] = mu
            for k in range(ny // STRIP):
                here = pl.ds(TOP + k * STRIP, STRIP)
                before = pl.ds(TOP + k * STRIP - 1, STRIP)
                after = pl.ds(TOP + k * STRIP + 1, STRIP)
                flat = pl.ds(k * STRIP, STRIP)
                c = a[x, here, :]
                fp = fx[flat, :]
                mp = mx[flat, :]
                for u in range(planes):
                    up = a[x + u + 1, here, :]
                    f, mu = flux(up - c)
                    numer = f - fp
                    denom = mu + mp
                    fp, mp = f, mu
                    f, mu = flux(a[x + u, after, :] - c)
                    fy[u, here, :] = f
                    my[u, here, :] = mu
                    numer = numer + (f - fy[u, before, :])
                    denom = denom + (mu + my[u, before, :])
                    f, mu = z_flux(c)
                    numer = numer + (f + src[u, flat, :])
                    denom = denom + (mu + 1.0)
                    store(u, k, finish(c, numer, denom))
                    c = up
                fx[flat, :] = fp
                mx[flat, :] = mp

        def first_x(a, x, fx, mx):
            for k in range(ny // STRIP):
                here = pl.ds(TOP + k * STRIP, STRIP)
                flat = pl.ds(k * STRIP, STRIP)
                f, mu = flux(a[x + 1, here, :] - a[x, here, :])
                fx[flat, :] = f
                mx[flat, :] = mu

        def sweep1(x, planes, flag=None):
            def store(u, k, v):
                q[x + u + 1, pl.ds(TOP + k * STRIP, STRIP), :] = v if flag is None else keep(flag, v)

            sweep(pe, x + 2, planes, fx1, mx1, fy1, my1, sb.at[pl.ds(x + 1, planes)], store)

        kk = both(kern[...])

        def sweep2(x, planes):
            def store(u, k, v):
                ob[x + u + UNIT, pl.ds(k * STRIP, STRIP), :] = v

            sweep(q, x + 1, planes, fx2, mx2, fy2, my2, sb.at[pl.ds(x + 1, planes)], store)

        def surface(x, planes):
            nt = (((1,), (1,)), ((), ()))
            for u in range(planes):
                v = ob[x + u + UNIT]
                hi = v.astype(jnp.bfloat16)
                lo = (v - hi.astype(jnp.float32)).astype(jnp.bfloat16)
                a = lax.dot_general(kk, hi, nt, preferred_element_type=jnp.float32)
                b = lax.dot_general(kk, lo, nt, preferred_element_type=jnp.float32)
                table[x + u + UNIT] = (a[8:16] + b[0:8]) + a[0:8]

        n_unit = nx // UNIT
        pcopy(0).wait()
        scopy(0).wait()
        first_x(pe, 0, fx1, mx1)
        sweep1(-1, 1, has[0])
        sweep1(0, 1)
        first_x(q, 0, fx2, mx2)
        pcopy(1).wait()
        scopy(1).wait()
        sweep1(1, UNIT)

        def body(b, _):
            @pl.when(b < n_unit - 1)
            def _():
                pcopy(b + 1).wait()
                scopy(b + 1).wait()

            surface((b - 2) * UNIT, UNIT)
            sweep2((b - 1) * UNIT, UNIT)
            sweep1(b * UNIT + 1, UNIT)
            ocopy(b - 1).start()
            return 0

        lax.fori_loop(1, n_unit, body, 0)

        @pl.when(jnp.logical_not(has[1]))
        def _():
            q[nx + 1] = jnp.zeros_like(q[nx + 1])

        surface(nx - 2 * UNIT, UNIT)
        sweep2(nx - UNIT, UNIT)
        ocopy(n_unit - 1).start()
        surface(nx - UNIT, UNIT)
        for c in range(n_chunk):
            ocopy(c).wait()

    f32 = jnp.float32
    vm = pl.BlockSpec(memory_space=pltpu.VMEM)
    hbm = pl.BlockSpec(memory_space=pl.ANY)
    plane = pltpu.VMEM((ny, nz), f32)
    edge = pltpu.VMEM((UNIT, rows, nz), f32)
    return pl.pallas_call(
        kernel,
        out_shape=(jax.ShapeDtypeStruct((nx, ny, nz), f32), jax.ShapeDtypeStruct((nx + UNIT, 8, ny), f32)),
        in_specs=[pl.BlockSpec(memory_space=pltpu.SMEM), hbm, hbm] + [vm] * 7,
        out_specs=(hbm, vm),
        scratch_shapes=[
            pltpu.VMEM((nx + 4, rows, nz), f32), pltpu.VMEM((nx + 2, rows, nz), f32),
            pltpu.VMEM((nx + 2, ny, nz), f32), pltpu.VMEM((nx + UNIT, ny, nz), f32),
            plane, plane, plane, plane, edge, edge, edge, edge,
            pltpu.SemaphoreType.DMA((nx // chunk,)), pltpu.SemaphoreType.DMA((nx // chunk,)),
            pltpu.SemaphoreType.DMA((nx // chunk,)),
        ],
        compiler_params=pltpu.CompilerParams(vmem_limit_bytes=40 * 2**20),
        cost_estimate=pl.CostEstimate(flops=nx * ny * nz * 100, bytes_accessed=nx * ny * nz * 12, transcendentals=nx * ny * nz * 10),
        name="relax",
    )


def pack_call(nx, ny, nz, n_tiles):
    def kernel(p_hbm, s_hbm, m_ref, head_lo, head_hi, track_lo, track_hi, p_lo, p_hi, s_lo, s_hi, sem):
        planes = [
            (p_hbm, 0, head_lo, 0), (p_hbm, 1, head_lo, 1), (s_hbm, 0, head_lo, 2),
            (p_hbm, nx - 2, head_hi, 0), (p_hbm, nx - 1, head_hi, 1), (s_hbm, nx - 1, head_hi, 2),
        ]
        copies = [
            pltpu.make_async_copy(src.at[at], dst.at[pl.ds(n * ny, ny)], sem.at[i])
            for i, (src, at, dst, n) in enumerate(planes)
        ]
        rows = [(p_hbm, 0, p_lo), (p_hbm, ny - 8, p_hi), (s_hbm, 0, s_lo), (s_hbm, ny - 8, s_hi)]
        copies += [
            pltpu.make_async_copy(src.at[:, pl.ds(at, 8)], dst, sem.at[6 + i])
            for i, (src, at, dst) in enumerate(rows)
        ]
        for copy in copies:
            copy.start()
        head_lo[pl.ds(3 * ny, 8), :] = jnp.zeros((8, nz), F32)
        head_hi[pl.ds(3 * ny, 8), :] = jnp.zeros((8, nz), F32)
        for c in range(3):
            head_lo[pl.ds(3 * ny + c, 1), :] = m_ref[pl.ds(c * n_tiles, 1), :]
            head_hi[pl.ds(3 * ny + c, 1), :] = m_ref[pl.ds((c + 1) * n_tiles - 1, 1), :]
        for copy in copies[6:]:
            copy.wait()
        for out, p_ref, s_ref, order in ((track_lo, p_lo, s_lo, (0, 1)), (track_hi, p_hi, s_hi, (7, 6))):
            p2 = p_ref.reshape(nx * 8, nz)
            s2 = s_ref.reshape(nx * 8, nz)
            out[pl.ds(0, nx), :] = p2[pl.ds(order[0], nx, stride=8), :]
            out[pl.ds(nx, nx), :] = p2[pl.ds(order[1], nx, stride=8), :]
            out[pl.ds(2 * nx, nx), :] = s2[pl.ds(order[0], nx, stride=8), :]
            out[pl.ds(3 * nx, 8), :] = jnp.zeros((8, nz), F32)
        for copy in copies[:6]:
            copy.wait()

    head = jax.ShapeDtypeStruct((3 * ny + 8, nz), F32)
    track = jax.ShapeDtypeStruct((3 * nx + 8, nz), F32)
    eight = pltpu.VMEM((nx, 8, nz), F32)
    return pl.pallas_call(
        kernel,
        out_shape=(head, head, track, track),
        in_specs=[ANY, ANY, VM],
        out_specs=(VM,) * 4,
        scratch_shapes=[eight] * 4 + [pltpu.SemaphoreType.DMA((10,))],
        compiler_params=pltpu.CompilerParams(vmem_limit_bytes=16 * 2**20),
        cost_estimate=cost(10**6, 4 * 2**20),
        name="pack",
    )


def corner_call(nx, ny, nz):
    def kernel(lo_in, hi_in, below, above, lo, hi):
        for src, dst, row in ((lo_in, lo, 0), (hi_in, hi, ny - 1)):
            dst[pl.ds(0, 3 * nx), :] = src[pl.ds(0, 3 * nx), :]
            dst[pl.ds(3 * nx, 8), :] = jnp.zeros((8, nz), F32)
            dst[pl.ds(3 * nx, 1), :] = below[pl.ds(ny + row, 1), :]
            dst[pl.ds(3 * nx + 1, 1), :] = above[pl.ds(row, 1), :]

    track = jax.ShapeDtypeStruct((3 * nx + 8, nz), F32)
    return pl.pallas_call(
        kernel, out_shape=(track, track), in_specs=[VM] * 4, out_specs=(VM, VM),
        compiler_params=pltpu.CompilerParams(vmem_limit_bytes=16 * 2**20),
        cost_estimate=cost(10**5, 2**20), name="corners",
    )


def request_call(n_track, n_tiles, cells, width, cap):
    slot_rows = n_track * cap // LANES

    def kernel(foot, index, profile, requests, slots, target):
        fp = foot[...]
        owner = lax.shift_right_logical(fp, int(math.log2(cells)))
        cell = fp & (cells - 1)
        marks = [(owner == o).astype(F32) for o in range(n_track)]
        stacked = jnp.concatenate(marks, axis=0).astype(BF16)
        row = lax.broadcasted_iota(jnp.int32, (LANES, LANES), 0)
        col = lax.broadcasted_iota(jnp.int32, (LANES, LANES), 1)
        within = mm(stacked, (row < col).astype(F32).astype(BF16))
        totals = mm(stacked, jnp.ones((LANES, LANES), BF16)).astype(BF16)
        t_row = lax.broadcasted_iota(jnp.int32, (n_tiles, n_tiles), 0)
        t_col = lax.broadcasted_iota(jnp.int32, (n_tiles, n_tiles), 1)
        lower = (t_col < t_row).astype(F32).astype(BF16)
        rank = jnp.zeros((n_tiles, LANES), F32)
        for o in range(n_track):
            part = slice(o * n_tiles, (o + 1) * n_tiles)
            rank = rank + marks[o] * (within[part] + mm(lower, totals[part]))
        slot = owner * cap + rank.astype(jnp.int32)
        slots[...] = slot
        at_row = lax.shift_right_logical(slot, int(math.log2(LANES)))
        at_lane = slot & (LANES - 1)
        high = lax.shift_right_logical(cell, int(math.log2(width))).astype(F32)
        low = (cell & (width - 1)).astype(F32)
        rows = lax.broadcasted_iota(jnp.int32, (slot_rows, LANES), 0)
        found = jnp.zeros((2 * slot_rows, LANES), F32)
        for k in range(n_tiles):
            here = rows == at_row[k : k + 1]
            values = jnp.concatenate(
                [jnp.where(here, high[k : k + 1], 0.0), jnp.where(here, low[k : k + 1], 0.0)], axis=0
            ).astype(BF16)
            lanes = (row == at_lane[k : k + 1]).astype(F32).astype(BF16)
            found = found + mm_nt(values, lanes)
        requests[...] = found[:slot_rows] * float(width) + found[slot_rows:]
        spread = jnp.broadcast_to(profile[...], (n_tiles, profile.shape[1]))
        temp = jnp.take_along_axis(spread, index[...], axis=1)
        target[...] = 0.05 + jnp.maximum(1.0 - temp, 0.0)

    tiles = (n_tiles, LANES)
    return pl.pallas_call(
        kernel,
        out_shape=(
            jax.ShapeDtypeStruct((slot_rows, LANES), F32),
            jax.ShapeDtypeStruct(tiles, jnp.int32),
            jax.ShapeDtypeStruct(tiles, F32),
        ),
        in_specs=[VM] * 3,
        out_specs=(VM,) * 3,
        compiler_params=pltpu.CompilerParams(vmem_limit_bytes=16 * 2**20),
        cost_estimate=cost(10**8, 2**20),
        name="requests",
    )


def look_up(table, lane, row, rows, width):
    n = lane.shape[1]
    here = (lax.broadcasted_iota(jnp.int32, (width, n), 0) == lane).astype(F32).astype(BF16)
    got = mm(table, jnp.concatenate([here, here], axis=0))
    mine = lax.broadcasted_iota(jnp.int32, (rows, n), 0) == row
    return [
        jnp.sum(jnp.where(mine, got[c * rows : (c + 1) * rows], 0.0), axis=0, keepdims=True) for c in range(3)
    ]


def answer_call(n_track, cap, nx, ny):
    per = cap // LANES

    def kernel(requests, surface, reply, parts):
        flat = surface.reshape(surface.shape[0] * 8, ny)
        for c in range(3):
            hi, lo = split(flat[pl.ds((surface.shape[0] - nx) * 8 + c, nx, stride=8), :])
            parts[pl.ds(c * nx, nx), pl.ds(0, ny)] = hi
            parts[pl.ds(c * nx, nx), pl.ds(ny, ny)] = lo
        table = parts[...]
        group = 8 // per if per < 8 else 1

        def body(o, _):
            asked = requests[pl.ds(pl.multiple_of(o * group * per, 8), group * per), :].astype(jnp.int32)
            at_row = lax.shift_right_logical(asked, int(math.log2(ny)))
            at_lane = asked & (ny - 1)
            for j in range(group * per):
                values = look_up(table, at_lane[j : j + 1], at_row[j : j + 1], nx, ny)
                for c in range(3):
                    reply[o * group + j // per, pl.ds(c * per + j % per, 1), :] = values[c]
            return 0

        lax.fori_loop(0, n_track // group, body, 0)

    return pl.pallas_call(
        kernel,
        out_shape=jax.ShapeDtypeStruct((n_track, 3 * per, LANES), F32),
        in_specs=[VM, VM],
        out_specs=VM,
        scratch_shapes=[pltpu.VMEM((3 * nx, 2 * ny), BF16)],
        compiler_params=pltpu.CompilerParams(vmem_limit_bytes=16 * 2**20),
        cost_estimate=cost(10**9, 2**20),
        name="answer",
    )


def llb(m, field, target):
    sq = m[0] * m[0] + m[1] * m[1] + m[2] * m[2]
    pull = 0.5 * (1.0 - sq / target)
    h = [field[c] + pull * m[c] for c in range(3)]

    def cross(a, b):
        return [a[(c + 1) % 3] * b[(c + 2) % 3] - a[(c + 2) % 3] * b[(c + 1) % 3] for c in range(3)]

    turn = cross(m, h)
    damp = cross(m, turn)
    along = m[0] * h[0] + m[1] * h[1] + m[2] * h[2]
    return [m[c] + 0.1 * (0.3 * along * m[c] - turn[c] - 0.5 * damp[c]) for c in range(3)]


def fold(by_hi, by_lo):
    return (by_hi[8:16] + by_lo[0:8]) + by_hi[0:8]


def tile_major(m_ref, tiles_ref, n_tiles):
    tiles_ref[...] = jnp.zeros_like(tiles_ref)
    flat = tiles_ref.reshape((n_tiles + 2) * 8, LANES)
    for c in range(3):
        flat[pl.ds(8 + c, n_tiles, stride=8), :] = m_ref[pl.ds(c * n_tiles, n_tiles), :]


def exchange(tiles_ref, pair_hi, pair_lo, out_ref, k, n_tiles, at):
    mid = both(tiles_ref[k + 1])
    low = both(tiles_ref[k])
    high = both(tiles_ref[k + 2])
    here = jnp.concatenate([mid, low], axis=1)
    hi = pair_hi[at]
    lo = pair_lo[at]
    field = fold(mm_nt(here, hi), mm_nt(here, lo))
    field = field + fold(mm(high, hi[:, LANES:]), mm(high, lo[:, LANES:]))
    for c in range(3):
        out_ref[pl.ds(c * n_tiles + k, 1), :] = field[c : c + 1]


def first_call(n_tiles, ny):
    step = 8

    def kernel(flags, own, nxt, m_ref, below, above, pair_hi, pair_lo, ex, tiles):
        i = pl.program_id(0)

        @pl.when(i == 0)
        def _():
            tile_major(m_ref, tiles, n_tiles)
            tiles[0] = jnp.where(flags[0] > 0, below[pl.ds(3 * ny, 8), :], 0.0)
            tiles[n_tiles + 1] = jnp.where(flags[1] > 0, above[pl.ds(3 * ny, 8), :], 0.0)

        for j in range(step):
            for ref, lanes in ((own, pl.ds(0, LANES)), (nxt, pl.ds(LANES, LANES))):
                hi, lo = split(ref[j])
                pair_hi[j, :, lanes] = hi
                pair_lo[j, :, lanes] = lo
        for j in range(step):
            exchange(tiles, pair_hi, pair_lo, ex, i * step + j, n_tiles, j)

    tile = pl.BlockSpec((step, LANES, LANES), lambda i: (i, 0, 0))
    pair = pl.BlockSpec((step, LANES, 2 * LANES), lambda i: (i, 0, 0))
    return pl.pallas_call(
        kernel,
        grid=(n_tiles // step,),
        out_shape=(
            jax.ShapeDtypeStruct((n_tiles, LANES, 2 * LANES), BF16),
            jax.ShapeDtypeStruct((n_tiles, LANES, 2 * LANES), BF16),
            jax.ShapeDtypeStruct((3 * n_tiles, LANES), F32),
        ),
        in_specs=[SM, tile, tile, VM, VM, VM],
        out_specs=(pair, pair, VM),
        scratch_shapes=[pltpu.VMEM((n_tiles + 2, 8, LANES), F32)],
        compiler_params=pltpu.CompilerParams(vmem_limit_bytes=24 * 2**20),
        cost_estimate=cost(10**9, 8 * 2**20),
        name="couple_first",
    )


def section_call(n_tiles, n_track, cap):
    per = cap // LANES
    slot_rows = n_track * per

    def kernel(answers, slots, m_ref, ex, target, applied, m_out, edge_lo, edge_hi, parts):
        for c in range(3):
            rows = jnp.concatenate([answers[o, pl.ds(c * per, per), :] for o in range(n_track)], axis=0)
            hi, lo = split(rows)
            parts[pl.ds(c * slot_rows, slot_rows), pl.ds(0, LANES)] = hi
            parts[pl.ds(c * slot_rows, slot_rows), pl.ds(LANES, LANES)] = lo
        table = parts[...]
        slot = slots[...]
        at_row = lax.shift_right_logical(slot, int(math.log2(LANES)))
        at_lane = slot & (LANES - 1)
        for k in range(n_tiles):
            values = look_up(table, at_lane[k : k + 1], at_row[k : k + 1], slot_rows, LANES)
            for c in range(3):
                applied[pl.ds(c * n_tiles + k, 1), :] = values[c]
        part = [pl.ds(c * n_tiles, n_tiles) for c in range(3)]
        m = [m_ref[part[c], :] for c in range(3)]
        m = llb(m, [applied[part[c], :] + ex[part[c], :] for c in range(3)], target[...])
        edge_lo[...] = jnp.zeros((8, LANES), F32)
        edge_hi[...] = jnp.zeros((8, LANES), F32)
        for c in range(3):
            m_out[part[c], :] = m[c]
            edge_lo[pl.ds(c, 1), :] = m[c][0:1]
            edge_hi[pl.ds(c, 1), :] = m[c][n_tiles - 1 :]

    grains = jax.ShapeDtypeStruct((3 * n_tiles, LANES), F32)
    edge = jax.ShapeDtypeStruct((8, LANES), F32)
    return pl.pallas_call(
        kernel,
        out_shape=(grains, grains, edge, edge),
        in_specs=[VM] * 5,
        out_specs=(VM,) * 4,
        scratch_shapes=[pltpu.VMEM((3 * slot_rows, 2 * LANES), BF16)],
        compiler_params=pltpu.CompilerParams(vmem_limit_bytes=16 * 2**20),
        cost_estimate=cost(10**9, 2**20),
        name="section_first",
    )


def second_call(n_tiles):
    def kernel(pair_hi, pair_lo, m_ref, ex, tiles):
        tile_major(m_ref, tiles, n_tiles)
        for k in range(n_tiles):
            exchange(tiles, pair_hi, pair_lo, ex, k, n_tiles, k)

    return pl.pallas_call(
        kernel,
        out_shape=jax.ShapeDtypeStruct((3 * n_tiles, LANES), F32),
        in_specs=[VM] * 3,
        out_specs=VM,
        scratch_shapes=[pltpu.VMEM((n_tiles + 2, 8, LANES), F32)],
        compiler_params=pltpu.CompilerParams(vmem_limit_bytes=24 * 2**20),
        cost_estimate=cost(10**9, 4 * 2**20),
        name="couple_second",
    )


def last_call(n_tiles):
    def kernel(flags, m_ref, ex, applied, target, below, above, hi_first, lo_first, hi_last, lo_last, out):
        low = both(jnp.where(flags[0] > 0, below[...], 0.0))
        high = both(jnp.where(flags[1] > 0, above[...], 0.0))
        beside = slice(LANES, 2 * LANES)
        first = fold(mm_nt(low, hi_first[0][:, beside]), mm_nt(low, lo_first[0][:, beside]))
        last = fold(mm(high, hi_last[0][:, beside]), mm(high, lo_last[0][:, beside]))
        at = lax.broadcasted_iota(jnp.int32, (n_tiles, LANES), 0)
        field = []
        m = []
        for c in range(3):
            part = pl.ds(c * n_tiles, n_tiles)
            extra = jnp.where(at == 0, first[c : c + 1], 0.0) + jnp.where(at == n_tiles - 1, last[c : c + 1], 0.0)
            field.append(applied[part, :] + (ex[part, :] + extra))
            m.append(m_ref[part, :])
        m = llb(m, field, target[...])
        for c in range(3):
            out[pl.ds(c * n_tiles, n_tiles), :] = m[c]

    def at(k):
        return pl.BlockSpec((1, LANES, 2 * LANES), lambda i: (k, 0, 0))

    def full(shape):
        return pl.BlockSpec(shape, lambda i: (0, 0))

    grains = full((3 * n_tiles, LANES))
    edge = full((8, LANES))
    return pl.pallas_call(
        kernel,
        grid=(1,),
        out_shape=jax.ShapeDtypeStruct((3 * n_tiles, LANES), F32),
        in_specs=[SM, grains, grains, grains, full((n_tiles, LANES)), edge, edge,
                  at(0), at(0), at(n_tiles - 1), at(n_tiles - 1)],
        out_specs=grains,
        compiler_params=pltpu.CompilerParams(vmem_limit_bytes=16 * 2**20),
        cost_estimate=cost(10**7, 2**20),
        name="section_last",
    )


def shifted(v, axis, by):
    n = lax.axis_size(axis)
    return lax.ppermute(v, axis, [(i, (i + by) % n) for i in range(n)])


def per_device(
    potential, source, depth_kernel, magnet, footprint, temp_index, temp_profile, self_tiles, next_tiles
):
    nx, ny, nz = potential.shape
    n_track = lax.axis_size("track")
    n_tiles = self_tiles.shape[1]
    grains = footprint.shape[1]
    cap = 2 * grains // n_track
    h = lax.axis_index("head")
    t = lax.axis_index("track")
    flags = jnp.stack([h > 0, h < lax.axis_size("head") - 1, t > 0, t < n_track - 1]).astype(jnp.int32)
    state = magnet.reshape(3 * n_tiles, LANES)

    head_lo, head_hi, track_lo, track_hi = pack_call(nx, ny, nz, n_tiles)(potential, source, state)
    below = shifted(head_hi, "head", 1)
    above = shifted(head_lo, "head", -1)
    requests, slots, target = request_call(n_track, n_tiles, nx * ny, ny, cap)(
        footprint.reshape(n_tiles, LANES), temp_index.reshape(n_tiles, LANES), temp_profile[None, :]
    )
    track_lo, track_hi = corner_call(nx, ny, nz)(track_lo, track_hi, below, above)
    left = shifted(track_hi, "track", 1)
    right = shifted(track_lo, "track", -1)
    asked = lax.all_to_all(requests.reshape(n_track, cap // LANES, LANES), "track", 0, 0)

    kern = jnp.pad(depth_kernel, ((0, 5), (0, 0)))
    relaxed, surface = relax_call(nx, ny, nz)(
        flags, potential, source, below, above, left, right, track_lo, track_hi, kern
    )
    reply = answer_call(n_track, cap, nx, ny)(asked.reshape(n_track * cap // LANES, LANES), surface)
    answers = lax.all_to_all(reply, "track", 0, 0)

    pair_hi, pair_lo, ex = first_call(n_tiles, ny)(flags, self_tiles[0], next_tiles[0], state, below, above)
    applied, state, edge_lo, edge_hi = section_call(n_tiles, n_track, cap)(answers, slots, state, ex, target)
    tile_below = shifted(edge_hi, "head", 1)
    tile_above = shifted(edge_lo, "head", -1)
    ex = second_call(n_tiles)(pair_hi, pair_lo, state)
    state = last_call(n_tiles)(
        flags, state, ex, applied, target, tile_below, tile_above, pair_hi, pair_lo, pair_hi, pair_lo
    )
    return relaxed, state.reshape(3, 1, grains)


def solution(mesh):
    in_specs = (
        P("head", "track", None),
        P("head", "track", None),
        P(),
        P(None, "track", "head"),
        P("track", "head"),
        P("track", "head"),
        P(),
        P("track", "head", None, None),
        P("track", "head", None, None),
    )
    out_specs = (P("head", "track", None), P(None, "track", "head"))
    return jax.shard_map(
        per_device, mesh=mesh, in_specs=in_specs, out_specs=out_specs, check_vma=False
    )
```

```python
import math

import jax
import jax.numpy as jnp
from jax import lax
from jax.experimental import pallas as pl
from jax.experimental.pallas import tpu as pltpu
from jax.sharding import PartitionSpec as P

F32 = jnp.float32
BF16 = jnp.bfloat16
STRIP = 16
UNIT = 4
TOP = 8
AHEAD = 4
LANES = 128
SMALL = 16 * 2**20
LARGE = 52 * 2**20
NT = (((1,), (1,)), ((), ()))
VM = pl.BlockSpec(memory_space=pltpu.VMEM)
SM = pl.BlockSpec(memory_space=pltpu.SMEM)
HBM = pl.BlockSpec(memory_space=pltpu.HBM)


def mm(a, b):
    return jnp.dot(a, b, preferred_element_type=F32)


def mm_nt(a, b):
    return lax.dot_general(a, b, NT, preferred_element_type=F32)


def split(v):
    hi = v.astype(BF16)
    return hi, (v - hi.astype(F32)).astype(BF16)


def cost(flops, moved):
    return pl.CostEstimate(flops=flops, bytes_accessed=moved, transcendentals=0)


def rcp(v):
    return pl.reciprocal(v, approx=True)


def flux(d):
    mu = 1.0 + rcp(0.25 + d * d)
    return mu * d, mu


def z_flux(c):
    lane = lax.broadcasted_iota(jnp.int32, c.shape, c.ndim - 1)
    n = c.shape[-1]
    zl = jnp.where(lane == 0, 0.0, pltpu.roll(c, 1, c.ndim - 1))
    zr = jnp.where(lane == n - 1, 0.0, pltpu.roll(c, n - 1, c.ndim - 1))
    fl, ml = flux(zl - c)
    fr, mr = flux(zr - c)
    return fl + fr, ml + mr


def both(v):
    hi = v.astype(jnp.bfloat16).astype(jnp.float32)
    return jnp.concatenate([hi, v - hi], axis=0).astype(jnp.bfloat16)


def finish(c, numer, denom):
    return c + 0.8 * (numer * rcp(denom))


def relax_call(nx, ny, nz, n_track, cap):
    chunk = UNIT
    per = cap // LANES
    rows = ny + 2 * TOP

    def kernel(flags, p_hbm, s_hbm, hlo, hhi, tlo, thi, own_lo, own_hi, kern, requests, ex_hbm, o_hbm, reply,
               table, parts, pe, q, sb, ob, fx1, mx1, fx2, mx2, fy1, my1, fy2, my2, psem, ssem, osem):
        n_chunk = nx // chunk

        def pcopy(c):
            return pltpu.make_async_copy(p_hbm.at[pl.ds(c * chunk, chunk)],
                                         pe.at[pl.ds(2 + c * chunk, chunk), pl.ds(TOP, ny)], psem.at[c])

        def scopy(c):
            return pltpu.make_async_copy(s_hbm.at[pl.ds(c * chunk, chunk)],
                                         sb.at[pl.ds(1 + c * chunk, chunk)], ssem.at[c])

        def ocopy(c):
            return pltpu.make_async_copy(ob.at[pl.ds(c * chunk + UNIT, chunk)],
                                         o_hbm.at[pl.ds(c * chunk, chunk)], osem.at[c])

        def fetch(c):
            pcopy(c).start()
            scopy(c).start()

        for c in range(AHEAD):
            fetch(c)

        has = [flags[n] > 0 for n in range(4)]

        def keep(flag, v):
            return jnp.where(flag, v, 0.0)

        main = pl.ds(TOP, ny)
        for at, ref, first in ((0, hlo, 0), (1, hlo, ny), (nx + 2, hhi, 0), (nx + 3, hhi, ny)):
            pe[at, main, :] = keep(has[0 if at < 2 else 1], ref[pl.ds(first, ny), :])
        sb[0, :, :] = hlo[pl.ds(2 * ny, ny), :]
        sb[nx + 1, :, :] = hhi[pl.ds(2 * ny, ny), :]
        pe2 = pe.reshape((nx + 4) * rows, nz)
        q2 = q.reshape((nx + 2) * rows, nz)
        for side, (ref, own, row) in enumerate(((tlo, own_lo, TOP - 1), (thi, own_hi, TOP + ny))):
            flag = has[2 + side]
            c = keep(flag, ref[pl.ds(0, nx), :])
            far = keep(flag, ref[pl.ds(nx, nx), :])
            src = ref[pl.ds(2 * nx, nx), :]
            near = own[pl.ds(0, nx), :]
            corners = keep(flag, ref[pl.ds(3 * nx, 8), :])
            below = keep(has[0], corners[0:1])
            above = keep(has[1], corners[1:2])
            ix = lax.broadcasted_iota(jnp.int32, c.shape, 0)
            xl = jnp.where(ix == 0, below, pltpu.roll(c, 1, 0))
            xr = jnp.where(ix == nx - 1, above, pltpu.roll(c, nx - 1, 0))
            numer, denom = z_flux(c)
            numer = numer + src
            denom = denom + 1.0
            for other in (far, near, xl, xr):
                f, mu = flux(other - c)
                numer = numer + f
                denom = denom + mu
            pe2[pl.ds(2 * rows + row, nx, stride=rows), :] = c
            pe2[pl.ds(rows + row, 1), :] = below
            pe2[pl.ds((nx + 2) * rows + row, 1), :] = above
            q2[pl.ds(rows + row, nx, stride=rows), :] = keep(flag, finish(c, numer, denom))

        def sweep(a, x, planes, fx, mx, fy, my, src, store):
            for u in range(planes):
                f, mu = flux(a[x + u, pl.ds(1, TOP), :] - a[x + u, pl.ds(0, TOP), :])
                fy[u, pl.ds(0, TOP), :] = f
                my[u, pl.ds(0, TOP), :] = mu
            for k in range(ny // STRIP):
                here = pl.ds(TOP + k * STRIP, STRIP)
                before = pl.ds(TOP + k * STRIP - 1, STRIP)
                after = pl.ds(TOP + k * STRIP + 1, STRIP)
                flat = pl.ds(k * STRIP, STRIP)
                c = a[x, here, :]
                fp = fx[flat, :]
                mp = mx[flat, :]
                for u in range(planes):
                    up = a[x + u + 1, here, :]
                    f, mu = flux(up - c)
                    numer = f - fp
                    denom = mu + mp
                    fp, mp = f, mu
                    f, mu = flux(a[x + u, after, :] - c)
                    fy[u, here, :] = f
                    my[u, here, :] = mu
                    numer = numer + (f - fy[u, before, :])
                    denom = denom + (mu + my[u, before, :])
                    f, mu = z_flux(c)
                    numer = numer + (f + src[u, flat, :])
                    denom = denom + (mu + 1.0)
                    store(u, k, finish(c, numer, denom))
                    c = up
                fx[flat, :] = fp
                mx[flat, :] = mp

        def first_x(a, x, fx, mx):
            for k in range(ny // STRIP):
                here = pl.ds(TOP + k * STRIP, STRIP)
                flat = pl.ds(k * STRIP, STRIP)
                f, mu = flux(a[x + 1, here, :] - a[x, here, :])
                fx[flat, :] = f
                mx[flat, :] = mu

        def sweep1(x, planes, flag=None):
            def store(u, k, v):
                q[x + u + 1, pl.ds(TOP + k * STRIP, STRIP), :] = v if flag is None else keep(flag, v)

            sweep(pe, x + 2, planes, fx1, mx1, fy1, my1, sb.at[pl.ds(x + 1, planes)], store)

        kk = both(kern[...])

        def sweep2(x, planes):
            def store(u, k, v):
                ob[x + u + UNIT, pl.ds(k * STRIP, STRIP), :] = v

            sweep(q, x + 1, planes, fx2, mx2, fy2, my2, sb.at[pl.ds(x + 1, planes)], store)

        def surface(x, planes):
            nt = (((1,), (1,)), ((), ()))
            for u in range(planes):
                v = ob[x + u + UNIT]
                hi = v.astype(jnp.bfloat16)
                lo = (v - hi.astype(jnp.float32)).astype(jnp.bfloat16)
                a = lax.dot_general(kk, hi, nt, preferred_element_type=jnp.float32)
                b = lax.dot_general(kk, lo, nt, preferred_element_type=jnp.float32)
                table[x + u + UNIT] = (a[8:16] + b[0:8]) + a[0:8]

        n_unit = nx // UNIT
        pcopy(0).wait()
        scopy(0).wait()
        first_x(pe, 0, fx1, mx1)
        sweep1(-1, 1, has[0])
        sweep1(0, 1)
        first_x(q, 0, fx2, mx2)
        pcopy(1).wait()
        scopy(1).wait()
        sweep1(1, UNIT)

        def body(b, _):
            @pl.when(b + AHEAD <= n_unit)
            def _():
                fetch(b + AHEAD - 1)

            @pl.when(b < n_unit - 1)
            def _():
                pcopy(b + 1).wait()
                scopy(b + 1).wait()

            surface((b - 2) * UNIT, UNIT)
            sweep2((b - 1) * UNIT, UNIT)
            sweep1(b * UNIT + 1, UNIT)
            ocopy(b - 1).start()
            return 0

        lax.fori_loop(1, n_unit, body, 0)

        @pl.when(jnp.logical_not(has[1]))
        def _():
            q[nx + 1] = jnp.zeros_like(q[nx + 1])

        surface(nx - 2 * UNIT, UNIT)
        sweep2(nx - UNIT, UNIT)
        ocopy(n_unit - 1).start()
        surface(nx - UNIT, UNIT)

        flat = table.reshape((nx + UNIT) * 8, ny)
        for c in range(3):
            hi, lo = split(flat[pl.ds(UNIT * 8 + c, nx, stride=8), :])
            parts[pl.ds(c * nx, nx), pl.ds(0, ny)] = hi
            parts[pl.ds(c * nx, nx), pl.ds(ny, ny)] = lo
        asked = requests[...].astype(jnp.int32)

        def answer(j, values):
            for c in range(3):
                reply[j // per, pl.ds(c * per + j % per, 1), :] = values[c]

        look_up_all(parts[...], asked & (ny - 1), lax.shift_right_logical(asked, int(math.log2(ny))), nx, ny, answer)
        for c in range(n_chunk):
            ocopy(c).wait()

    f32 = jnp.float32
    vm = pl.BlockSpec(memory_space=pltpu.VMEM)
    hbm = pl.BlockSpec(memory_space=pltpu.HBM)
    plane = pltpu.VMEM((ny, nz), f32)
    edge = pltpu.VMEM((UNIT, rows, nz), f32)
    return pl.pallas_call(
        kernel,
        out_shape=(
            jax.ShapeDtypeStruct((nx, ny, nz), f32),
            jax.ShapeDtypeStruct((n_track, 3 * per, 128), f32),
        ),
        in_specs=[pl.BlockSpec(memory_space=pltpu.SMEM), hbm, hbm] + [vm] * 8 + [pl.BlockSpec(memory_space=pl.ANY)],
        out_specs=(hbm, vm),
        scratch_shapes=[
            pltpu.VMEM((nx + UNIT, 8, ny), f32), pltpu.VMEM((3 * nx, 2 * ny), jnp.bfloat16),
            pltpu.VMEM((nx + 4, rows, nz), f32), pltpu.VMEM((nx + 2, rows, nz), f32),
            pltpu.VMEM((nx + 2, ny, nz), f32), pltpu.VMEM((nx + UNIT, ny, nz), f32),
            plane, plane, plane, plane, edge, edge, edge, edge,
            pltpu.SemaphoreType.DMA((nx // chunk,)), pltpu.SemaphoreType.DMA((nx // chunk,)),
            pltpu.SemaphoreType.DMA((nx // chunk,)),
        ],
        compiler_params=pltpu.CompilerParams(vmem_limit_bytes=LARGE),
        cost_estimate=pl.CostEstimate(flops=nx * ny * nz * 100, bytes_accessed=nx * ny * nz * 12, transcendentals=nx * ny * nz * 10),
        name="relax",
    )


def pack_call(nx, ny, nz, n_tiles):
    def kernel(p_hbm, s_hbm, m_hbm, head_lo, head_hi, track_lo, track_hi, p_lo, p_hi, s_lo, s_hi, m_ends, sem):
        planes = [
            (p_hbm, 0, head_lo, 0), (p_hbm, 1, head_lo, 1), (s_hbm, 0, head_lo, 2),
            (p_hbm, nx - 2, head_hi, 0), (p_hbm, nx - 1, head_hi, 1), (s_hbm, nx - 1, head_hi, 2),
        ]
        copies = [
            pltpu.make_async_copy(src.at[at], dst.at[pl.ds(n * ny, ny)], sem.at[i])
            for i, (src, at, dst, n) in enumerate(planes)
        ]
        rows = [(p_hbm, 0, p_lo), (p_hbm, ny - 8, p_hi), (s_hbm, 0, s_lo), (s_hbm, ny - 8, s_hi)]
        copies += [
            pltpu.make_async_copy(src.at[:, pl.ds(at, 8)], dst, sem.at[6 + i])
            for i, (src, at, dst) in enumerate(rows)
        ]
        copies += [
            pltpu.make_async_copy(
                m_hbm.at[pl.ds(c * n_tiles + side * (n_tiles - 8), 8)], m_ends.at[2 * c + side], sem.at[10 + 2 * c + side]
            )
            for c in range(3)
            for side in range(2)
        ]
        for copy in copies:
            copy.start()
        head_lo[pl.ds(3 * ny, 8), :] = jnp.zeros((8, nz), F32)
        head_hi[pl.ds(3 * ny, 8), :] = jnp.zeros((8, nz), F32)
        for copy in copies[6:]:
            copy.wait()
        for c in range(3):
            head_lo[pl.ds(3 * ny + c, 1), :] = m_ends[2 * c, pl.ds(0, 1), :]
            head_hi[pl.ds(3 * ny + c, 1), :] = m_ends[2 * c + 1, pl.ds(7, 1), :]
        for out, p_ref, s_ref, order in ((track_lo, p_lo, s_lo, (0, 1)), (track_hi, p_hi, s_hi, (7, 6))):
            p2 = p_ref.reshape(nx * 8, nz)
            s2 = s_ref.reshape(nx * 8, nz)
            out[pl.ds(0, nx), :] = p2[pl.ds(order[0], nx, stride=8), :]
            out[pl.ds(nx, nx), :] = p2[pl.ds(order[1], nx, stride=8), :]
            out[pl.ds(2 * nx, nx), :] = s2[pl.ds(order[0], nx, stride=8), :]
            out[pl.ds(3 * nx, 8), :] = jnp.zeros((8, nz), F32)
        for copy in copies[:6]:
            copy.wait()

    head = jax.ShapeDtypeStruct((3 * ny + 8, nz), F32)
    track = jax.ShapeDtypeStruct((3 * nx + 8, nz), F32)
    eight = pltpu.VMEM((nx, 8, nz), F32)
    return pl.pallas_call(
        kernel,
        out_shape=(head, head, track, track),
        in_specs=[HBM] * 3,
        out_specs=(VM,) * 4,
        scratch_shapes=[eight] * 4 + [pltpu.VMEM((6, 8, LANES), F32), pltpu.SemaphoreType.DMA((16,))],
        compiler_params=pltpu.CompilerParams(vmem_limit_bytes=LARGE),
        cost_estimate=cost(10**6, 4 * 2**20),
        name="pack",
    )


def corner_call(nx, ny, nz):
    def kernel(lo_in, hi_in, below, above, lo, hi):
        for src, dst, row in ((lo_in, lo, 0), (hi_in, hi, ny - 1)):
            dst[pl.ds(0, 3 * nx), :] = src[pl.ds(0, 3 * nx), :]
            dst[pl.ds(3 * nx, 8), :] = jnp.zeros((8, nz), F32)
            dst[pl.ds(3 * nx, 1), :] = below[pl.ds(ny + row, 1), :]
            dst[pl.ds(3 * nx + 1, 1), :] = above[pl.ds(row, 1), :]

    track = jax.ShapeDtypeStruct((3 * nx + 8, nz), F32)
    return pl.pallas_call(
        kernel, out_shape=(track, track), in_specs=[VM] * 4, out_specs=(VM, VM),
        compiler_params=pltpu.CompilerParams(vmem_limit_bytes=SMALL),
        cost_estimate=cost(10**5, 2**20), name="corners",
    )


def request_call(n_track, n_tiles, cells, width, cap):
    slot_rows = n_track * cap // LANES

    def kernel(foot, index, profile, requests, slots, target):
        fp = foot[...]
        owner = lax.shift_right_logical(fp, int(math.log2(cells)))
        cell = fp & (cells - 1)
        marks = [(owner == o).astype(F32) for o in range(n_track)]
        stacked = jnp.concatenate(marks, axis=0).astype(BF16)
        row = lax.broadcasted_iota(jnp.int32, (LANES, LANES), 0)
        col = lax.broadcasted_iota(jnp.int32, (LANES, LANES), 1)
        within = mm(stacked, (row < col).astype(F32).astype(BF16))
        totals = mm(stacked, jnp.ones((LANES, LANES), BF16)).astype(BF16)
        t_row = lax.broadcasted_iota(jnp.int32, (n_tiles, n_tiles), 0)
        t_col = lax.broadcasted_iota(jnp.int32, (n_tiles, n_tiles), 1)
        lower = (t_col < t_row).astype(F32).astype(BF16)
        rank = jnp.zeros((n_tiles, LANES), F32)
        for o in range(n_track):
            part = slice(o * n_tiles, (o + 1) * n_tiles)
            rank = rank + marks[o] * (within[part] + mm(lower, totals[part]))
        slot = owner * cap + rank.astype(jnp.int32)
        slots[...] = slot
        at_row = lax.shift_right_logical(slot, int(math.log2(LANES)))
        at_lane = slot & (LANES - 1)
        high = lax.shift_right_logical(cell, int(math.log2(width))).astype(F32)
        low = (cell & (width - 1)).astype(F32)
        rows = lax.broadcasted_iota(jnp.int32, (slot_rows, LANES), 0)
        found = jnp.zeros((2 * slot_rows, LANES), F32)
        for k in range(n_tiles):
            here = rows == at_row[k : k + 1]
            values = jnp.concatenate(
                [jnp.where(here, high[k : k + 1], 0.0), jnp.where(here, low[k : k + 1], 0.0)], axis=0
            ).astype(BF16)
            lanes = (row == at_lane[k : k + 1]).astype(F32).astype(BF16)
            found = found + mm_nt(values, lanes)
        requests[...] = found[:slot_rows] * float(width) + found[slot_rows:]
        spread = jnp.broadcast_to(profile[...], (n_tiles, profile.shape[1]))
        temp = jnp.take_along_axis(spread, index[...], axis=1)
        target[...] = 0.05 + jnp.maximum(1.0 - temp, 0.0)

    tiles = (n_tiles, LANES)
    return pl.pallas_call(
        kernel,
        out_shape=(
            jax.ShapeDtypeStruct((slot_rows, LANES), F32),
            jax.ShapeDtypeStruct(tiles, jnp.int32),
            jax.ShapeDtypeStruct(tiles, F32),
        ),
        in_specs=[VM] * 3,
        out_specs=(VM,) * 3,
        compiler_params=pltpu.CompilerParams(vmem_limit_bytes=SMALL),
        cost_estimate=cost(10**8, 2**20),
        name="requests",
    )


def look_up(table, lane, row, rows, width):
    n = lane.shape[1]
    lanes = lax.broadcasted_iota(jnp.int32, (width, n), 0).astype(F32).astype(BF16)
    here = jnp.where(lanes == lane.astype(F32).astype(BF16), jnp.array(1, BF16), jnp.array(0, BF16))
    got = mm(table, jnp.concatenate([here, here], axis=0))
    mine = lax.broadcasted_iota(jnp.int32, (rows, n), 0) == row
    return [
        jnp.sum(jnp.where(mine, got[c * rows : (c + 1) * rows], 0.0), axis=0, keepdims=True) for c in range(3)
    ]


def look_up_all(table, lane, row, rows, width, store):
    for j in range(0, lane.shape[0], 2):
        pair = [jnp.concatenate([v[j : j + 1], v[j + 1 : j + 2]], axis=1) for v in (lane, row)]
        values = look_up(table, pair[0], pair[1], rows, width)
        for i in range(2):
            store(j + i, [v[:, i * LANES : (i + 1) * LANES] for v in values])


def llb(m, field, target):
    sq = m[0] * m[0] + m[1] * m[1] + m[2] * m[2]
    pull = 0.5 * (1.0 - sq / target)
    h = [field[c] + pull * m[c] for c in range(3)]

    def cross(a, b):
        return [a[(c + 1) % 3] * b[(c + 2) % 3] - a[(c + 2) % 3] * b[(c + 1) % 3] for c in range(3)]

    turn = cross(m, h)
    damp = cross(m, turn)
    along = m[0] * h[0] + m[1] * h[1] + m[2] * h[2]
    return [m[c] + 0.1 * (0.3 * along * m[c] - turn[c] - 0.5 * damp[c]) for c in range(3)]


def fold(by_hi, by_lo):
    return (by_hi[8:16] + by_lo[0:8]) + by_hi[0:8]


def tile_major(m_ref, tiles_ref, n_tiles):
    tiles_ref[...] = jnp.zeros_like(tiles_ref)
    flat = tiles_ref.reshape((n_tiles + 2) * 8, LANES)
    for c in range(3):
        flat[pl.ds(8 + c, n_tiles, stride=8), :] = m_ref[pl.ds(c * n_tiles, n_tiles), :]


def exchange(tiles_ref, own, nxt, k):
    here = jnp.concatenate([both(tiles_ref[k + 1]), both(tiles_ref[k])], axis=1)
    high = both(tiles_ref[k + 2])
    own_hi, own_lo = split(own)
    nxt_hi, nxt_lo = split(nxt)
    field = fold(
        mm_nt(here, jnp.concatenate([own_hi, nxt_hi], axis=1)),
        mm_nt(here, jnp.concatenate([own_lo, nxt_lo], axis=1)),
    )
    return field + fold(mm(high, nxt_hi), mm(high, nxt_lo))


def first_call(n_tiles, ny, start, count):
    step = 4
    chunks = count // step

    def kernel(flags, own_hbm, nxt_hbm, m_ref, below, above, ex, own, nxt, tiles, sem):
        def copies(c):
            part = pl.ds(c * step, step)
            return [
                pltpu.make_async_copy(own_hbm.at[pl.ds(start + c * step, step)], own.at[part], sem.at[0, c]),
                pltpu.make_async_copy(nxt_hbm.at[pl.ds(start + c * step, step)], nxt.at[part], sem.at[1, c]),
            ]

        for c in range(chunks):
            for copy in copies(c):
                copy.start()
        tile_major(m_ref, tiles, n_tiles)
        tiles[0] = jnp.where(flags[0] > 0, below[pl.ds(3 * ny, 8), :], 0.0)
        tiles[n_tiles + 1] = jnp.where(flags[1] > 0, above[pl.ds(3 * ny, 8), :], 0.0)
        for c in range(chunks):
            for copy in copies(c):
                copy.wait()
            for k in range(c * step, (c + 1) * step):
                field = exchange(tiles, own[k], nxt[k], start + k)
                for n in range(3):
                    ex[pl.ds(n * count + k, 1), :] = field[n : n + 1]

    return pl.pallas_call(
        kernel,
        out_shape=jax.ShapeDtypeStruct((3 * count, LANES), F32),
        in_specs=[SM, HBM, HBM, VM, VM, VM],
        out_specs=VM,
        scratch_shapes=[
            pltpu.VMEM((count, LANES, LANES), F32),
            pltpu.VMEM((count, LANES, LANES), F32),
            pltpu.VMEM((n_tiles + 2, 8, LANES), F32),
            pltpu.SemaphoreType.DMA((2, chunks)),
        ],
        compiler_params=pltpu.CompilerParams(vmem_limit_bytes=LARGE),
        cost_estimate=cost(10**9, 4 * 2**20),
        name="couple_first",
    )


def section_call(n_tiles, n_track, cap):
    per = cap // LANES
    slot_rows = n_track * per

    def kernel(answers, slots, m_ref, ex_a, ex_b, target, applied, m_out, edge_lo, edge_hi, parts):
        for c in range(3):
            rows = jnp.concatenate([answers[o, pl.ds(c * per, per), :] for o in range(n_track)], axis=0)
            hi, lo = split(rows)
            parts[pl.ds(c * slot_rows, slot_rows), pl.ds(0, LANES)] = hi
            parts[pl.ds(c * slot_rows, slot_rows), pl.ds(LANES, LANES)] = lo
        table = parts[...]
        slot = slots[...]
        at_row = lax.shift_right_logical(slot, int(math.log2(LANES)))
        at_lane = slot & (LANES - 1)

        def store(k, values):
            for c in range(3):
                applied[pl.ds(c * n_tiles + k, 1), :] = values[c]

        look_up_all(table, at_lane, at_row, slot_rows, LANES, store)
        part = [pl.ds(c * n_tiles, n_tiles) for c in range(3)]
        m = [m_ref[part[c], :] for c in range(3)]
        half = n_tiles // 2
        ex = [
            jnp.concatenate([ref[pl.ds(c * half, half), :] for ref in (ex_a, ex_b)], axis=0) for c in range(3)
        ]
        m = llb(m, [applied[part[c], :] + ex[c] for c in range(3)], target[...])
        edge_lo[...] = jnp.zeros((8, LANES), F32)
        edge_hi[...] = jnp.zeros((8, LANES), F32)
        for c in range(3):
            m_out[part[c], :] = m[c]
            edge_lo[pl.ds(c, 1), :] = m[c][0:1]
            edge_hi[pl.ds(c, 1), :] = m[c][n_tiles - 1 :]

    grains = jax.ShapeDtypeStruct((3 * n_tiles, LANES), F32)
    edge = jax.ShapeDtypeStruct((8, LANES), F32)
    return pl.pallas_call(
        kernel,
        out_shape=(grains, grains, edge, edge),
        in_specs=[VM] * 6,
        out_specs=(VM,) * 4,
        scratch_shapes=[pltpu.VMEM((3 * slot_rows, 2 * LANES), BF16)],
        compiler_params=pltpu.CompilerParams(vmem_limit_bytes=SMALL),
        cost_estimate=cost(10**9, 2**20),
        name="section_first",
    )


def second_call(n_tiles):
    def kernel(own, nxt, m_ref, ex, tiles):
        tile_major(m_ref, tiles, n_tiles)
        for k in range(n_tiles):
            field = exchange(tiles, own[k], nxt[k], k)
            for n in range(3):
                ex[pl.ds(n * n_tiles + k, 1), :] = field[n : n + 1]

    return pl.pallas_call(
        kernel,
        out_shape=jax.ShapeDtypeStruct((3 * n_tiles, LANES), F32),
        in_specs=[VM] * 3,
        out_specs=VM,
        scratch_shapes=[pltpu.VMEM((n_tiles + 2, 8, LANES), F32)],
        compiler_params=pltpu.CompilerParams(vmem_limit_bytes=SMALL),
        cost_estimate=cost(10**9, 4 * 2**20),
        name="couple_second",
    )


def last_call(n_tiles):
    def kernel(flags, m_ref, ex, applied, target, below, above, nxt, out):
        low = both(jnp.where(flags[0] > 0, below[...], 0.0))
        high = both(jnp.where(flags[1] > 0, above[...], 0.0))
        hi, lo = split(nxt[0])
        first = fold(mm_nt(low, hi), mm_nt(low, lo))
        hi, lo = split(nxt[n_tiles - 1])
        last = fold(mm(high, hi), mm(high, lo))
        at = lax.broadcasted_iota(jnp.int32, (n_tiles, LANES), 0)
        field = []
        m = []
        for c in range(3):
            part = pl.ds(c * n_tiles, n_tiles)
            extra = jnp.where(at == 0, first[c : c + 1], 0.0) + jnp.where(at == n_tiles - 1, last[c : c + 1], 0.0)
            field.append(applied[part, :] + (ex[part, :] + extra))
            m.append(m_ref[part, :])
        m = llb(m, field, target[...])
        for c in range(3):
            out[pl.ds(c * n_tiles, n_tiles), :] = m[c]

    return pl.pallas_call(
        kernel,
        out_shape=jax.ShapeDtypeStruct((3 * n_tiles, LANES), F32),
        in_specs=[SM] + [VM] * 7,
        out_specs=VM,
        compiler_params=pltpu.CompilerParams(vmem_limit_bytes=SMALL),
        cost_estimate=cost(10**7, 2**20),
        name="section_last",
    )


def shifted(v, axis, by):
    n = lax.axis_size(axis)
    return lax.ppermute(v, axis, [(i, (i + by) % n) for i in range(n)])


def per_device(
    potential, source, depth_kernel, magnet, footprint, temp_index, temp_profile, self_tiles, next_tiles
):
    nx, ny, nz = potential.shape
    n_track = lax.axis_size("track")
    n_tiles = self_tiles.shape[1]
    grains = footprint.shape[1]
    cap = 2 * grains // n_track
    h = lax.axis_index("head")
    t = lax.axis_index("track")
    flags = jnp.stack([h > 0, h < lax.axis_size("head") - 1, t > 0, t < n_track - 1]).astype(jnp.int32)
    state = magnet.reshape(3 * n_tiles, LANES)

    head_lo, head_hi, track_lo, track_hi = pack_call(nx, ny, nz, n_tiles)(potential, source, state)
    below = shifted(head_hi, "head", 1)
    above = shifted(head_lo, "head", -1)
    requests, slots, target = request_call(n_track, n_tiles, nx * ny, ny, cap)(
        footprint.reshape(n_tiles, LANES), temp_index.reshape(n_tiles, LANES), temp_profile[None, :]
    )
    track_lo, track_hi = corner_call(nx, ny, nz)(track_lo, track_hi, below, above)
    left = shifted(track_hi, "track", 1)
    right = shifted(track_lo, "track", -1)
    asked = lax.all_to_all(requests.reshape(n_track, cap // LANES, LANES), "track", 0, 0)

    kern = jnp.pad(depth_kernel, ((0, 5), (0, 0)))
    half = n_tiles // 2
    couplings = (flags, self_tiles[0], next_tiles[0], state, below, above)
    ex_a = first_call(n_tiles, ny, 0, half)(*couplings)
    relaxed, reply = relax_call(nx, ny, nz, n_track, cap)(
        flags, potential, source, below, above, left, right, track_lo, track_hi, kern,
        asked.reshape(n_track * cap // LANES, LANES), ex_a,
    )
    answers = lax.all_to_all(reply, "track", 0, 0)
    ex_b = first_call(n_tiles, ny, half, n_tiles - half)(*couplings)
    applied, state, edge_lo, edge_hi = section_call(n_tiles, n_track, cap)(
        answers, slots, state, ex_a, ex_b, target
    )
    tile_below = shifted(edge_hi, "head", 1)
    tile_above = shifted(edge_lo, "head", -1)
    ex = second_call(n_tiles)(self_tiles[0], next_tiles[0], state)
    state = last_call(n_tiles)(
        flags, state, ex, applied, target, tile_below, tile_above, next_tiles[0]
    )
    return relaxed, state.reshape(3, 1, grains)


def solution(mesh):
    in_specs = (
        P("head", "track", None),
        P("head", "track", None),
        P(),
        P(None, "track", "head"),
        P("track", "head"),
        P("track", "head"),
        P(),
        P("track", "head", None, None),
        P("track", "head", None, None),
    )
    out_specs = (P("head", "track", None), P(None, "track", "head"))
    return jax.shard_map(
        per_device, mesh=mesh, in_specs=in_specs, out_specs=out_specs, check_vma=False
    )
```

```python
import math

import jax
import jax.numpy as jnp
from jax import lax
from jax.experimental import pallas as pl
from jax.experimental.pallas import tpu as pltpu
from jax.sharding import PartitionSpec as P

F32 = jnp.float32
BF16 = jnp.bfloat16
STRIP = 16
UNIT = 4
TOP = 8
AHEAD = 4
LANES = 128
SMALL = 16 * 2**20
LARGE = 52 * 2**20
NT = (((1,), (1,)), ((), ()))
VM = pl.BlockSpec(memory_space=pltpu.VMEM)
SM = pl.BlockSpec(memory_space=pltpu.SMEM)
HBM = pl.BlockSpec(memory_space=pltpu.HBM)
ANY = pl.BlockSpec(memory_space=pl.ANY)


def mm(a, b):
    return jnp.dot(a, b, preferred_element_type=F32)


def mm_nt(a, b):
    return lax.dot_general(a, b, NT, preferred_element_type=F32)


def split(v):
    hi = v.astype(BF16)
    return hi, (v - hi.astype(F32)).astype(BF16)


def place():
    h = lax.axis_index("head")
    t = lax.axis_index("track")
    flags = (h > 0, h < lax.axis_size("head") - 1, t > 0, t < lax.axis_size("track") - 1, h % 2 == 1)
    return [flag.astype(jnp.int32) for flag in flags]


def cost(flops, moved):
    return pl.CostEstimate(flops=flops, bytes_accessed=moved, transcendentals=0)


def rcp(v):
    return pl.reciprocal(v, approx=True)


def flux(d):
    mu = 1.0 + rcp(0.25 + d * d)
    return mu * d, mu


def z_flux(c):
    lane = lax.broadcasted_iota(jnp.int32, c.shape, c.ndim - 1)
    n = c.shape[-1]
    zl = jnp.where(lane == 0, 0.0, pltpu.roll(c, 1, c.ndim - 1))
    zr = jnp.where(lane == n - 1, 0.0, pltpu.roll(c, n - 1, c.ndim - 1))
    fl, ml = flux(zl - c)
    fr, mr = flux(zr - c)
    return fl + fr, ml + mr


def both(v):
    hi = v.astype(jnp.bfloat16).astype(jnp.float32)
    return jnp.concatenate([hi, v - hi], axis=0).astype(jnp.bfloat16)


def finish(c, numer, denom):
    return c + 0.8 * (numer * rcp(denom))


def relax_call(nx, ny, nz, n_track, cap):
    chunk = UNIT
    per = cap // LANES
    rows = ny + 2 * TOP

    def kernel(p_hbm, s_hbm, from_a, from_b, tlo, thi, own_lo, own_hi, kern, requests, ex_hbm, o_hbm, reply,
               table, parts, pe, q, sb, ob, fx1, mx1, fx2, mx2, fy1, my1, fy2, my2, psem, ssem, osem):
        n_chunk = nx // chunk

        def pcopy(c):
            return pltpu.make_async_copy(p_hbm.at[pl.ds(c * chunk, chunk)],
                                         pe.at[pl.ds(2 + c * chunk, chunk), pl.ds(TOP, ny)], psem.at[c])

        def scopy(c):
            return pltpu.make_async_copy(s_hbm.at[pl.ds(c * chunk, chunk)],
                                         sb.at[pl.ds(1 + c * chunk, chunk)], ssem.at[c])

        def ocopy(c):
            return pltpu.make_async_copy(ob.at[pl.ds(c * chunk + UNIT, chunk)],
                                         o_hbm.at[pl.ds(c * chunk, chunk)], osem.at[c])

        def fetch(c):
            pcopy(c).start()
            scopy(c).start()

        for c in range(AHEAD):
            fetch(c)

        flags = place()
        has = [flags[n] > 0 for n in range(4)]

        def keep(flag, v):
            return jnp.where(flag, v, 0.0)

        main = pl.ds(TOP, ny)
        odd = flags[4] > 0
        for side, (at, to) in enumerate((((0, 1), 0), ((nx + 2, nx + 3), nx + 1))):
            swap = odd if side == 0 else jnp.logical_not(odd)
            planes = [
                jnp.where(swap, from_a[pl.ds(n * ny, ny), :], from_b[pl.ds(n * ny, ny), :]) for n in range(3)
            ]
            pe[at[0], main, :] = keep(has[side], planes[0])
            pe[at[1], main, :] = keep(has[side], planes[1])
            sb[to, :, :] = planes[2]
        pe2 = pe.reshape((nx + 4) * rows, nz)
        q2 = q.reshape((nx + 2) * rows, nz)
        for side, (ref, own, row) in enumerate(((tlo, own_lo, TOP - 1), (thi, own_hi, TOP + ny))):
            flag = has[2 + side]
            c = keep(flag, ref[pl.ds(0, nx), :])
            far = keep(flag, ref[pl.ds(nx, nx), :])
            src = ref[pl.ds(2 * nx, nx), :]
            near = own[pl.ds(0, nx), :]
            corners = keep(flag, ref[pl.ds(3 * nx, 8), :])
            below = keep(has[0], corners[0:1])
            above = keep(has[1], corners[1:2])
            ix = lax.broadcasted_iota(jnp.int32, c.shape, 0)
            xl = jnp.where(ix == 0, below, pltpu.roll(c, 1, 0))
            xr = jnp.where(ix == nx - 1, above, pltpu.roll(c, nx - 1, 0))
            numer, denom = z_flux(c)
            numer = numer + src
            denom = denom + 1.0
            for other in (far, near, xl, xr):
                f, mu = flux(other - c)
                numer = numer + f
                denom = denom + mu
            pe2[pl.ds(2 * rows + row, nx, stride=rows), :] = c
            pe2[pl.ds(rows + row, 1), :] = below
            pe2[pl.ds((nx + 2) * rows + row, 1), :] = above
            q2[pl.ds(rows + row, nx, stride=rows), :] = keep(flag, finish(c, numer, denom))

        def sweep(a, x, planes, fx, mx, fy, my, src, store):
            for u in range(planes):
                f, mu = flux(a[x + u, pl.ds(1, TOP), :] - a[x + u, pl.ds(0, TOP), :])
                fy[u, pl.ds(0, TOP), :] = f
                my[u, pl.ds(0, TOP), :] = mu
            for k in range(ny // STRIP):
                here = pl.ds(TOP + k * STRIP, STRIP)
                before = pl.ds(TOP + k * STRIP - 1, STRIP)
                after = pl.ds(TOP + k * STRIP + 1, STRIP)
                flat = pl.ds(k * STRIP, STRIP)
                c = a[x, here, :]
                fp = fx[flat, :]
                mp = mx[flat, :]
                for u in range(planes):
                    up = a[x + u + 1, here, :]
                    f, mu = flux(up - c)
                    numer = f - fp
                    denom = mu + mp
                    fp, mp = f, mu
                    f, mu = flux(a[x + u, after, :] - c)
                    fy[u, here, :] = f
                    my[u, here, :] = mu
                    numer = numer + (f - fy[u, before, :])
                    denom = denom + (mu + my[u, before, :])
                    f, mu = z_flux(c)
                    numer = numer + (f + src[u, flat, :])
                    denom = denom + (mu + 1.0)
                    store(u, k, finish(c, numer, denom))
                    c = up
                fx[flat, :] = fp
                mx[flat, :] = mp

        def first_x(a, x, fx, mx):
            for k in range(ny // STRIP):
                here = pl.ds(TOP + k * STRIP, STRIP)
                flat = pl.ds(k * STRIP, STRIP)
                f, mu = flux(a[x + 1, here, :] - a[x, here, :])
                fx[flat, :] = f
                mx[flat, :] = mu

        def sweep1(x, planes, flag=None):
            def store(u, k, v):
                q[x + u + 1, pl.ds(TOP + k * STRIP, STRIP), :] = v if flag is None else keep(flag, v)

            sweep(pe, x + 2, planes, fx1, mx1, fy1, my1, sb.at[pl.ds(x + 1, planes)], store)

        kk = both(kern[...])

        def sweep2(x, planes):
            def store(u, k, v):
                ob[x + u + UNIT, pl.ds(k * STRIP, STRIP), :] = v

            sweep(q, x + 1, planes, fx2, mx2, fy2, my2, sb.at[pl.ds(x + 1, planes)], store)

        def surface(x, planes):
            nt = (((1,), (1,)), ((), ()))
            for u in range(planes):
                v = ob[x + u + UNIT]
                hi = v.astype(jnp.bfloat16)
                lo = (v - hi.astype(jnp.float32)).astype(jnp.bfloat16)
                a = lax.dot_general(kk, hi, nt, preferred_element_type=jnp.float32)
                b = lax.dot_general(kk, lo, nt, preferred_element_type=jnp.float32)
                table[x + u + UNIT] = (a[8:16] + b[0:8]) + a[0:8]

        n_unit = nx // UNIT
        pcopy(0).wait()
        scopy(0).wait()
        first_x(pe, 0, fx1, mx1)
        sweep1(-1, 1, has[0])
        sweep1(0, 1)
        first_x(q, 0, fx2, mx2)
        pcopy(1).wait()
        scopy(1).wait()
        sweep1(1, UNIT)

        def body(b, _):
            @pl.when(b + AHEAD <= n_unit)
            def _():
                fetch(b + AHEAD - 1)

            @pl.when(b < n_unit - 1)
            def _():
                pcopy(b + 1).wait()
                scopy(b + 1).wait()

            surface((b - 2) * UNIT, UNIT)
            sweep2((b - 1) * UNIT, UNIT)
            sweep1(b * UNIT + 1, UNIT)
            ocopy(b - 1).start()
            return 0

        lax.fori_loop(1, n_unit, body, 0)

        @pl.when(jnp.logical_not(has[1]))
        def _():
            q[nx + 1] = jnp.zeros_like(q[nx + 1])

        surface(nx - 2 * UNIT, UNIT)
        sweep2(nx - UNIT, UNIT)
        ocopy(n_unit - 1).start()
        surface(nx - UNIT, UNIT)

        flat = table.reshape((nx + UNIT) * 8, ny)
        for c in range(3):
            hi, lo = split(flat[pl.ds(UNIT * 8 + c, nx, stride=8), :])
            parts[pl.ds(c * nx, nx), pl.ds(0, ny)] = hi
            parts[pl.ds(c * nx, nx), pl.ds(ny, ny)] = lo
        asked = requests[...].astype(jnp.int32)

        def answer(j, values):
            for c in range(3):
                reply[j // per, pl.ds(c * per + j % per, 1), :] = values[c]

        look_up_all(parts[...], asked & (ny - 1), lax.shift_right_logical(asked, int(math.log2(ny))), nx, ny, answer)
        for c in range(n_chunk):
            ocopy(c).wait()

    f32 = jnp.float32
    vm = pl.BlockSpec(memory_space=pltpu.VMEM)
    hbm = pl.BlockSpec(memory_space=pltpu.HBM)
    plane = pltpu.VMEM((ny, nz), f32)
    edge = pltpu.VMEM((UNIT, rows, nz), f32)
    return pl.pallas_call(
        kernel,
        out_shape=(
            jax.ShapeDtypeStruct((nx, ny, nz), f32),
            jax.ShapeDtypeStruct((n_track, 3 * per, 128), f32),
        ),
        in_specs=[hbm, hbm] + [vm] * 8 + [pl.BlockSpec(memory_space=pl.ANY)],
        out_specs=(hbm, vm),
        scratch_shapes=[
            pltpu.VMEM((nx + UNIT, 8, ny), f32), pltpu.VMEM((3 * nx, 2 * ny), jnp.bfloat16),
            pltpu.VMEM((nx + 4, rows, nz), f32), pltpu.VMEM((nx + 2, rows, nz), f32),
            pltpu.VMEM((nx + 2, ny, nz), f32), pltpu.VMEM((nx + UNIT, ny, nz), f32),
            plane, plane, plane, plane, edge, edge, edge, edge,
            pltpu.SemaphoreType.DMA((nx // chunk,)), pltpu.SemaphoreType.DMA((nx // chunk,)),
            pltpu.SemaphoreType.DMA((nx // chunk,)),
        ],
        compiler_params=pltpu.CompilerParams(vmem_limit_bytes=LARGE),
        cost_estimate=pl.CostEstimate(flops=nx * ny * nz * 100, bytes_accessed=nx * ny * nz * 12, transcendentals=nx * ny * nz * 10),
        name="relax",
    )


def pack_call(nx, ny, nz):
    def kernel(p_hbm, s_hbm, head_a, head_b, track_lo, track_hi, p_lo, p_hi, s_lo, s_hi, sem):
        odd = place()[4]
        copies = []
        for i, (out, low) in enumerate(((head_a, odd), (head_b, 1 - odd))):
            at_p = jnp.where(low > 0, 0, nx - 2)
            at_s = jnp.where(low > 0, 0, nx - 1)
            copies += [
                pltpu.make_async_copy(p_hbm.at[at_p], out.at[pl.ds(0, ny)], sem.at[3 * i]),
                pltpu.make_async_copy(p_hbm.at[at_p + 1], out.at[pl.ds(ny, ny)], sem.at[3 * i + 1]),
                pltpu.make_async_copy(s_hbm.at[at_s], out.at[pl.ds(2 * ny, ny)], sem.at[3 * i + 2]),
            ]
        rows = [(p_hbm, 0, p_lo), (p_hbm, ny - 8, p_hi), (s_hbm, 0, s_lo), (s_hbm, ny - 8, s_hi)]
        copies += [
            pltpu.make_async_copy(src.at[:, pl.ds(at, 8)], dst, sem.at[6 + i])
            for i, (src, at, dst) in enumerate(rows)
        ]
        for copy in copies:
            copy.start()
        head_a[pl.ds(3 * ny, 8), :] = jnp.zeros((8, nz), F32)
        head_b[pl.ds(3 * ny, 8), :] = jnp.zeros((8, nz), F32)
        for copy in copies[6:]:
            copy.wait()
        for out, p_ref, s_ref, order in ((track_lo, p_lo, s_lo, (0, 1)), (track_hi, p_hi, s_hi, (7, 6))):
            p2 = p_ref.reshape(nx * 8, nz)
            s2 = s_ref.reshape(nx * 8, nz)
            out[pl.ds(0, nx), :] = p2[pl.ds(order[0], nx, stride=8), :]
            out[pl.ds(nx, nx), :] = p2[pl.ds(order[1], nx, stride=8), :]
            out[pl.ds(2 * nx, nx), :] = s2[pl.ds(order[0], nx, stride=8), :]
            out[pl.ds(3 * nx, 8), :] = jnp.zeros((8, nz), F32)
        for copy in copies[:6]:
            copy.wait()

    head = jax.ShapeDtypeStruct((3 * ny + 8, nz), F32)
    track = jax.ShapeDtypeStruct((3 * nx + 8, nz), F32)
    eight = pltpu.VMEM((nx, 8, nz), F32)
    return pl.pallas_call(
        kernel,
        out_shape=(head, head, track, track),
        in_specs=[HBM, HBM],
        out_specs=(VM,) * 4,
        scratch_shapes=[eight] * 4 + [pltpu.SemaphoreType.DMA((10,))],
        compiler_params=pltpu.CompilerParams(vmem_limit_bytes=LARGE),
        cost_estimate=cost(10**6, 4 * 2**20),
        name="pack",
    )


def ends_call(ny, n_tiles):
    def kernel(m_ref, a_in, b_in, head_a, head_b):
        flags = place()
        for out, low in ((head_a, flags[4]), (head_b, 1 - flags[4])):
            for c in range(3):
                first = m_ref[pl.ds(c * n_tiles, 1), :]
                last = m_ref[pl.ds((c + 1) * n_tiles - 1, 1), :]
                out[pl.ds(3 * ny + c, 1), :] = jnp.where(low > 0, first, last)

    head = jax.ShapeDtypeStruct((3 * ny + 8, LANES), F32)
    return pl.pallas_call(
        kernel, out_shape=(head, head), in_specs=[VM, VM, VM], out_specs=(VM, VM),
        input_output_aliases={1: 0, 2: 1},
        compiler_params=pltpu.CompilerParams(vmem_limit_bytes=SMALL),
        cost_estimate=cost(10**5, 10**5), name="ends",
    )


def corner_call(nx, ny, nz):
    def kernel(lo_in, hi_in, from_a, from_b, lo, hi):
        odd = place()[4] > 0
        for src, dst, row in ((lo_in, lo, 0), (hi_in, hi, ny - 1)):
            dst[pl.ds(0, 3 * nx), :] = src[pl.ds(0, 3 * nx), :]
            dst[pl.ds(3 * nx, 8), :] = jnp.zeros((8, nz), F32)
            below = pl.ds(ny + row, 1)
            above = pl.ds(row, 1)
            dst[pl.ds(3 * nx, 1), :] = jnp.where(odd, from_a[below, :], from_b[below, :])
            dst[pl.ds(3 * nx + 1, 1), :] = jnp.where(odd, from_b[above, :], from_a[above, :])

    track = jax.ShapeDtypeStruct((3 * nx + 8, nz), F32)
    return pl.pallas_call(
        kernel, out_shape=(track, track), in_specs=[VM] * 4, out_specs=(VM, VM),
        compiler_params=pltpu.CompilerParams(vmem_limit_bytes=SMALL),
        cost_estimate=cost(10**5, 2**20), name="corners",
    )


def request_call(n_track, n_tiles, cells, width, cap):
    slot_rows = n_track * cap // LANES

    def kernel(foot, index, profile, requests, slots, target):
        fp = foot[...]
        owner = lax.shift_right_logical(fp, int(math.log2(cells)))
        cell = fp & (cells - 1)
        marks = [(owner == o).astype(F32) for o in range(n_track)]
        stacked = jnp.concatenate(marks, axis=0).astype(BF16)
        row = lax.broadcasted_iota(jnp.int32, (LANES, LANES), 0)
        col = lax.broadcasted_iota(jnp.int32, (LANES, LANES), 1)
        within = mm(stacked, (row < col).astype(F32).astype(BF16))
        totals = mm(stacked, jnp.ones((LANES, LANES), BF16)).astype(BF16)
        t_row = lax.broadcasted_iota(jnp.int32, (n_tiles, n_tiles), 0)
        t_col = lax.broadcasted_iota(jnp.int32, (n_tiles, n_tiles), 1)
        lower = (t_col < t_row).astype(F32).astype(BF16)
        rank = jnp.zeros((n_tiles, LANES), F32)
        for o in range(n_track):
            part = slice(o * n_tiles, (o + 1) * n_tiles)
            rank = rank + marks[o] * (within[part] + mm(lower, totals[part]))
        slot = owner * cap + rank.astype(jnp.int32)
        slots[...] = slot
        at_row = lax.shift_right_logical(slot, int(math.log2(LANES)))
        at_lane = slot & (LANES - 1)
        high = lax.shift_right_logical(cell, int(math.log2(width))).astype(F32)
        low = (cell & (width - 1)).astype(F32)
        rows = lax.broadcasted_iota(jnp.int32, (slot_rows, LANES), 0)
        found = jnp.zeros((2 * slot_rows, LANES), F32)
        for k in range(n_tiles):
            here = rows == at_row[k : k + 1]
            values = jnp.concatenate(
                [jnp.where(here, high[k : k + 1], 0.0), jnp.where(here, low[k : k + 1], 0.0)], axis=0
            ).astype(BF16)
            lanes = (row == at_lane[k : k + 1]).astype(F32).astype(BF16)
            found = found + mm_nt(values, lanes)
        requests[...] = found[:slot_rows] * float(width) + found[slot_rows:]
        spread = jnp.broadcast_to(profile[...], (n_tiles, profile.shape[1]))
        temp = jnp.take_along_axis(spread, index[...], axis=1)
        target[...] = 0.05 + jnp.maximum(1.0 - temp, 0.0)

    tiles = (n_tiles, LANES)
    return pl.pallas_call(
        kernel,
        out_shape=(
            jax.ShapeDtypeStruct((slot_rows, LANES), F32),
            jax.ShapeDtypeStruct(tiles, jnp.int32),
            jax.ShapeDtypeStruct(tiles, F32),
        ),
        in_specs=[VM] * 3,
        out_specs=(VM,) * 3,
        compiler_params=pltpu.CompilerParams(vmem_limit_bytes=SMALL),
        cost_estimate=cost(10**8, 2**20),
        name="requests",
    )


def look_up(table, lane, row, rows, width):
    n = lane.shape[1]
    lanes = lax.broadcasted_iota(jnp.int32, (width, n), 0).astype(F32).astype(BF16)
    here = jnp.where(lanes == lane.astype(F32).astype(BF16), jnp.array(1, BF16), jnp.array(0, BF16))
    got = mm(table, jnp.concatenate([here, here], axis=0))
    mine = lax.broadcasted_iota(jnp.int32, (rows, n), 0) == row
    return [
        jnp.sum(jnp.where(mine, got[c * rows : (c + 1) * rows], 0.0), axis=0, keepdims=True) for c in range(3)
    ]


def look_up_all(table, lane, row, rows, width, store):
    for j in range(0, lane.shape[0], 2):
        pair = [jnp.concatenate([v[j : j + 1], v[j + 1 : j + 2]], axis=1) for v in (lane, row)]
        values = look_up(table, pair[0], pair[1], rows, width)
        for i in range(2):
            store(j + i, [v[:, i * LANES : (i + 1) * LANES] for v in values])


def llb(m, field, target):
    sq = m[0] * m[0] + m[1] * m[1] + m[2] * m[2]
    pull = 0.5 * (1.0 - sq / target)
    h = [field[c] + pull * m[c] for c in range(3)]

    def cross(a, b):
        return [a[(c + 1) % 3] * b[(c + 2) % 3] - a[(c + 2) % 3] * b[(c + 1) % 3] for c in range(3)]

    turn = cross(m, h)
    damp = cross(m, turn)
    along = m[0] * h[0] + m[1] * h[1] + m[2] * h[2]
    return [m[c] + 0.1 * (0.3 * along * m[c] - turn[c] - 0.5 * damp[c]) for c in range(3)]


def fold(by_hi, by_lo):
    return (by_hi[8:16] + by_lo[0:8]) + by_hi[0:8]


def tile_major(m_ref, tiles_ref, n_tiles):
    tiles_ref[...] = jnp.zeros_like(tiles_ref)
    flat = tiles_ref.reshape((n_tiles + 2) * 8, LANES)
    for c in range(3):
        flat[pl.ds(8 + c, n_tiles, stride=8), :] = m_ref[pl.ds(c * n_tiles, n_tiles), :]


def exchange(tiles_ref, own, nxt, k):
    here = jnp.concatenate([both(tiles_ref[k + 1]), both(tiles_ref[k])], axis=1)
    high = both(tiles_ref[k + 2])
    own_hi, own_lo = split(own)
    nxt_hi, nxt_lo = split(nxt)
    field = fold(
        mm_nt(here, jnp.concatenate([own_hi, nxt_hi], axis=1)),
        mm_nt(here, jnp.concatenate([own_lo, nxt_lo], axis=1)),
    )
    return field + fold(mm(high, nxt_hi), mm(high, nxt_lo))


def first_call(n_tiles, ny, start, count):
    step = 4
    chunks = count // step

    def kernel(own_hbm, nxt_hbm, m_ref, from_a, from_b, after, ex, own, nxt, tiles, sem):
        def copies(c):
            part = pl.ds(c * step, step)
            return [
                pltpu.make_async_copy(own_hbm.at[pl.ds(start + c * step, step)], own.at[part], sem.at[0, c]),
                pltpu.make_async_copy(nxt_hbm.at[pl.ds(start + c * step, step)], nxt.at[part], sem.at[1, c]),
            ]

        for c in range(chunks):
            for copy in copies(c):
                copy.start()
        tile_major(m_ref, tiles, n_tiles)
        flags = place()
        odd = flags[4] > 0
        by_a = from_a[pl.ds(3 * ny, 8), :]
        by_b = from_b[pl.ds(3 * ny, 8), :]
        tiles[0] = jnp.where(flags[0] > 0, jnp.where(odd, by_a, by_b), 0.0)
        tiles[n_tiles + 1] = jnp.where(flags[1] > 0, jnp.where(odd, by_b, by_a), 0.0)
        for c in range(chunks):
            for copy in copies(c):
                copy.wait()
            for k in range(c * step, (c + 1) * step):
                field = exchange(tiles, own[k], nxt[k], start + k)
                for n in range(3):
                    ex[pl.ds(n * count + k, 1), :] = field[n : n + 1]

    return pl.pallas_call(
        kernel,
        out_shape=jax.ShapeDtypeStruct((3 * count, LANES), F32),
        in_specs=[HBM, HBM, VM, VM, VM, ANY],
        out_specs=VM,
        scratch_shapes=[
            pltpu.VMEM((count, LANES, LANES), F32),
            pltpu.VMEM((count, LANES, LANES), F32),
            pltpu.VMEM((n_tiles + 2, 8, LANES), F32),
            pltpu.SemaphoreType.DMA((2, chunks)),
        ],
        compiler_params=pltpu.CompilerParams(vmem_limit_bytes=LARGE),
        cost_estimate=cost(10**9, 4 * 2**20),
        name="couple_first",
    )


def section_call(n_tiles, n_track, cap):
    per = cap // LANES
    slot_rows = n_track * per

    def kernel(answers, slots, m_ref, ex_a, ex_b, target, applied, m_out, edge_a, edge_b, parts):
        for c in range(3):
            rows = jnp.concatenate([answers[o, pl.ds(c * per, per), :] for o in range(n_track)], axis=0)
            hi, lo = split(rows)
            parts[pl.ds(c * slot_rows, slot_rows), pl.ds(0, LANES)] = hi
            parts[pl.ds(c * slot_rows, slot_rows), pl.ds(LANES, LANES)] = lo
        table = parts[...]
        slot = slots[...]
        at_row = lax.shift_right_logical(slot, int(math.log2(LANES)))
        at_lane = slot & (LANES - 1)

        def store(k, values):
            for c in range(3):
                applied[pl.ds(c * n_tiles + k, 1), :] = values[c]

        look_up_all(table, at_lane, at_row, slot_rows, LANES, store)
        part = [pl.ds(c * n_tiles, n_tiles) for c in range(3)]
        m = [m_ref[part[c], :] for c in range(3)]
        half = n_tiles // 2
        ex = [
            jnp.concatenate([ref[pl.ds(c * half, half), :] for ref in (ex_a, ex_b)], axis=0) for c in range(3)
        ]
        m = llb(m, [applied[part[c], :] + ex[c] for c in range(3)], target[...])
        odd = place()[4] > 0
        edge_a[...] = jnp.zeros((8, LANES), F32)
        edge_b[...] = jnp.zeros((8, LANES), F32)
        for c in range(3):
            m_out[part[c], :] = m[c]
            edge_a[pl.ds(c, 1), :] = jnp.where(odd, m[c][0:1], m[c][n_tiles - 1 :])
            edge_b[pl.ds(c, 1), :] = jnp.where(odd, m[c][n_tiles - 1 :], m[c][0:1])

    grains = jax.ShapeDtypeStruct((3 * n_tiles, LANES), F32)
    edge = jax.ShapeDtypeStruct((8, LANES), F32)
    return pl.pallas_call(
        kernel,
        out_shape=(grains, grains, edge, edge),
        in_specs=[VM] * 6,
        out_specs=(VM,) * 4,
        scratch_shapes=[pltpu.VMEM((3 * slot_rows, 2 * LANES), BF16)],
        compiler_params=pltpu.CompilerParams(vmem_limit_bytes=SMALL),
        cost_estimate=cost(10**9, 2**20),
        name="section_first",
    )


def second_call(n_tiles):
    def kernel(own, nxt, m_ref, ex, tiles):
        tile_major(m_ref, tiles, n_tiles)
        for k in range(n_tiles):
            field = exchange(tiles, own[k], nxt[k], k)
            for n in range(3):
                ex[pl.ds(n * n_tiles + k, 1), :] = field[n : n + 1]

    return pl.pallas_call(
        kernel,
        out_shape=jax.ShapeDtypeStruct((3 * n_tiles, LANES), F32),
        in_specs=[VM] * 3,
        out_specs=VM,
        scratch_shapes=[pltpu.VMEM((n_tiles + 2, 8, LANES), F32)],
        compiler_params=pltpu.CompilerParams(vmem_limit_bytes=SMALL),
        cost_estimate=cost(10**9, 4 * 2**20),
        name="couple_second",
    )


def last_call(n_tiles):
    def kernel(m_ref, ex, applied, target, from_a, from_b, nxt, out):
        flags = place()
        odd = flags[4] > 0
        below = jnp.where(odd, from_a[...], from_b[...])
        above = jnp.where(odd, from_b[...], from_a[...])
        low = both(jnp.where(flags[0] > 0, below, 0.0))
        high = both(jnp.where(flags[1] > 0, above, 0.0))
        hi, lo = split(nxt[0])
        first = fold(mm_nt(low, hi), mm_nt(low, lo))
        hi, lo = split(nxt[n_tiles - 1])
        last = fold(mm(high, hi), mm(high, lo))
        at = lax.broadcasted_iota(jnp.int32, (n_tiles, LANES), 0)
        field = []
        m = []
        for c in range(3):
            part = pl.ds(c * n_tiles, n_tiles)
            extra = jnp.where(at == 0, first[c : c + 1], 0.0) + jnp.where(at == n_tiles - 1, last[c : c + 1], 0.0)
            field.append(applied[part, :] + (ex[part, :] + extra))
            m.append(m_ref[part, :])
        m = llb(m, field, target[...])
        for c in range(3):
            out[pl.ds(c * n_tiles, n_tiles), :] = m[c]

    return pl.pallas_call(
        kernel,
        out_shape=jax.ShapeDtypeStruct((3 * n_tiles, LANES), F32),
        in_specs=[VM] * 7,
        out_specs=VM,
        compiler_params=pltpu.CompilerParams(vmem_limit_bytes=SMALL),
        cost_estimate=cost(10**7, 2**20),
        name="section_last",
    )


def shifted(v, axis, by):
    n = lax.axis_size(axis)
    return lax.ppermute(v, axis, [(i, (i + by) % n) for i in range(n)])


def traded(to_a, to_b, axis):
    n = lax.axis_size(axis)
    first = [(i, i ^ 1) for i in range(n)]
    second = [(i, (i + 1) % n if i % 2 else (i - 1) % n) for i in range(n)]
    return lax.ppermute(to_a, axis, first), lax.ppermute(to_b, axis, second)


def per_device(
    potential, source, depth_kernel, magnet, footprint, temp_index, temp_profile, self_tiles, next_tiles
):
    nx, ny, nz = potential.shape
    n_track = lax.axis_size("track")
    n_tiles = self_tiles.shape[1]
    grains = footprint.shape[1]
    cap = 2 * grains // n_track
    state = magnet.reshape(3 * n_tiles, LANES)

    head_a, head_b, track_lo, track_hi = pack_call(nx, ny, nz)(potential, source)
    head_a, head_b = ends_call(ny, n_tiles)(state, head_a, head_b)
    from_a, from_b = traded(head_a, head_b, "head")
    requests, slots, target = request_call(n_track, n_tiles, nx * ny, ny, cap)(
        footprint.reshape(n_tiles, LANES), temp_index.reshape(n_tiles, LANES), temp_profile[None, :]
    )
    track_lo, track_hi = corner_call(nx, ny, nz)(track_lo, track_hi, from_a, from_b)
    left = shifted(track_hi, "track", 1)
    right = shifted(track_lo, "track", -1)
    asked = lax.all_to_all(requests.reshape(n_track, cap // LANES, LANES), "track", 0, 0)

    kern = jnp.pad(depth_kernel, ((0, 5), (0, 0)))
    half = n_tiles // 2
    couplings = (self_tiles[0], next_tiles[0], state, from_a, from_b, asked)
    ex_a = first_call(n_tiles, ny, 0, half)(*couplings)
    relaxed, reply = relax_call(nx, ny, nz, n_track, cap)(
        potential, source, from_a, from_b, left, right, track_lo, track_hi, kern,
        asked.reshape(n_track * cap // LANES, LANES), ex_a,
    )
    answers = lax.all_to_all(reply, "track", 0, 0)
    ex_b = first_call(n_tiles, ny, half, n_tiles - half)(*couplings)
    applied, state, edge_a, edge_b = section_call(n_tiles, n_track, cap)(
        answers, slots, state, ex_a, ex_b, target
    )
    tile_a, tile_b = traded(edge_a, edge_b, "head")
    ex = second_call(n_tiles)(self_tiles[0], next_tiles[0], state)
    state = last_call(n_tiles)(
        state, ex, applied, target, tile_a, tile_b, next_tiles[0]
    )
    return relaxed, state.reshape(3, 1, grains)


def solution(mesh):
    in_specs = (
        P("head", "track", None),
        P("head", "track", None),
        P(),
        P(None, "track", "head"),
        P("track", "head"),
        P("track", "head"),
        P(),
        P("track", "head", None, None),
        P("track", "head", None, None),
    )
    out_specs = (P("head", "track", None), P(None, "track", "head"))
    return jax.shard_map(
        per_device, mesh=mesh, in_specs=in_specs, out_specs=out_specs, check_vma=False
    )
```

```python
import math

import jax
import jax.numpy as jnp
from jax import lax
from jax.experimental import pallas as pl
from jax.experimental.pallas import tpu as pltpu
from jax.sharding import PartitionSpec as P

F32 = jnp.float32
BF16 = jnp.bfloat16
STRIP = 16
UNIT = 4
TOP = 8
AHEAD = 4
LANES = 128
SMALL = 16 * 2**20
LARGE = 52 * 2**20
NT = (((1,), (1,)), ((), ()))
VM = pl.BlockSpec(memory_space=pltpu.VMEM)
SM = pl.BlockSpec(memory_space=pltpu.SMEM)
HBM = pl.BlockSpec(memory_space=pltpu.HBM)
ANY = pl.BlockSpec(memory_space=pl.ANY)


def mm(a, b):
    return jnp.dot(a, b, preferred_element_type=F32)


def mm_nt(a, b):
    return lax.dot_general(a, b, NT, preferred_element_type=F32)


def split(v):
    hi = v.astype(BF16)
    return hi, (v - hi.astype(F32)).astype(BF16)


def place():
    h = lax.axis_index("head")
    t = lax.axis_index("track")
    flags = (h > 0, h < lax.axis_size("head") - 1, t > 0, t < lax.axis_size("track") - 1, h % 2 == 1)
    return [flag.astype(jnp.int32) for flag in flags]


def cost(flops, moved):
    return pl.CostEstimate(flops=flops, bytes_accessed=moved, transcendentals=0)


def rcp(v):
    return pl.reciprocal(v, approx=True)


def flux(d):
    mu = 1.0 + rcp(0.25 + d * d)
    return mu * d, mu


def z_flux(c):
    lane = lax.broadcasted_iota(jnp.int32, c.shape, c.ndim - 1)
    n = c.shape[-1]
    zl = jnp.where(lane == 0, 0.0, pltpu.roll(c, 1, c.ndim - 1))
    zr = jnp.where(lane == n - 1, 0.0, pltpu.roll(c, n - 1, c.ndim - 1))
    fl, ml = flux(zl - c)
    fr, mr = flux(zr - c)
    return fl + fr, ml + mr


def both(v):
    hi = v.astype(jnp.bfloat16).astype(jnp.float32)
    return jnp.concatenate([hi, v - hi], axis=0).astype(jnp.bfloat16)


def finish(c, numer, denom):
    return c + 0.8 * (numer * rcp(denom))


def relax_call(nx, ny, nz, n_track, cap):
    chunk = UNIT
    per = cap // LANES
    rows = ny + 2 * TOP

    def kernel(p_hbm, s_hbm, from_a, from_b, tlo, thi, own_lo, own_hi, kern, requests, ex_hbm, o_hbm, reply_out,
               reply, rsem, table, parts, pe, q, sb, ob, fx1, mx1, fx2, mx2, fy1, my1, fy2, my2, psem, ssem, osem):
        n_chunk = nx // chunk

        def pcopy(c):
            return pltpu.make_async_copy(p_hbm.at[pl.ds(c * chunk, chunk)],
                                         pe.at[pl.ds(2 + c * chunk, chunk), pl.ds(TOP, ny)], psem.at[c])

        def scopy(c):
            return pltpu.make_async_copy(s_hbm.at[pl.ds(c * chunk, chunk)],
                                         sb.at[pl.ds(1 + c * chunk, chunk)], ssem.at[c])

        def ocopy(c):
            return pltpu.make_async_copy(ob.at[pl.ds(c * chunk + UNIT, chunk)],
                                         o_hbm.at[pl.ds(c * chunk, chunk)], osem.at[c])

        def fetch(c):
            pcopy(c).start()
            scopy(c).start()

        for c in range(AHEAD):
            fetch(c)

        flags = place()
        has = [flags[n] > 0 for n in range(4)]

        def keep(flag, v):
            return jnp.where(flag, v, 0.0)

        main = pl.ds(TOP, ny)
        odd = flags[4] > 0
        for side, (at, to) in enumerate((((0, 1), 0), ((nx + 2, nx + 3), nx + 1))):
            swap = odd if side == 0 else jnp.logical_not(odd)
            planes = [
                jnp.where(swap, from_a[pl.ds(n * ny, ny), :], from_b[pl.ds(n * ny, ny), :]) for n in range(3)
            ]
            pe[at[0], main, :] = keep(has[side], planes[0])
            pe[at[1], main, :] = keep(has[side], planes[1])
            sb[to, :, :] = planes[2]
        pe2 = pe.reshape((nx + 4) * rows, nz)
        q2 = q.reshape((nx + 2) * rows, nz)
        for side, (ref, own, row) in enumerate(((tlo, own_lo, TOP - 1), (thi, own_hi, TOP + ny))):
            flag = has[2 + side]
            c = keep(flag, ref[pl.ds(0, nx), :])
            far = keep(flag, ref[pl.ds(nx, nx), :])
            src = ref[pl.ds(2 * nx, nx), :]
            near = own[pl.ds(0, nx), :]
            corners = keep(flag, ref[pl.ds(3 * nx, 8), :])
            below = keep(has[0], corners[0:1])
            above = keep(has[1], corners[1:2])
            ix = lax.broadcasted_iota(jnp.int32, c.shape, 0)
            xl = jnp.where(ix == 0, below, pltpu.roll(c, 1, 0))
            xr = jnp.where(ix == nx - 1, above, pltpu.roll(c, nx - 1, 0))
            numer, denom = z_flux(c)
            numer = numer + src
            denom = denom + 1.0
            for other in (far, near, xl, xr):
                f, mu = flux(other - c)
                numer = numer + f
                denom = denom + mu
            pe2[pl.ds(2 * rows + row, nx, stride=rows), :] = c
            pe2[pl.ds(rows + row, 1), :] = below
            pe2[pl.ds((nx + 2) * rows + row, 1), :] = above
            q2[pl.ds(rows + row, nx, stride=rows), :] = keep(flag, finish(c, numer, denom))

        def sweep(a, x, planes, fx, mx, fy, my, src, store):
            for u in range(planes):
                f, mu = flux(a[x + u, pl.ds(1, TOP), :] - a[x + u, pl.ds(0, TOP), :])
                fy[u, pl.ds(0, TOP), :] = f
                my[u, pl.ds(0, TOP), :] = mu
            for k in range(ny // STRIP):
                here = pl.ds(TOP + k * STRIP, STRIP)
                before = pl.ds(TOP + k * STRIP - 1, STRIP)
                after = pl.ds(TOP + k * STRIP + 1, STRIP)
                flat = pl.ds(k * STRIP, STRIP)
                c = a[x, here, :]
                fp = fx[flat, :]
                mp = mx[flat, :]
                for u in range(planes):
                    up = a[x + u + 1, here, :]
                    f, mu = flux(up - c)
                    numer = f - fp
                    denom = mu + mp
                    fp, mp = f, mu
                    f, mu = flux(a[x + u, after, :] - c)
                    fy[u, here, :] = f
                    my[u, here, :] = mu
                    numer = numer + (f - fy[u, before, :])
                    denom = denom + (mu + my[u, before, :])
                    f, mu = z_flux(c)
                    numer = numer + (f + src[u, flat, :])
                    denom = denom + (mu + 1.0)
                    store(u, k, finish(c, numer, denom))
                    c = up
                fx[flat, :] = fp
                mx[flat, :] = mp

        def first_x(a, x, fx, mx):
            for k in range(ny // STRIP):
                here = pl.ds(TOP + k * STRIP, STRIP)
                flat = pl.ds(k * STRIP, STRIP)
                f, mu = flux(a[x + 1, here, :] - a[x, here, :])
                fx[flat, :] = f
                mx[flat, :] = mu

        def sweep1(x, planes, flag=None):
            def store(u, k, v):
                q[x + u + 1, pl.ds(TOP + k * STRIP, STRIP), :] = v if flag is None else keep(flag, v)

            sweep(pe, x + 2, planes, fx1, mx1, fy1, my1, sb.at[pl.ds(x + 1, planes)], store)

        kk = both(kern[...])

        def sweep2(x, planes):
            def store(u, k, v):
                ob[x + u + UNIT, pl.ds(k * STRIP, STRIP), :] = v

            sweep(q, x + 1, planes, fx2, mx2, fy2, my2, sb.at[pl.ds(x + 1, planes)], store)

        def surface(x, planes):
            nt = (((1,), (1,)), ((), ()))
            for u in range(planes):
                v = ob[x + u + UNIT]
                hi = v.astype(jnp.bfloat16)
                lo = (v - hi.astype(jnp.float32)).astype(jnp.bfloat16)
                a = lax.dot_general(kk, hi, nt, preferred_element_type=jnp.float32)
                b = lax.dot_general(kk, lo, nt, preferred_element_type=jnp.float32)
                table[x + u + UNIT] = (a[8:16] + b[0:8]) + a[0:8]

        n_unit = nx // UNIT
        pcopy(0).wait()
        scopy(0).wait()
        first_x(pe, 0, fx1, mx1)
        sweep1(-1, 1, has[0])
        sweep1(0, 1)
        first_x(q, 0, fx2, mx2)
        pcopy(1).wait()
        scopy(1).wait()
        sweep1(1, UNIT)

        def body(b, _):
            @pl.when(b + AHEAD <= n_unit)
            def _():
                fetch(b + AHEAD - 1)

            @pl.when(b < n_unit - 1)
            def _():
                pcopy(b + 1).wait()
                scopy(b + 1).wait()

            surface((b - 2) * UNIT, UNIT)
            sweep2((b - 1) * UNIT, UNIT)
            sweep1(b * UNIT + 1, UNIT)
            ocopy(b - 1).start()
            return 0

        lax.fori_loop(1, n_unit, body, 0)

        @pl.when(jnp.logical_not(has[1]))
        def _():
            q[nx + 1] = jnp.zeros_like(q[nx + 1])

        surface(nx - 2 * UNIT, UNIT)
        sweep2(nx - UNIT, UNIT)
        ocopy(n_unit - 1).start()
        surface(nx - UNIT, UNIT)

        flat = table.reshape((nx + UNIT) * 8, ny)
        for c in range(3):
            hi, lo = split(flat[pl.ds(UNIT * 8 + c, nx, stride=8), :])
            parts[pl.ds(c * nx, nx), pl.ds(0, ny)] = hi
            parts[pl.ds(c * nx, nx), pl.ds(ny, ny)] = lo
        asked = requests[...]

        share = n_track // 4

        def rcopy(n):
            part = pl.ds(n * share, share)
            return pltpu.make_async_copy(reply.at[part], reply_out.at[part], rsem.at[n])

        def answer(j, values):
            for c in range(3):
                reply[j // per, pl.ds(c * per + j % per, 1), :] = values[c]
            if (j + 1) % (share * per) == 0:
                rcopy(j // (share * per)).start()

        look_up_all(parts[...], asked & (ny - 1), lax.shift_right_logical(asked, int(math.log2(ny))), nx, ny, answer)
        for n in range(4):
            rcopy(n).wait()
        for c in range(n_chunk):
            ocopy(c).wait()

    f32 = jnp.float32
    vm = pl.BlockSpec(memory_space=pltpu.VMEM)
    hbm = pl.BlockSpec(memory_space=pltpu.HBM)
    plane = pltpu.VMEM((ny, nz), f32)
    edge = pltpu.VMEM((UNIT, rows, nz), f32)
    return pl.pallas_call(
        kernel,
        out_shape=(
            jax.ShapeDtypeStruct((nx, ny, nz), f32),
            jax.ShapeDtypeStruct((n_track, 3 * per, 128), f32),
        ),
        in_specs=[hbm, hbm] + [vm] * 8 + [pl.BlockSpec(memory_space=pl.ANY)],
        out_specs=(hbm, hbm),
        scratch_shapes=[
            pltpu.VMEM((n_track, 3 * per, 128), f32), pltpu.SemaphoreType.DMA((4,)),
            pltpu.VMEM((nx + UNIT, 8, ny), f32), pltpu.VMEM((3 * nx, 2 * ny), jnp.bfloat16),
            pltpu.VMEM((nx + 4, rows, nz), f32), pltpu.VMEM((nx + 2, rows, nz), f32),
            pltpu.VMEM((nx + 2, ny, nz), f32), pltpu.VMEM((nx + UNIT, ny, nz), f32),
            plane, plane, plane, plane, edge, edge, edge, edge,
            pltpu.SemaphoreType.DMA((nx // chunk,)), pltpu.SemaphoreType.DMA((nx // chunk,)),
            pltpu.SemaphoreType.DMA((nx // chunk,)),
        ],
        compiler_params=pltpu.CompilerParams(vmem_limit_bytes=LARGE),
        cost_estimate=pl.CostEstimate(flops=nx * ny * nz * 100, bytes_accessed=nx * ny * nz * 12, transcendentals=nx * ny * nz * 10),
        name="relax",
    )


def pack_call(nx, ny, nz):
    def kernel(p_hbm, s_hbm, head_a, head_b, track_lo, track_hi, p_lo, p_hi, s_lo, s_hi, sem):
        odd = place()[4]
        copies = []
        for i, (out, low) in enumerate(((head_a, odd), (head_b, 1 - odd))):
            at_p = jnp.where(low > 0, 0, nx - 2)
            at_s = jnp.where(low > 0, 0, nx - 1)
            copies += [
                pltpu.make_async_copy(p_hbm.at[at_p], out.at[pl.ds(0, ny)], sem.at[3 * i]),
                pltpu.make_async_copy(p_hbm.at[at_p + 1], out.at[pl.ds(ny, ny)], sem.at[3 * i + 1]),
                pltpu.make_async_copy(s_hbm.at[at_s], out.at[pl.ds(2 * ny, ny)], sem.at[3 * i + 2]),
            ]
        rows = [(p_hbm, 0, p_lo), (p_hbm, ny - 8, p_hi), (s_hbm, 0, s_lo), (s_hbm, ny - 8, s_hi)]
        copies += [
            pltpu.make_async_copy(src.at[:, pl.ds(at, 8)], dst, sem.at[6 + i])
            for i, (src, at, dst) in enumerate(rows)
        ]
        for copy in copies:
            copy.start()
        head_a[pl.ds(3 * ny, 8), :] = jnp.zeros((8, nz), F32)
        head_b[pl.ds(3 * ny, 8), :] = jnp.zeros((8, nz), F32)
        for copy in copies[6:]:
            copy.wait()
        for out, p_ref, s_ref, order in ((track_lo, p_lo, s_lo, (0, 1)), (track_hi, p_hi, s_hi, (7, 6))):
            p2 = p_ref.reshape(nx * 8, nz)
            s2 = s_ref.reshape(nx * 8, nz)
            out[pl.ds(0, nx), :] = p2[pl.ds(order[0], nx, stride=8), :]
            out[pl.ds(nx, nx), :] = p2[pl.ds(order[1], nx, stride=8), :]
            out[pl.ds(2 * nx, nx), :] = s2[pl.ds(order[0], nx, stride=8), :]
            out[pl.ds(3 * nx, 8), :] = jnp.zeros((8, nz), F32)
        for copy in copies[:6]:
            copy.wait()

    head = jax.ShapeDtypeStruct((3 * ny + 8, nz), F32)
    track = jax.ShapeDtypeStruct((3 * nx + 8, nz), F32)
    eight = pltpu.VMEM((nx, 8, nz), F32)
    return pl.pallas_call(
        kernel,
        out_shape=(head, head, track, track),
        in_specs=[HBM, HBM],
        out_specs=(VM,) * 4,
        scratch_shapes=[eight] * 4 + [pltpu.SemaphoreType.DMA((10,))],
        compiler_params=pltpu.CompilerParams(vmem_limit_bytes=LARGE),
        cost_estimate=cost(10**6, 4 * 2**20),
        name="pack",
    )


def ends_call(ny, n_tiles):
    def kernel(m_ref, a_in, b_in, head_a, head_b):
        flags = place()
        for out, low in ((head_a, flags[4]), (head_b, 1 - flags[4])):
            for c in range(3):
                first = m_ref[pl.ds(c * n_tiles, 1), :]
                last = m_ref[pl.ds((c + 1) * n_tiles - 1, 1), :]
                out[pl.ds(3 * ny + c, 1), :] = jnp.where(low > 0, first, last)

    head = jax.ShapeDtypeStruct((3 * ny + 8, LANES), F32)
    return pl.pallas_call(
        kernel, out_shape=(head, head), in_specs=[VM, VM, VM], out_specs=(VM, VM),
        input_output_aliases={1: 0, 2: 1},
        compiler_params=pltpu.CompilerParams(vmem_limit_bytes=SMALL),
        cost_estimate=cost(10**5, 10**5), name="ends",
    )


def corner_call(nx, ny, nz):
    def kernel(lo_in, hi_in, from_a, from_b, lo, hi):
        odd = place()[4] > 0
        for src, dst, row in ((lo_in, lo, 0), (hi_in, hi, ny - 1)):
            dst[pl.ds(0, 3 * nx), :] = src[pl.ds(0, 3 * nx), :]
            dst[pl.ds(3 * nx, 8), :] = jnp.zeros((8, nz), F32)
            below = pl.ds(ny + row, 1)
            above = pl.ds(row, 1)
            dst[pl.ds(3 * nx, 1), :] = jnp.where(odd, from_a[below, :], from_b[below, :])
            dst[pl.ds(3 * nx + 1, 1), :] = jnp.where(odd, from_b[above, :], from_a[above, :])

    track = jax.ShapeDtypeStruct((3 * nx + 8, nz), F32)
    return pl.pallas_call(
        kernel, out_shape=(track, track), in_specs=[VM] * 4, out_specs=(VM, VM),
        compiler_params=pltpu.CompilerParams(vmem_limit_bytes=SMALL),
        cost_estimate=cost(10**5, 2**20), name="corners",
    )


def request_call(n_track, n_tiles, cells, width, cap):
    slot_rows = n_track * cap // LANES

    def kernel(foot, index, profile, requests, slots, target):
        fp = foot[...]
        owner = lax.shift_right_logical(fp, int(math.log2(cells)))
        cell = fp & (cells - 1)
        marks = [(owner == o).astype(F32) for o in range(n_track)]
        stacked = jnp.concatenate(marks, axis=0).astype(BF16)
        row = lax.broadcasted_iota(jnp.int32, (LANES, LANES), 0)
        col = lax.broadcasted_iota(jnp.int32, (LANES, LANES), 1)
        within = mm(stacked, (row < col).astype(F32).astype(BF16))
        totals = mm(stacked, jnp.ones((LANES, LANES), BF16)).astype(BF16)
        t_row = lax.broadcasted_iota(jnp.int32, (n_tiles, n_tiles), 0)
        t_col = lax.broadcasted_iota(jnp.int32, (n_tiles, n_tiles), 1)
        lower = (t_col < t_row).astype(F32).astype(BF16)
        rank = jnp.zeros((n_tiles, LANES), F32)
        for o in range(n_track):
            part = slice(o * n_tiles, (o + 1) * n_tiles)
            rank = rank + marks[o] * (within[part] + mm(lower, totals[part]))
        slot = owner * cap + rank.astype(jnp.int32)
        slots[...] = slot
        at_row = lax.shift_right_logical(slot, int(math.log2(LANES)))
        at_lane = slot & (LANES - 1)
        high = lax.shift_right_logical(cell, int(math.log2(width))).astype(F32)
        low = (cell & (width - 1)).astype(F32)
        rows = lax.broadcasted_iota(jnp.int32, (slot_rows, LANES), 0)
        found = jnp.zeros((2 * slot_rows, LANES), F32)
        row_b = row.astype(F32).astype(BF16)
        lane_b = at_lane.astype(F32).astype(BF16)
        for k in range(0, n_tiles, 2):
            values = []
            lanes = []
            for i in (k, k + 1):
                here = rows == at_row[i : i + 1]
                parts = [jnp.where(here, v[i : i + 1], 0.0) for v in (high, low)]
                values.append(jnp.concatenate(parts, axis=0).astype(BF16))
                lanes.append(jnp.where(row_b == lane_b[i : i + 1], jnp.array(1, BF16), jnp.array(0, BF16)))
            found = found + mm_nt(jnp.concatenate(values, axis=1), jnp.concatenate(lanes, axis=1))
        requests[...] = found[:slot_rows] * float(width) + found[slot_rows:]
        spread = jnp.broadcast_to(profile[...], (n_tiles, profile.shape[1]))
        temp = jnp.take_along_axis(spread, index[...], axis=1)
        target[...] = 0.05 + jnp.maximum(1.0 - temp, 0.0)

    tiles = (n_tiles, LANES)
    return pl.pallas_call(
        kernel,
        out_shape=(
            jax.ShapeDtypeStruct((slot_rows, LANES), F32),
            jax.ShapeDtypeStruct(tiles, jnp.int32),
            jax.ShapeDtypeStruct(tiles, F32),
        ),
        in_specs=[VM] * 3,
        out_specs=(VM,) * 3,
        compiler_params=pltpu.CompilerParams(vmem_limit_bytes=SMALL),
        cost_estimate=cost(10**8, 2**20),
        name="requests",
    )


def look_up(table, lane, row, rows, width):
    n = lane.shape[1]
    lanes = lax.broadcasted_iota(jnp.int32, (width, n), 0).astype(F32).astype(BF16)
    here = jnp.where(lanes == lane.astype(F32).astype(BF16), jnp.array(1, BF16), jnp.array(0, BF16))
    got = mm(table, jnp.concatenate([here, here], axis=0))
    mine = lax.broadcasted_iota(jnp.int32, (rows, n), 0) == row
    return [
        jnp.sum(jnp.where(mine, got[c * rows : (c + 1) * rows], 0.0), axis=0, keepdims=True) for c in range(3)
    ]


def look_up_all(table, lane, row, rows, width, store):
    for j in range(0, lane.shape[0], 2):
        pair = [jnp.concatenate([v[j : j + 1], v[j + 1 : j + 2]], axis=1) for v in (lane, row)]
        values = look_up(table, pair[0], pair[1], rows, width)
        for i in range(2):
            store(j + i, [v[:, i * LANES : (i + 1) * LANES] for v in values])


def llb(m, field, target):
    sq = m[0] * m[0] + m[1] * m[1] + m[2] * m[2]
    pull = 0.5 * (1.0 - sq / target)
    h = [field[c] + pull * m[c] for c in range(3)]

    def cross(a, b):
        return [a[(c + 1) % 3] * b[(c + 2) % 3] - a[(c + 2) % 3] * b[(c + 1) % 3] for c in range(3)]

    turn = cross(m, h)
    damp = cross(m, turn)
    along = m[0] * h[0] + m[1] * h[1] + m[2] * h[2]
    return [m[c] + 0.1 * (0.3 * along * m[c] - turn[c] - 0.5 * damp[c]) for c in range(3)]


def fold(by_hi, by_lo):
    return (by_hi[8:16] + by_lo[0:8]) + by_hi[0:8]


def tile_major(m_ref, tiles_ref, n_tiles):
    tiles_ref[...] = jnp.zeros_like(tiles_ref)
    flat = tiles_ref.reshape((n_tiles + 2) * 8, LANES)
    for c in range(3):
        flat[pl.ds(8 + c, n_tiles, stride=8), :] = m_ref[pl.ds(c * n_tiles, n_tiles), :]


def exchange(tiles_ref, own, nxt, k):
    here = jnp.concatenate([both(tiles_ref[k + 1]), both(tiles_ref[k])], axis=1)
    high = both(tiles_ref[k + 2])
    own_hi, own_lo = split(own)
    nxt_hi, nxt_lo = split(nxt)
    field = fold(
        mm_nt(here, jnp.concatenate([own_hi, nxt_hi], axis=1)),
        mm_nt(here, jnp.concatenate([own_lo, nxt_lo], axis=1)),
    )
    return field + fold(mm(high, nxt_hi), mm(high, nxt_lo))


def first_call(n_tiles, ny, start, count):
    step = 4
    chunks = count // step

    def kernel(own_hbm, nxt_hbm, m_ref, from_a, from_b, ex, own, nxt, tiles, sem):
        def copies(c):
            part = pl.ds(c * step, step)
            return [
                pltpu.make_async_copy(own_hbm.at[pl.ds(start + c * step, step)], own.at[part], sem.at[0, c]),
                pltpu.make_async_copy(nxt_hbm.at[pl.ds(start + c * step, step)], nxt.at[part], sem.at[1, c]),
            ]

        for c in range(chunks):
            for copy in copies(c):
                copy.start()
        tile_major(m_ref, tiles, n_tiles)
        flags = place()
        odd = flags[4] > 0
        by_a = from_a[pl.ds(3 * ny, 8), :]
        by_b = from_b[pl.ds(3 * ny, 8), :]
        tiles[0] = jnp.where(flags[0] > 0, jnp.where(odd, by_a, by_b), 0.0)
        tiles[n_tiles + 1] = jnp.where(flags[1] > 0, jnp.where(odd, by_b, by_a), 0.0)
        for c in range(chunks):
            for copy in copies(c):
                copy.wait()
            for k in range(c * step, (c + 1) * step):
                field = exchange(tiles, own[k], nxt[k], start + k)
                for n in range(3):
                    ex[pl.ds(n * count + k, 1), :] = field[n : n + 1]

    return pl.pallas_call(
        kernel,
        out_shape=jax.ShapeDtypeStruct((3 * count, LANES), F32),
        in_specs=[HBM, HBM, VM, VM, VM],
        out_specs=VM,
        scratch_shapes=[
            pltpu.VMEM((count, LANES, LANES), F32),
            pltpu.VMEM((count, LANES, LANES), F32),
            pltpu.VMEM((n_tiles + 2, 8, LANES), F32),
            pltpu.SemaphoreType.DMA((2, chunks)),
        ],
        compiler_params=pltpu.CompilerParams(vmem_limit_bytes=LARGE),
        cost_estimate=cost(1, 1),
        name="couple_first",
    )


def section_call(n_tiles, n_track, cap):
    per = cap // LANES
    slot_rows = n_track * per

    def kernel(answers, slots, m_ref, ex_a, ex_b, target, applied, m_out, edge_a, edge_b, parts):
        for c in range(3):
            rows = jnp.concatenate([answers[o, pl.ds(c * per, per), :] for o in range(n_track)], axis=0)
            hi, lo = split(rows)
            parts[pl.ds(c * slot_rows, slot_rows), pl.ds(0, LANES)] = hi
            parts[pl.ds(c * slot_rows, slot_rows), pl.ds(LANES, LANES)] = lo
        table = parts[...]
        slot = slots[...]
        at_row = lax.shift_right_logical(slot, int(math.log2(LANES)))
        at_lane = slot & (LANES - 1)

        def store(k, values):
            for c in range(3):
                applied[pl.ds(c * n_tiles + k, 1), :] = values[c]

        look_up_all(table, at_lane, at_row, slot_rows, LANES, store)
        part = [pl.ds(c * n_tiles, n_tiles) for c in range(3)]
        m = [m_ref[part[c], :] for c in range(3)]
        half = n_tiles // 2
        ex = [
            jnp.concatenate([ref[pl.ds(c * half, half), :] for ref in (ex_a, ex_b)], axis=0) for c in range(3)
        ]
        m = llb(m, [applied[part[c], :] + ex[c] for c in range(3)], target[...])
        odd = place()[4] > 0
        edge_a[...] = jnp.zeros((8, LANES), F32)
        edge_b[...] = jnp.zeros((8, LANES), F32)
        for c in range(3):
            m_out[part[c], :] = m[c]
            edge_a[pl.ds(c, 1), :] = jnp.where(odd, m[c][0:1], m[c][n_tiles - 1 :])
            edge_b[pl.ds(c, 1), :] = jnp.where(odd, m[c][n_tiles - 1 :], m[c][0:1])

    grains = jax.ShapeDtypeStruct((3 * n_tiles, LANES), F32)
    edge = jax.ShapeDtypeStruct((8, LANES), F32)
    return pl.pallas_call(
        kernel,
        out_shape=(grains, grains, edge, edge),
        in_specs=[VM] * 6,
        out_specs=(VM,) * 4,
        scratch_shapes=[pltpu.VMEM((3 * slot_rows, 2 * LANES), BF16)],
        compiler_params=pltpu.CompilerParams(vmem_limit_bytes=SMALL),
        cost_estimate=cost(10**9, 2**20),
        name="section_first",
    )


def second_call(n_tiles):
    def kernel(own, nxt, m_ref, ex, tiles):
        tile_major(m_ref, tiles, n_tiles)
        for k in range(n_tiles):
            field = exchange(tiles, own[k], nxt[k], k)
            for n in range(3):
                ex[pl.ds(n * n_tiles + k, 1), :] = field[n : n + 1]

    return pl.pallas_call(
        kernel,
        out_shape=jax.ShapeDtypeStruct((3 * n_tiles, LANES), F32),
        in_specs=[VM] * 3,
        out_specs=VM,
        scratch_shapes=[pltpu.VMEM((n_tiles + 2, 8, LANES), F32)],
        compiler_params=pltpu.CompilerParams(vmem_limit_bytes=SMALL),
        cost_estimate=cost(10**9, 4 * 2**20),
        name="couple_second",
    )


def last_call(n_tiles):
    def kernel(m_ref, ex, applied, target, from_a, from_b, nxt, out):
        flags = place()
        odd = flags[4] > 0
        below = jnp.where(odd, from_a[...], from_b[...])
        above = jnp.where(odd, from_b[...], from_a[...])
        low = both(jnp.where(flags[0] > 0, below, 0.0))
        high = both(jnp.where(flags[1] > 0, above, 0.0))
        hi, lo = split(nxt[0])
        first = fold(mm_nt(low, hi), mm_nt(low, lo))
        hi, lo = split(nxt[n_tiles - 1])
        last = fold(mm(high, hi), mm(high, lo))
        at = lax.broadcasted_iota(jnp.int32, (n_tiles, LANES), 0)
        field = []
        m = []
        for c in range(3):
            part = pl.ds(c * n_tiles, n_tiles)
            extra = jnp.where(at == 0, first[c : c + 1], 0.0) + jnp.where(at == n_tiles - 1, last[c : c + 1], 0.0)
            field.append(applied[part, :] + (ex[part, :] + extra))
            m.append(m_ref[part, :])
        m = llb(m, field, target[...])
        for c in range(3):
            out[pl.ds(c * n_tiles, n_tiles), :] = m[c]

    return pl.pallas_call(
        kernel,
        out_shape=jax.ShapeDtypeStruct((3 * n_tiles, LANES), F32),
        in_specs=[VM] * 7,
        out_specs=VM,
        compiler_params=pltpu.CompilerParams(vmem_limit_bytes=SMALL),
        cost_estimate=cost(10**7, 2**20),
        name="section_last",
    )


def shifted(v, axis, by):
    n = lax.axis_size(axis)
    return lax.ppermute(v, axis, [(i, (i + by) % n) for i in range(n)])


def traded(to_a, to_b, axis):
    n = lax.axis_size(axis)
    first = [(i, i ^ 1) for i in range(n)]
    second = [(i, (i + 1) % n if i % 2 else (i - 1) % n) for i in range(n)]
    return lax.ppermute(to_a, axis, first), lax.ppermute(to_b, axis, second)


def cells_call(rows):
    def kernel(asked, ex, cells):
        cells[...] = asked[...].astype(jnp.int32)

    return pl.pallas_call(
        kernel, out_shape=jax.ShapeDtypeStruct((rows, LANES), jnp.int32), in_specs=[VM, ANY], out_specs=VM,
        compiler_params=pltpu.CompilerParams(vmem_limit_bytes=SMALL),
        cost_estimate=cost(10**9, 4 * 2**20), name="cells",
    )


def per_device(
    potential, source, depth_kernel, magnet, footprint, temp_index, temp_profile, self_tiles, next_tiles
):
    nx, ny, nz = potential.shape
    n_track = lax.axis_size("track")
    n_tiles = self_tiles.shape[1]
    grains = footprint.shape[1]
    cap = 2 * grains // n_track
    state = magnet.reshape(3 * n_tiles, LANES)

    head_a, head_b, track_lo, track_hi = pack_call(nx, ny, nz)(potential, source)
    head_a, head_b = ends_call(ny, n_tiles)(state, head_a, head_b)
    from_a, from_b = traded(head_a, head_b, "head")
    requests, slots, target = request_call(n_track, n_tiles, nx * ny, ny, cap)(
        footprint.reshape(n_tiles, LANES), temp_index.reshape(n_tiles, LANES), temp_profile[None, :]
    )
    track_lo, track_hi = corner_call(nx, ny, nz)(track_lo, track_hi, from_a, from_b)
    left = shifted(track_hi, "track", 1)
    right = shifted(track_lo, "track", -1)
    asked = lax.all_to_all(requests.reshape(n_track, cap // LANES, LANES), "track", 0, 0)

    kern = jnp.pad(depth_kernel, ((0, 5), (0, 0)))
    half = n_tiles // 2
    couplings = (self_tiles[0], next_tiles[0], state, from_a, from_b)
    ex_a = first_call(n_tiles, ny, 0, half)(*couplings)
    asked = cells_call(n_track * cap // LANES)(asked.reshape(n_track * cap // LANES, LANES), ex_a)
    relaxed, reply = relax_call(nx, ny, nz, n_track, cap)(
        potential, source, from_a, from_b, left, right, track_lo, track_hi, kern,
        asked, ex_a,
    )
    answers = lax.all_to_all(reply, "track", 0, 0)
    ex_b = first_call(n_tiles, ny, half, n_tiles - half)(*couplings)
    applied, state, edge_a, edge_b = section_call(n_tiles, n_track, cap)(
        answers, slots, state, ex_a, ex_b, target
    )
    tile_a, tile_b = traded(edge_a, edge_b, "head")
    ex = second_call(n_tiles)(self_tiles[0], next_tiles[0], state)
    state = last_call(n_tiles)(
        state, ex, applied, target, tile_a, tile_b, next_tiles[0]
    )
    return relaxed, state.reshape(3, 1, grains)


def solution(mesh):
    in_specs = (
        P("head", "track", None),
        P("head", "track", None),
        P(),
        P(None, "track", "head"),
        P("track", "head"),
        P("track", "head"),
        P(),
        P("track", "head", None, None),
        P("track", "head", None, None),
    )
    out_specs = (P("head", "track", None), P(None, "track", "head"))
    return jax.shard_map(
        per_device, mesh=mesh, in_specs=in_specs, out_specs=out_specs, check_vma=False
    )
```

```python
import math

import jax
import jax.numpy as jnp
from jax import lax
from jax.experimental import pallas as pl
from jax.experimental.pallas import tpu as pltpu
from jax.sharding import PartitionSpec as P

F32 = jnp.float32
BF16 = jnp.bfloat16
STRIP = 16
UNIT = 4
TOP = 8
AHEAD = 6
LANES = 128
SMALL = 16 * 2**20
LARGE = 52 * 2**20
NT = (((1,), (1,)), ((), ()))
VM = pl.BlockSpec(memory_space=pltpu.VMEM)
SM = pl.BlockSpec(memory_space=pltpu.SMEM)
HBM = pl.BlockSpec(memory_space=pltpu.HBM)
ANY = pl.BlockSpec(memory_space=pl.ANY)


def mm(a, b):
    return jnp.dot(a, b, preferred_element_type=F32)


def mm_nt(a, b):
    return lax.dot_general(a, b, NT, preferred_element_type=F32)


def split(v):
    hi = v.astype(BF16)
    return hi, (v - hi.astype(F32)).astype(BF16)


def place():
    h = lax.axis_index("head")
    t = lax.axis_index("track")
    flags = (h > 0, h < lax.axis_size("head") - 1, t > 0, t < lax.axis_size("track") - 1, h % 2 == 1)
    return [flag.astype(jnp.int32) for flag in flags]


def cost(flops, moved):
    return pl.CostEstimate(flops=flops, bytes_accessed=moved, transcendentals=0)


def rcp(v):
    return pl.reciprocal(v, approx=True)


def flux(d):
    mu = 1.0 + rcp(0.25 + d * d)
    return mu * d, mu


def z_flux(c):
    lane = lax.broadcasted_iota(jnp.int32, c.shape, c.ndim - 1)
    n = c.shape[-1]
    zl = jnp.where(lane == 0, 0.0, pltpu.roll(c, 1, c.ndim - 1))
    zr = jnp.where(lane == n - 1, 0.0, pltpu.roll(c, n - 1, c.ndim - 1))
    fl, ml = flux(zl - c)
    fr, mr = flux(zr - c)
    return fl + fr, ml + mr


def both(v):
    hi = v.astype(jnp.bfloat16).astype(jnp.float32)
    return jnp.concatenate([hi, v - hi], axis=0).astype(jnp.bfloat16)


def finish(c, numer, denom):
    return c + 0.8 * (numer * rcp(denom))


def sweep(a, x, planes, strips, fx, mx, fy, my, src, store):
    for u in range(planes):
        for k in strips:
            if k - 1 not in strips:
                row = TOP + k * STRIP - 8
                f, mu = flux(a[x + u, pl.ds(row + 1, 8), :] - a[x + u, pl.ds(row, 8), :])
                fy[u, pl.ds(row, 8), :] = f
                my[u, pl.ds(row, 8), :] = mu
    for k in strips:
        here = pl.ds(TOP + k * STRIP, STRIP)
        before = pl.ds(TOP + k * STRIP - 1, STRIP)
        after = pl.ds(TOP + k * STRIP + 1, STRIP)
        flat = pl.ds(k * STRIP, STRIP)
        c = a[x, here, :]
        fp = fx[flat, :]
        mp = mx[flat, :]
        for u in range(planes):
            up = a[x + u + 1, here, :]
            f, mu = flux(up - c)
            numer = f - fp
            denom = mu + mp
            fp, mp = f, mu
            f, mu = flux(a[x + u, after, :] - c)
            fy[u, here, :] = f
            my[u, here, :] = mu
            numer = numer + (f - fy[u, before, :])
            denom = denom + (mu + my[u, before, :])
            f, mu = z_flux(c)
            numer = numer + (f + src[u, flat, :])
            denom = denom + (mu + 1.0)
            store(u, k, finish(c, numer, denom))
            c = up
        fx[flat, :] = fp
        mx[flat, :] = mp


def first_x(a, x, strips, fx, mx):
    for k in strips:
        here = pl.ds(TOP + k * STRIP, STRIP)
        flat = pl.ds(k * STRIP, STRIP)
        f, mu = flux(a[x + 1, here, :] - a[x, here, :])
        fx[flat, :] = f
        mx[flat, :] = mu


def keep(flag, v):
    return jnp.where(flag, v, 0.0)


def head_planes(from_a, from_b, ny, flags, side):
    swap = flags[4] > 0 if side == 0 else flags[4] == 0
    planes = [jnp.where(swap, from_a[pl.ds(n * ny, ny), :], from_b[pl.ds(n * ny, ny), :]) for n in range(3)]
    return [keep(flags[side] > 0, planes[0]), keep(flags[side] > 0, planes[1]), planes[2]]


def inner_call(nx, ny, nz):
    n_strip = ny // STRIP
    strips = range(1, n_strip - 1)
    inner = ny - 2 * STRIP
    n_unit = nx // UNIT

    def kernel(p_hbm, s_hbm, from_a, from_b, q_hbm, token, pe, q, sb, fx, mx, fy, my, psem, ssem, qsem):
        flags = place()

        def pcopy(c):
            return pltpu.make_async_copy(
                p_hbm.at[pl.ds(c * UNIT, UNIT), pl.ds(8, ny - 16)],
                pe.at[pl.ds(2 + c * UNIT, UNIT), pl.ds(TOP + 8, ny - 16)], psem.at[c])

        def scopy(c):
            return pltpu.make_async_copy(
                s_hbm.at[pl.ds(c * UNIT, UNIT), pl.ds(STRIP, inner)],
                sb.at[pl.ds(1 + c * UNIT, UNIT), pl.ds(STRIP, inner)], ssem.at[c])

        def qcopy(c):
            return pltpu.make_async_copy(q.at[pl.ds(2 + c * UNIT, UNIT)], q_hbm.at[pl.ds(2 + c * UNIT, UNIT)], qsem.at[c])

        first = pltpu.make_async_copy(q.at[pl.ds(0, 2)], q_hbm.at[pl.ds(0, 2)], qsem.at[n_unit])

        def fetch(c):
            pcopy(c).start()
            scopy(c).start()

        for c in range(n_unit):
            fetch(c)
        token[...] = jnp.zeros_like(token)
        for side, (at, to) in enumerate((((0, 1), 0), ((nx + 2, nx + 3), nx + 1))):
            planes = head_planes(from_a, from_b, ny, flags, side)
            pe[at[0], pl.ds(TOP, ny), :] = planes[0]
            pe[at[1], pl.ds(TOP, ny), :] = planes[1]
            sb[to, :, :] = planes[2]

        def part(x, planes, at=None, flag=None):
            def store(u, k, v):
                q[x + u + 1, pl.ds((k - 1) * STRIP, STRIP), :] = keep(flag, v) if u == at else v

            sweep(pe, x + 2, planes, strips, fx, mx, fy, my, sb.at[pl.ds(x + 1, planes)], store)

        for c in range(2):
            pcopy(c).wait()
            scopy(c).wait()
        first_x(pe, 0, strips, fx, mx)
        part(-1, UNIT + 2, 0, flags[0] > 0)
        first.start()
        qcopy(0).start()

        def body(b, _):
            pcopy(b + 1).wait()
            scopy(b + 1).wait()
            part(b * UNIT + 1, UNIT)
            qcopy(b).start()
            return 0

        lax.fori_loop(1, n_unit - 1, body, 0)
        part((n_unit - 1) * UNIT + 1, UNIT, UNIT - 1, flags[1] > 0)
        qcopy(n_unit - 1).start()
        first.wait()
        for c in range(n_unit):
            qcopy(c).wait()

    plane = pltpu.VMEM((ny, nz), F32)
    edge = pltpu.VMEM((UNIT + 2, ny + 2 * TOP, nz), F32)
    return pl.pallas_call(
        kernel,
        out_shape=(jax.ShapeDtypeStruct((nx + 2, inner, nz), F32), jax.ShapeDtypeStruct((8, LANES), F32)),
        in_specs=[HBM, HBM, VM, VM],
        out_specs=(HBM, VM),
        scratch_shapes=[
            pltpu.VMEM((nx + 4, ny + 2 * TOP, nz), F32), pltpu.VMEM((nx + 2, inner, nz), F32),
            pltpu.VMEM((nx + 2, ny, nz), F32), plane, plane, edge, edge,
            pltpu.SemaphoreType.DMA((n_unit,)), pltpu.SemaphoreType.DMA((n_unit,)),
            pltpu.SemaphoreType.DMA((n_unit + 1,)),
        ],
        compiler_params=pltpu.CompilerParams(vmem_limit_bytes=LARGE),
        cost_estimate=cost(1, 1),
        name="sweep_inner",
    )


def relax_call(nx, ny, nz, n_track, cap):
    chunk = UNIT
    per = cap // LANES
    rows = ny + 2 * TOP

    def kernel(p_hbm, s_hbm, from_a, from_b, tlo, thi, own_lo, own_hi, kern, requests, q_hbm, o_hbm, reply_out,
               reply, rsem, table, parts, pe, q, sb, ob, fx1, mx1, fx2, mx2, fy1, my1, fy2, my2, psem, ssem, osem, qsem):
        n_chunk = nx // chunk

        reach = STRIP + 8
        inner = ny - 2 * STRIP
        ends = (0, ny // STRIP - 1)
        whole = range(ny // STRIP)

        def pcopies(c):
            return [
                pltpu.make_async_copy(
                    p_hbm.at[pl.ds(c * chunk, chunk), pl.ds(row, reach)],
                    pe.at[pl.ds(2 + c * chunk, chunk), pl.ds(TOP + row, reach)], psem.at[n, c])
                for n, row in enumerate((0, ny - reach))
            ]

        def qcopy(c):
            return pltpu.make_async_copy(q_hbm.at[pl.ds(2 + c * chunk, chunk)],
                                         q.at[pl.ds(2 + c * chunk, chunk), pl.ds(TOP + STRIP, inner)], qsem.at[c])

        qfirst = pltpu.make_async_copy(q_hbm.at[pl.ds(0, 2)], q.at[pl.ds(0, 2), pl.ds(TOP + STRIP, inner)],
                                       qsem.at[nx // chunk])

        def scopy(c):
            return pltpu.make_async_copy(s_hbm.at[pl.ds(c * chunk, chunk)],
                                         sb.at[pl.ds(1 + c * chunk, chunk)], ssem.at[c])

        def ocopy(c):
            return pltpu.make_async_copy(ob.at[pl.ds(c * chunk + UNIT, chunk)],
                                         o_hbm.at[pl.ds(c * chunk, chunk)], osem.at[c])

        def fetch(c):
            for copy in pcopies(c):
                copy.start()
            scopy(c).start()
            qcopy(c).start()

        def arrive(c):
            for copy in pcopies(c):
                copy.wait()
            scopy(c).wait()
            qcopy(c).wait()

        qfirst.start()
        for c in range(AHEAD):
            fetch(c)

        flags = place()
        has = [flags[n] > 0 for n in range(4)]

        main = pl.ds(TOP, ny)
        odd = flags[4] > 0
        for side, (at, to) in enumerate((((0, 1), 0), ((nx + 2, nx + 3), nx + 1))):
            swap = odd if side == 0 else jnp.logical_not(odd)
            planes = [
                jnp.where(swap, from_a[pl.ds(n * ny, ny), :], from_b[pl.ds(n * ny, ny), :]) for n in range(3)
            ]
            pe[at[0], main, :] = keep(has[side], planes[0])
            pe[at[1], main, :] = keep(has[side], planes[1])
            sb[to, :, :] = planes[2]
        pe2 = pe.reshape((nx + 4) * rows, nz)
        q2 = q.reshape((nx + 2) * rows, nz)
        for side, (ref, own, row) in enumerate(((tlo, own_lo, TOP - 1), (thi, own_hi, TOP + ny))):
            flag = has[2 + side]
            c = keep(flag, ref[pl.ds(0, nx), :])
            far = keep(flag, ref[pl.ds(nx, nx), :])
            src = ref[pl.ds(2 * nx, nx), :]
            near = own[pl.ds(0, nx), :]
            corners = keep(flag, ref[pl.ds(3 * nx, 8), :])
            below = keep(has[0], corners[0:1])
            above = keep(has[1], corners[1:2])
            ix = lax.broadcasted_iota(jnp.int32, c.shape, 0)
            xl = jnp.where(ix == 0, below, pltpu.roll(c, 1, 0))
            xr = jnp.where(ix == nx - 1, above, pltpu.roll(c, nx - 1, 0))
            numer, denom = z_flux(c)
            numer = numer + src
            denom = denom + 1.0
            for other in (far, near, xl, xr):
                f, mu = flux(other - c)
                numer = numer + f
                denom = denom + mu
            pe2[pl.ds(2 * rows + row, nx, stride=rows), :] = c
            pe2[pl.ds(rows + row, 1), :] = below
            pe2[pl.ds((nx + 2) * rows + row, 1), :] = above
            q2[pl.ds(rows + row, nx, stride=rows), :] = keep(flag, finish(c, numer, denom))

        def sweep1(x, planes, flag=None):
            def store(u, k, v):
                q[x + u + 1, pl.ds(TOP + k * STRIP, STRIP), :] = v if flag is None else keep(flag, v)

            sweep(pe, x + 2, planes, ends, fx1, mx1, fy1, my1, sb.at[pl.ds(x + 1, planes)], store)

        kk = both(kern[...])

        def sweep2(x, planes):
            def store(u, k, v):
                ob[x + u + UNIT, pl.ds(k * STRIP, STRIP), :] = v

            sweep(q, x + 1, planes, whole, fx2, mx2, fy2, my2, sb.at[pl.ds(x + 1, planes)], store)

        def surface(x, planes):
            nt = (((1,), (1,)), ((), ()))
            for u in range(planes):
                v = ob[x + u + UNIT]
                hi = v.astype(jnp.bfloat16)
                lo = (v - hi.astype(jnp.float32)).astype(jnp.bfloat16)
                a = lax.dot_general(kk, hi, nt, preferred_element_type=jnp.float32)
                b = lax.dot_general(kk, lo, nt, preferred_element_type=jnp.float32)
                table[x + u + UNIT] = (a[8:16] + b[0:8]) + a[0:8]

        n_unit = nx // UNIT
        qfirst.wait()
        arrive(0)
        first_x(pe, 0, ends, fx1, mx1)
        sweep1(-1, 1, has[0])
        sweep1(0, 1)
        first_x(q, 0, whole, fx2, mx2)
        arrive(1)
        sweep1(1, UNIT)

        def body(b, _):
            @pl.when(b + AHEAD <= n_unit)
            def _():
                fetch(b + AHEAD - 1)

            @pl.when(b < n_unit - 1)
            def _():
                arrive(b + 1)

            surface((b - 2) * UNIT, UNIT)
            sweep2((b - 1) * UNIT, UNIT)
            sweep1(b * UNIT + 1, UNIT)
            ocopy(b - 1).start()
            return 0

        lax.fori_loop(1, n_unit, body, 0)

        @pl.when(jnp.logical_not(has[1]))
        def _():
            q[nx + 1] = jnp.zeros_like(q[nx + 1])

        surface(nx - 2 * UNIT, UNIT)
        sweep2(nx - UNIT, UNIT)
        ocopy(n_unit - 1).start()
        surface(nx - UNIT, UNIT)

        flat = table.reshape((nx + UNIT) * 8, ny)
        for c in range(3):
            hi, lo = split(flat[pl.ds(UNIT * 8 + c, nx, stride=8), :])
            parts[pl.ds(c * nx, nx), pl.ds(0, ny)] = hi
            parts[pl.ds(c * nx, nx), pl.ds(ny, ny)] = lo
        asked = requests[...]

        share = n_track // 4

        def rcopy(n):
            part = pl.ds(n * share, share)
            return pltpu.make_async_copy(reply.at[part], reply_out.at[part], rsem.at[n])

        def answer(j, values):
            for c in range(3):
                reply[j // per, pl.ds(c * per + j % per, 1), :] = values[c]
            if (j + 1) % (share * per) == 0:
                rcopy(j // (share * per)).start()

        look_up_all(parts[...], asked & (ny - 1), lax.shift_right_logical(asked, int(math.log2(ny))), nx, ny, answer)
        for n in range(4):
            rcopy(n).wait()
        for c in range(n_chunk):
            ocopy(c).wait()

    f32 = jnp.float32
    vm = pl.BlockSpec(memory_space=pltpu.VMEM)
    hbm = pl.BlockSpec(memory_space=pltpu.HBM)
    plane = pltpu.VMEM((ny, nz), f32)
    edge = pltpu.VMEM((UNIT, rows, nz), f32)
    return pl.pallas_call(
        kernel,
        out_shape=(
            jax.ShapeDtypeStruct((nx, ny, nz), f32),
            jax.ShapeDtypeStruct((n_track, 3 * per, 128), f32),
        ),
        in_specs=[hbm, hbm] + [vm] * 8 + [hbm],
        out_specs=(hbm, hbm),
        scratch_shapes=[
            pltpu.VMEM((n_track, 3 * per, 128), f32), pltpu.SemaphoreType.DMA((4,)),
            pltpu.VMEM((nx + UNIT, 8, ny), f32), pltpu.VMEM((3 * nx, 2 * ny), jnp.bfloat16),
            pltpu.VMEM((nx + 4, rows, nz), f32), pltpu.VMEM((nx + 2, rows, nz), f32),
            pltpu.VMEM((nx + 2, ny, nz), f32), pltpu.VMEM((nx + UNIT, ny, nz), f32),
            plane, plane, plane, plane, edge, edge, edge, edge,
            pltpu.SemaphoreType.DMA((2, nx // chunk)), pltpu.SemaphoreType.DMA((nx // chunk,)),
            pltpu.SemaphoreType.DMA((nx // chunk,)), pltpu.SemaphoreType.DMA((nx // chunk + 1,)),
        ],
        compiler_params=pltpu.CompilerParams(vmem_limit_bytes=LARGE),
        cost_estimate=pl.CostEstimate(flops=nx * ny * nz * 100, bytes_accessed=nx * ny * nz * 12, transcendentals=nx * ny * nz * 10),
        name="relax",
    )


def pack_call(nx, ny, nz):
    def kernel(p_hbm, s_hbm, head_a, head_b, track_lo, track_hi, p_lo, p_hi, s_lo, s_hi, sem):
        odd = place()[4]
        copies = []
        for i, (out, low) in enumerate(((head_a, odd), (head_b, 1 - odd))):
            at_p = jnp.where(low > 0, 0, nx - 2)
            at_s = jnp.where(low > 0, 0, nx - 1)
            copies += [
                pltpu.make_async_copy(p_hbm.at[at_p], out.at[pl.ds(0, ny)], sem.at[3 * i]),
                pltpu.make_async_copy(p_hbm.at[at_p + 1], out.at[pl.ds(ny, ny)], sem.at[3 * i + 1]),
                pltpu.make_async_copy(s_hbm.at[at_s], out.at[pl.ds(2 * ny, ny)], sem.at[3 * i + 2]),
            ]
        rows = [(p_hbm, 0, p_lo), (p_hbm, ny - 8, p_hi), (s_hbm, 0, s_lo), (s_hbm, ny - 8, s_hi)]
        copies += [
            pltpu.make_async_copy(src.at[:, pl.ds(at, 8)], dst, sem.at[6 + i])
            for i, (src, at, dst) in enumerate(rows)
        ]
        for copy in copies:
            copy.start()
        head_a[pl.ds(3 * ny, 8), :] = jnp.zeros((8, nz), F32)
        head_b[pl.ds(3 * ny, 8), :] = jnp.zeros((8, nz), F32)
        for copy in copies[6:]:
            copy.wait()
        for out, p_ref, s_ref, order in ((track_lo, p_lo, s_lo, (0, 1)), (track_hi, p_hi, s_hi, (7, 6))):
            p2 = p_ref.reshape(nx * 8, nz)
            s2 = s_ref.reshape(nx * 8, nz)
            out[pl.ds(0, nx), :] = p2[pl.ds(order[0], nx, stride=8), :]
            out[pl.ds(nx, nx), :] = p2[pl.ds(order[1], nx, stride=8), :]
            out[pl.ds(2 * nx, nx), :] = s2[pl.ds(order[0], nx, stride=8), :]
            out[pl.ds(3 * nx, 8), :] = jnp.zeros((8, nz), F32)
        for copy in copies[:6]:
            copy.wait()

    head = jax.ShapeDtypeStruct((3 * ny + 8, nz), F32)
    track = jax.ShapeDtypeStruct((3 * nx + 8, nz), F32)
    eight = pltpu.VMEM((nx, 8, nz), F32)
    return pl.pallas_call(
        kernel,
        out_shape=(head, head, track, track),
        in_specs=[HBM, HBM],
        out_specs=(VM,) * 4,
        scratch_shapes=[eight] * 4 + [pltpu.SemaphoreType.DMA((10,))],
        compiler_params=pltpu.CompilerParams(vmem_limit_bytes=LARGE),
        cost_estimate=cost(10**6, 4 * 2**20),
        name="pack",
    )


def ends_call(ny, n_tiles):
    def kernel(m_ref, a_in, b_in, head_a, head_b):
        flags = place()
        for out, low in ((head_a, flags[4]), (head_b, 1 - flags[4])):
            for c in range(3):
                first = m_ref[pl.ds(c * n_tiles, 1), :]
                last = m_ref[pl.ds((c + 1) * n_tiles - 1, 1), :]
                out[pl.ds(3 * ny + c, 1), :] = jnp.where(low > 0, first, last)

    head = jax.ShapeDtypeStruct((3 * ny + 8, LANES), F32)
    return pl.pallas_call(
        kernel, out_shape=(head, head), in_specs=[VM, VM, VM], out_specs=(VM, VM),
        input_output_aliases={1: 0, 2: 1},
        compiler_params=pltpu.CompilerParams(vmem_limit_bytes=SMALL),
        cost_estimate=cost(10**5, 10**5), name="ends",
    )


def corner_call(nx, ny, nz):
    def kernel(lo_in, hi_in, from_a, from_b, lo, hi):
        odd = place()[4] > 0
        for src, dst, row in ((lo_in, lo, 0), (hi_in, hi, ny - 1)):
            dst[pl.ds(0, 3 * nx), :] = src[pl.ds(0, 3 * nx), :]
            dst[pl.ds(3 * nx, 8), :] = jnp.zeros((8, nz), F32)
            below = pl.ds(ny + row, 1)
            above = pl.ds(row, 1)
            dst[pl.ds(3 * nx, 1), :] = jnp.where(odd, from_a[below, :], from_b[below, :])
            dst[pl.ds(3 * nx + 1, 1), :] = jnp.where(odd, from_b[above, :], from_a[above, :])

    track = jax.ShapeDtypeStruct((3 * nx + 8, nz), F32)
    return pl.pallas_call(
        kernel, out_shape=(track, track), in_specs=[VM] * 4, out_specs=(VM, VM),
        compiler_params=pltpu.CompilerParams(vmem_limit_bytes=SMALL),
        cost_estimate=cost(10**5, 2**20), name="corners",
    )


def request_call(n_track, n_tiles, cells, width, cap):
    slot_rows = n_track * cap // LANES

    def kernel(foot, index, profile, requests, slots, target):
        fp = foot[...]
        owner = lax.shift_right_logical(fp, int(math.log2(cells)))
        cell = fp & (cells - 1)
        marks = [(owner == o).astype(F32) for o in range(n_track)]
        stacked = jnp.concatenate(marks, axis=0).astype(BF16)
        row = lax.broadcasted_iota(jnp.int32, (LANES, LANES), 0)
        col = lax.broadcasted_iota(jnp.int32, (LANES, LANES), 1)
        within = mm(stacked, (row < col).astype(F32).astype(BF16))
        totals = mm(stacked, jnp.ones((LANES, LANES), BF16)).astype(BF16)
        t_row = lax.broadcasted_iota(jnp.int32, (n_tiles, n_tiles), 0)
        t_col = lax.broadcasted_iota(jnp.int32, (n_tiles, n_tiles), 1)
        lower = (t_col < t_row).astype(F32).astype(BF16)
        rank = jnp.zeros((n_tiles, LANES), F32)
        for o in range(n_track):
            part = slice(o * n_tiles, (o + 1) * n_tiles)
            rank = rank + marks[o] * (within[part] + mm(lower, totals[part]))
        slot = owner * cap + rank.astype(jnp.int32)
        slots[...] = slot
        at_row = lax.shift_right_logical(slot, int(math.log2(LANES)))
        at_lane = slot & (LANES - 1)
        high = lax.shift_right_logical(cell, int(math.log2(width))).astype(F32)
        low = (cell & (width - 1)).astype(F32)
        rows = lax.broadcasted_iota(jnp.int32, (slot_rows, LANES), 0)
        found = jnp.zeros((2 * slot_rows, LANES), F32)
        row_b = row.astype(F32).astype(BF16)
        lane_b = at_lane.astype(F32).astype(BF16)
        for k in range(0, n_tiles, 2):
            values = []
            lanes = []
            for i in (k, k + 1):
                here = rows == at_row[i : i + 1]
                parts = [jnp.where(here, v[i : i + 1], 0.0) for v in (high, low)]
                values.append(jnp.concatenate(parts, axis=0).astype(BF16))
                lanes.append(jnp.where(row_b == lane_b[i : i + 1], jnp.array(1, BF16), jnp.array(0, BF16)))
            found = found + mm_nt(jnp.concatenate(values, axis=1), jnp.concatenate(lanes, axis=1))
        requests[...] = found[:slot_rows] * float(width) + found[slot_rows:]
        spread = jnp.broadcast_to(profile[...], (n_tiles, profile.shape[1]))
        temp = jnp.take_along_axis(spread, index[...], axis=1)
        target[...] = 0.05 + jnp.maximum(1.0 - temp, 0.0)

    tiles = (n_tiles, LANES)
    return pl.pallas_call(
        kernel,
        out_shape=(
            jax.ShapeDtypeStruct((slot_rows, LANES), F32),
            jax.ShapeDtypeStruct(tiles, jnp.int32),
            jax.ShapeDtypeStruct(tiles, F32),
        ),
        in_specs=[VM] * 3,
        out_specs=(VM,) * 3,
        compiler_params=pltpu.CompilerParams(vmem_limit_bytes=SMALL),
        cost_estimate=cost(10**8, 2**20),
        name="requests",
    )


def look_up(table, lane, row, rows, width):
    n = lane.shape[1]
    lanes = lax.broadcasted_iota(jnp.int32, (width, n), 0).astype(F32).astype(BF16)
    here = jnp.where(lanes == lane.astype(F32).astype(BF16), jnp.array(1, BF16), jnp.array(0, BF16))
    got = mm(table, jnp.concatenate([here, here], axis=0))
    mine = lax.broadcasted_iota(jnp.int32, (rows, n), 0) == row
    return [
        jnp.sum(jnp.where(mine, got[c * rows : (c + 1) * rows], 0.0), axis=0, keepdims=True) for c in range(3)
    ]


def look_up_all(table, lane, row, rows, width, store):
    for j in range(0, lane.shape[0], 2):
        pair = [jnp.concatenate([v[j : j + 1], v[j + 1 : j + 2]], axis=1) for v in (lane, row)]
        values = look_up(table, pair[0], pair[1], rows, width)
        for i in range(2):
            store(j + i, [v[:, i * LANES : (i + 1) * LANES] for v in values])


def llb(m, field, target):
    sq = m[0] * m[0] + m[1] * m[1] + m[2] * m[2]
    pull = 0.5 * (1.0 - sq / target)
    h = [field[c] + pull * m[c] for c in range(3)]

    def cross(a, b):
        return [a[(c + 1) % 3] * b[(c + 2) % 3] - a[(c + 2) % 3] * b[(c + 1) % 3] for c in range(3)]

    turn = cross(m, h)
    damp = cross(m, turn)
    along = m[0] * h[0] + m[1] * h[1] + m[2] * h[2]
    return [m[c] + 0.1 * (0.3 * along * m[c] - turn[c] - 0.5 * damp[c]) for c in range(3)]


def fold(by_hi, by_lo):
    return (by_hi[8:16] + by_lo[0:8]) + by_hi[0:8]


def tile_major(m_ref, tiles_ref, n_tiles):
    tiles_ref[...] = jnp.zeros_like(tiles_ref)
    flat = tiles_ref.reshape((n_tiles + 2) * 8, LANES)
    for c in range(3):
        flat[pl.ds(8 + c, n_tiles, stride=8), :] = m_ref[pl.ds(c * n_tiles, n_tiles), :]


def exchange(tiles_ref, own, nxt, k):
    here = jnp.concatenate([both(tiles_ref[k + 1]), both(tiles_ref[k])], axis=1)
    high = both(tiles_ref[k + 2])
    own_hi, own_lo = split(own)
    nxt_hi, nxt_lo = split(nxt)
    pairs = [jnp.concatenate(v, axis=1) for v in ((own_hi, nxt_hi), (own_lo, nxt_lo))]
    before = mm_nt(here, jnp.concatenate(pairs, axis=0))
    field = fold(before[:, :LANES], before[:, LANES:])
    only_hi = jnp.where(lax.broadcasted_iota(jnp.int32, high.shape, 0) < 8, high.astype(F32), 0.0).astype(BF16)
    after = mm(jnp.concatenate([high, only_hi], axis=1), jnp.concatenate([nxt_hi, nxt_lo], axis=0))
    return field + (after[0:8] + after[8:16])


def first_call(n_tiles, ny, start, count):
    step = 4
    chunks = count // step

    def kernel(own_hbm, nxt_hbm, m_ref, from_a, from_b, ex, own, nxt, tiles, sem):
        def copies(c):
            part = pl.ds(c * step, step)
            return [
                pltpu.make_async_copy(own_hbm.at[pl.ds(start + c * step, step)], own.at[part], sem.at[0, c]),
                pltpu.make_async_copy(nxt_hbm.at[pl.ds(start + c * step, step)], nxt.at[part], sem.at[1, c]),
            ]

        for c in range(chunks):
            for copy in copies(c):
                copy.start()
        tile_major(m_ref, tiles, n_tiles)
        flags = place()
        odd = flags[4] > 0
        by_a = from_a[pl.ds(3 * ny, 8), :]
        by_b = from_b[pl.ds(3 * ny, 8), :]
        tiles[0] = jnp.where(flags[0] > 0, jnp.where(odd, by_a, by_b), 0.0)
        tiles[n_tiles + 1] = jnp.where(flags[1] > 0, jnp.where(odd, by_b, by_a), 0.0)
        for c in range(chunks):
            for copy in copies(c):
                copy.wait()
            for k in range(c * step, (c + 1) * step):
                field = exchange(tiles, own[k], nxt[k], start + k)
                for n in range(3):
                    ex[pl.ds(n * count + k, 1), :] = field[n : n + 1]

    return pl.pallas_call(
        kernel,
        out_shape=jax.ShapeDtypeStruct((3 * count, LANES), F32),
        in_specs=[HBM, HBM, VM, VM, VM],
        out_specs=VM,
        scratch_shapes=[
            pltpu.VMEM((count, LANES, LANES), F32),
            pltpu.VMEM((count, LANES, LANES), F32),
            pltpu.VMEM((n_tiles + 2, 8, LANES), F32),
            pltpu.SemaphoreType.DMA((2, chunks)),
        ],
        compiler_params=pltpu.CompilerParams(vmem_limit_bytes=LARGE),
        cost_estimate=cost(1, 1),
        name="couple_first",
    )


def section_call(n_tiles, n_track, cap):
    per = cap // LANES
    slot_rows = n_track * per

    def kernel(answers, slots, m_ref, ex_a, ex_b, target, applied, m_out, edge_a, edge_b, parts):
        for c in range(3):
            rows = jnp.concatenate([answers[o, pl.ds(c * per, per), :] for o in range(n_track)], axis=0)
            hi, lo = split(rows)
            parts[pl.ds(c * slot_rows, slot_rows), pl.ds(0, LANES)] = hi
            parts[pl.ds(c * slot_rows, slot_rows), pl.ds(LANES, LANES)] = lo
        table = parts[...]
        slot = slots[...]
        at_row = lax.shift_right_logical(slot, int(math.log2(LANES)))
        at_lane = slot & (LANES - 1)

        def store(k, values):
            for c in range(3):
                applied[pl.ds(c * n_tiles + k, 1), :] = values[c]

        look_up_all(table, at_lane, at_row, slot_rows, LANES, store)
        part = [pl.ds(c * n_tiles, n_tiles) for c in range(3)]
        m = [m_ref[part[c], :] for c in range(3)]
        half = n_tiles // 2
        ex = [
            jnp.concatenate([ref[pl.ds(c * half, half), :] for ref in (ex_a, ex_b)], axis=0) for c in range(3)
        ]
        m = llb(m, [applied[part[c], :] + ex[c] for c in range(3)], target[...])
        odd = place()[4] > 0
        edge_a[...] = jnp.zeros((8, LANES), F32)
        edge_b[...] = jnp.zeros((8, LANES), F32)
        for c in range(3):
            m_out[part[c], :] = m[c]
            edge_a[pl.ds(c, 1), :] = jnp.where(odd, m[c][0:1], m[c][n_tiles - 1 :])
            edge_b[pl.ds(c, 1), :] = jnp.where(odd, m[c][n_tiles - 1 :], m[c][0:1])

    grains = jax.ShapeDtypeStruct((3 * n_tiles, LANES), F32)
    edge = jax.ShapeDtypeStruct((8, LANES), F32)
    return pl.pallas_call(
        kernel,
        out_shape=(grains, grains, edge, edge),
        in_specs=[VM] * 6,
        out_specs=(VM,) * 4,
        scratch_shapes=[pltpu.VMEM((3 * slot_rows, 2 * LANES), BF16)],
        compiler_params=pltpu.CompilerParams(vmem_limit_bytes=SMALL),
        cost_estimate=cost(10**9, 2**20),
        name="section_first",
    )


def second_call(n_tiles):
    def kernel(own, nxt, m_ref, ex, tiles):
        tile_major(m_ref, tiles, n_tiles)
        for k in range(n_tiles):
            field = exchange(tiles, own[k], nxt[k], k)
            for n in range(3):
                ex[pl.ds(n * n_tiles + k, 1), :] = field[n : n + 1]

    return pl.pallas_call(
        kernel,
        out_shape=jax.ShapeDtypeStruct((3 * n_tiles, LANES), F32),
        in_specs=[VM] * 3,
        out_specs=VM,
        scratch_shapes=[pltpu.VMEM((n_tiles + 2, 8, LANES), F32)],
        compiler_params=pltpu.CompilerParams(vmem_limit_bytes=SMALL),
        cost_estimate=cost(10**9, 4 * 2**20),
        name="couple_second",
    )


def last_call(n_tiles):
    def kernel(m_ref, ex, applied, target, from_a, from_b, nxt, out):
        flags = place()
        odd = flags[4] > 0
        below = jnp.where(odd, from_a[...], from_b[...])
        above = jnp.where(odd, from_b[...], from_a[...])
        low = both(jnp.where(flags[0] > 0, below, 0.0))
        high = both(jnp.where(flags[1] > 0, above, 0.0))
        hi, lo = split(nxt[0])
        first = fold(mm_nt(low, hi), mm_nt(low, lo))
        hi, lo = split(nxt[n_tiles - 1])
        last = fold(mm(high, hi), mm(high, lo))
        at = lax.broadcasted_iota(jnp.int32, (n_tiles, LANES), 0)
        field = []
        m = []
        for c in range(3):
            part = pl.ds(c * n_tiles, n_tiles)
            extra = jnp.where(at == 0, first[c : c + 1], 0.0) + jnp.where(at == n_tiles - 1, last[c : c + 1], 0.0)
            field.append(applied[part, :] + (ex[part, :] + extra))
            m.append(m_ref[part, :])
        m = llb(m, field, target[...])
        for c in range(3):
            out[pl.ds(c * n_tiles, n_tiles), :] = m[c]

    return pl.pallas_call(
        kernel,
        out_shape=jax.ShapeDtypeStruct((3 * n_tiles, LANES), F32),
        in_specs=[VM] * 7,
        out_specs=VM,
        compiler_params=pltpu.CompilerParams(vmem_limit_bytes=SMALL),
        cost_estimate=cost(10**7, 2**20),
        name="section_last",
    )


def shifted(v, axis, by):
    n = lax.axis_size(axis)
    return lax.ppermute(v, axis, [(i, (i + by) % n) for i in range(n)])


def traded(to_a, to_b, axis):
    n = lax.axis_size(axis)
    first = [(i, i ^ 1) for i in range(n)]
    second = [(i, (i + 1) % n if i % 2 else (i - 1) % n) for i in range(n)]
    return lax.ppermute(to_a, axis, first), lax.ppermute(to_b, axis, second)


def cells_call(rows):
    def kernel(asked, ex, cells):
        cells[...] = asked[...].astype(jnp.int32)

    return pl.pallas_call(
        kernel, out_shape=jax.ShapeDtypeStruct((rows, LANES), jnp.int32), in_specs=[VM, ANY], out_specs=VM,
        compiler_params=pltpu.CompilerParams(vmem_limit_bytes=SMALL),
        cost_estimate=cost(10**9, 4 * 2**20), name="cells",
    )


def per_device(
    potential, source, depth_kernel, magnet, footprint, temp_index, temp_profile, self_tiles, next_tiles
):
    nx, ny, nz = potential.shape
    n_track = lax.axis_size("track")
    n_tiles = self_tiles.shape[1]
    grains = footprint.shape[1]
    cap = 2 * grains // n_track
    state = magnet.reshape(3 * n_tiles, LANES)

    head_a, head_b, track_lo, track_hi = pack_call(nx, ny, nz)(potential, source)
    head_a, head_b = ends_call(ny, n_tiles)(state, head_a, head_b)
    from_a, from_b = traded(head_a, head_b, "head")
    requests, slots, target = request_call(n_track, n_tiles, nx * ny, ny, cap)(
        footprint.reshape(n_tiles, LANES), temp_index.reshape(n_tiles, LANES), temp_profile[None, :]
    )
    track_lo, track_hi = corner_call(nx, ny, nz)(track_lo, track_hi, from_a, from_b)
    left = shifted(track_hi, "track", 1)
    right = shifted(track_lo, "track", -1)
    asked = lax.all_to_all(requests.reshape(n_track, cap // LANES, LANES), "track", 0, 0)

    kern = jnp.pad(depth_kernel, ((0, 5), (0, 0)))
    half = n_tiles // 2
    couplings = (self_tiles[0], next_tiles[0], state, from_a, from_b)
    q_inner, token = inner_call(nx, ny, nz)(potential, source, from_a, from_b)
    asked = cells_call(n_track * cap // LANES)(asked.reshape(n_track * cap // LANES, LANES), token)
    relaxed, reply = relax_call(nx, ny, nz, n_track, cap)(
        potential, source, from_a, from_b, left, right, track_lo, track_hi, kern,
        asked, q_inner,
    )
    answers = lax.all_to_all(reply, "track", 0, 0)
    ex_a = first_call(n_tiles, ny, 0, half)(*couplings)
    ex_b = first_call(n_tiles, ny, half, n_tiles - half)(*couplings)
    applied, state, edge_a, edge_b = section_call(n_tiles, n_track, cap)(
        answers, slots, state, ex_a, ex_b, target
    )
    tile_a, tile_b = traded(edge_a, edge_b, "head")
    ex = second_call(n_tiles)(self_tiles[0], next_tiles[0], state)
    state = last_call(n_tiles)(
        state, ex, applied, target, tile_a, tile_b, next_tiles[0]
    )
    return relaxed, state.reshape(3, 1, grains)


def solution(mesh):
    in_specs = (
        P("head", "track", None),
        P("head", "track", None),
        P(),
        P(None, "track", "head"),
        P("track", "head"),
        P("track", "head"),
        P(),
        P("track", "head", None, None),
        P("track", "head", None, None),
    )
    out_specs = (P("head", "track", None), P(None, "track", "head"))
    return jax.shard_map(
        per_device, mesh=mesh, in_specs=in_specs, out_specs=out_specs, check_vma=False
    )
```

```python
import math

import jax
import jax.numpy as jnp
from jax import lax
from jax.experimental import pallas as pl
from jax.experimental.pallas import tpu as pltpu
from jax.sharding import PartitionSpec as P

F32 = jnp.float32
BF16 = jnp.bfloat16
STRIP = 16
UNIT = 8
TOP = 8
AHEAD = 4
LANES = 128
SMALL = 16 * 2**20
LARGE = 52 * 2**20
NT = (((1,), (1,)), ((), ()))
VM = pl.BlockSpec(memory_space=pltpu.VMEM)
SM = pl.BlockSpec(memory_space=pltpu.SMEM)
HBM = pl.BlockSpec(memory_space=pltpu.HBM)
ANY = pl.BlockSpec(memory_space=pl.ANY)


def mm(a, b):
    return jnp.dot(a, b, preferred_element_type=F32)


def mm_nt(a, b):
    return lax.dot_general(a, b, NT, preferred_element_type=F32)


def split(v):
    hi = v.astype(BF16)
    return hi, (v - hi.astype(F32)).astype(BF16)


def place():
    h = lax.axis_index("head")
    t = lax.axis_index("track")
    flags = (h > 0, h < lax.axis_size("head") - 1, t > 0, t < lax.axis_size("track") - 1, h % 2 == 1)
    return [flag.astype(jnp.int32) for flag in flags]


def cost(flops, moved):
    return pl.CostEstimate(flops=flops, bytes_accessed=moved, transcendentals=0)


def rcp(v):
    return pl.reciprocal(v, approx=True)


def flux(d):
    mu = 1.0 + rcp(0.25 + d * d)
    return mu * d, mu


def z_flux(c):
    lane = lax.broadcasted_iota(jnp.int32, c.shape, c.ndim - 1)
    n = c.shape[-1]
    zl = jnp.where(lane == 0, 0.0, pltpu.roll(c, 1, c.ndim - 1))
    zr = jnp.where(lane == n - 1, 0.0, pltpu.roll(c, n - 1, c.ndim - 1))
    fl, ml = flux(zl - c)
    fr, mr = flux(zr - c)
    return fl + fr, ml + mr


def both(v):
    hi = v.astype(jnp.bfloat16).astype(jnp.float32)
    return jnp.concatenate([hi, v - hi], axis=0).astype(jnp.bfloat16)


def finish(c, numer, denom):
    return c + 0.8 * (numer * rcp(denom))


def sweep(a, x, planes, strips, fx, mx, fy, my, src, store):
    for u in range(planes):
        for k in strips:
            if k - 1 not in strips:
                row = TOP + k * STRIP - 8
                f, mu = flux(a[x + u, pl.ds(row + 1, 8), :] - a[x + u, pl.ds(row, 8), :])
                fy[u, pl.ds(row, 8), :] = f
                my[u, pl.ds(row, 8), :] = mu
    for k in strips:
        here = pl.ds(TOP + k * STRIP, STRIP)
        before = pl.ds(TOP + k * STRIP - 1, STRIP)
        after = pl.ds(TOP + k * STRIP + 1, STRIP)
        flat = pl.ds(k * STRIP, STRIP)
        c = a[x, here, :]
        fp = fx[flat, :]
        mp = mx[flat, :]
        for u in range(planes):
            up = a[x + u + 1, here, :]
            f, mu = flux(up - c)
            numer = f - fp
            denom = mu + mp
            fp, mp = f, mu
            f, mu = flux(a[x + u, after, :] - c)
            fy[u, here, :] = f
            my[u, here, :] = mu
            numer = numer + (f - fy[u, before, :])
            denom = denom + (mu + my[u, before, :])
            f, mu = z_flux(c)
            numer = numer + (f + src[u, flat, :])
            denom = denom + (mu + 1.0)
            store(u, k, finish(c, numer, denom))
            c = up
        fx[flat, :] = fp
        mx[flat, :] = mp


def first_x(a, x, strips, fx, mx):
    for k in strips:
        here = pl.ds(TOP + k * STRIP, STRIP)
        flat = pl.ds(k * STRIP, STRIP)
        f, mu = flux(a[x + 1, here, :] - a[x, here, :])
        fx[flat, :] = f
        mx[flat, :] = mu


def keep(flag, v):
    return jnp.where(flag, v, 0.0)


def head_planes(from_a, from_b, ny, flags, side):
    swap = flags[4] > 0 if side == 0 else flags[4] == 0
    planes = [jnp.where(swap, from_a[pl.ds(n * ny, ny), :], from_b[pl.ds(n * ny, ny), :]) for n in range(3)]
    return [keep(flags[side] > 0, planes[0]), keep(flags[side] > 0, planes[1]), planes[2]]


def inner_call(nx, ny, nz):
    n_strip = ny // STRIP
    strips = range(1, n_strip - 1)
    inner = ny - 2 * STRIP
    n_unit = nx // UNIT

    def kernel(p_hbm, s_hbm, from_a, from_b, q_hbm, token, pe, q, sb, fx, mx, fy, my, psem, ssem, qsem):
        flags = place()

        def pcopy(c):
            return pltpu.make_async_copy(
                p_hbm.at[pl.ds(c * UNIT, UNIT), pl.ds(8, ny - 16)],
                pe.at[pl.ds(2 + c * UNIT, UNIT), pl.ds(TOP + 8, ny - 16)], psem.at[c])

        def scopy(c):
            return pltpu.make_async_copy(
                s_hbm.at[pl.ds(c * UNIT, UNIT), pl.ds(STRIP, inner)],
                sb.at[pl.ds(1 + c * UNIT, UNIT), pl.ds(STRIP, inner)], ssem.at[c])

        def qcopy(c):
            return pltpu.make_async_copy(q.at[pl.ds(2 + c * UNIT, UNIT)], q_hbm.at[pl.ds(2 + c * UNIT, UNIT)], qsem.at[c])

        first = pltpu.make_async_copy(q.at[pl.ds(0, 2)], q_hbm.at[pl.ds(0, 2)], qsem.at[n_unit])

        def fetch(c):
            pcopy(c).start()
            scopy(c).start()

        for c in range(n_unit):
            fetch(c)
        token[...] = jnp.zeros_like(token)
        for side, (at, to) in enumerate((((0, 1), 0), ((nx + 2, nx + 3), nx + 1))):
            planes = head_planes(from_a, from_b, ny, flags, side)
            pe[at[0], pl.ds(TOP, ny), :] = planes[0]
            pe[at[1], pl.ds(TOP, ny), :] = planes[1]
            sb[to, :, :] = planes[2]

        def part(x, planes, at=None, flag=None):
            def store(u, k, v):
                q[x + u + 1, pl.ds((k - 1) * STRIP, STRIP), :] = keep(flag, v) if u == at else v

            sweep(pe, x + 2, planes, strips, fx, mx, fy, my, sb.at[pl.ds(x + 1, planes)], store)

        for c in range(2):
            pcopy(c).wait()
            scopy(c).wait()
        first_x(pe, 0, strips, fx, mx)
        part(-1, UNIT + 2, 0, flags[0] > 0)
        first.start()
        qcopy(0).start()

        def body(b, _):
            pcopy(b + 1).wait()
            scopy(b + 1).wait()
            part(b * UNIT + 1, UNIT)
            qcopy(b).start()
            return 0

        lax.fori_loop(1, n_unit - 1, body, 0)
        part((n_unit - 1) * UNIT + 1, UNIT, UNIT - 1, flags[1] > 0)
        qcopy(n_unit - 1).start()
        first.wait()
        for c in range(n_unit):
            qcopy(c).wait()

    plane = pltpu.VMEM((ny, nz), F32)
    edge = pltpu.VMEM((UNIT + 2, ny + 2 * TOP, nz), F32)
    return pl.pallas_call(
        kernel,
        out_shape=(jax.ShapeDtypeStruct((nx + 2, inner, nz), F32), jax.ShapeDtypeStruct((8, LANES), F32)),
        in_specs=[HBM, HBM, VM, VM],
        out_specs=(HBM, VM),
        scratch_shapes=[
            pltpu.VMEM((nx + 4, ny + 2 * TOP, nz), F32), pltpu.VMEM((nx + 2, inner, nz), F32),
            pltpu.VMEM((nx + 2, ny, nz), F32), plane, plane, edge, edge,
            pltpu.SemaphoreType.DMA((n_unit,)), pltpu.SemaphoreType.DMA((n_unit,)),
            pltpu.SemaphoreType.DMA((n_unit + 1,)),
        ],
        compiler_params=pltpu.CompilerParams(vmem_limit_bytes=LARGE),
        cost_estimate=cost(1, 1),
        name="sweep_inner",
    )


def relax_call(nx, ny, nz, n_track, cap):
    chunk = UNIT
    per = cap // LANES
    rows = ny + 2 * TOP

    def kernel(p_hbm, s_hbm, from_a, from_b, tlo, thi, own_lo, own_hi, kern, requests, q_hbm, o_hbm, reply_out,
               reply, rsem, table, parts, pe, q, sb, ob, fx1, mx1, fx2, mx2, fy1, my1, fy2, my2, psem, ssem, osem, qsem):
        n_chunk = nx // chunk

        reach = STRIP + 8
        inner = ny - 2 * STRIP
        ends = (0, ny // STRIP - 1)
        whole = range(ny // STRIP)

        def pcopies(c):
            return [
                pltpu.make_async_copy(
                    p_hbm.at[pl.ds(c * chunk, chunk), pl.ds(row, reach)],
                    pe.at[pl.ds(2 + c * chunk, chunk), pl.ds(TOP + row, reach)], psem.at[n, c])
                for n, row in enumerate((0, ny - reach))
            ]

        def qcopy(c):
            return pltpu.make_async_copy(q_hbm.at[pl.ds(2 + c * chunk, chunk)],
                                         q.at[pl.ds(2 + c * chunk, chunk), pl.ds(TOP + STRIP, inner)], qsem.at[c])

        qfirst = pltpu.make_async_copy(q_hbm.at[pl.ds(0, 2)], q.at[pl.ds(0, 2), pl.ds(TOP + STRIP, inner)],
                                       qsem.at[nx // chunk])

        def scopy(c):
            return pltpu.make_async_copy(s_hbm.at[pl.ds(c * chunk, chunk)],
                                         sb.at[pl.ds(1 + c * chunk, chunk)], ssem.at[c])

        def ocopy(c):
            return pltpu.make_async_copy(ob.at[pl.ds(c * chunk + UNIT, chunk)],
                                         o_hbm.at[pl.ds(c * chunk, chunk)], osem.at[c])

        def fetch(c):
            for copy in pcopies(c):
                copy.start()
            scopy(c).start()
            qcopy(c).start()

        def arrive(c):
            for copy in pcopies(c):
                copy.wait()
            scopy(c).wait()
            qcopy(c).wait()

        qfirst.start()
        for c in range(AHEAD):
            fetch(c)

        flags = place()
        has = [flags[n] > 0 for n in range(4)]

        main = pl.ds(TOP, ny)
        odd = flags[4] > 0
        for side, (at, to) in enumerate((((0, 1), 0), ((nx + 2, nx + 3), nx + 1))):
            swap = odd if side == 0 else jnp.logical_not(odd)
            planes = [
                jnp.where(swap, from_a[pl.ds(n * ny, ny), :], from_b[pl.ds(n * ny, ny), :]) for n in range(3)
            ]
            pe[at[0], main, :] = keep(has[side], planes[0])
            pe[at[1], main, :] = keep(has[side], planes[1])
            sb[to, :, :] = planes[2]
        pe2 = pe.reshape((nx + 4) * rows, nz)
        q2 = q.reshape((nx + 2) * rows, nz)
        for side, (ref, own, row) in enumerate(((tlo, own_lo, TOP - 1), (thi, own_hi, TOP + ny))):
            flag = has[2 + side]
            c = keep(flag, ref[pl.ds(0, nx), :])
            far = keep(flag, ref[pl.ds(nx, nx), :])
            src = ref[pl.ds(2 * nx, nx), :]
            near = own[pl.ds(0, nx), :]
            corners = keep(flag, ref[pl.ds(3 * nx, 8), :])
            below = keep(has[0], corners[0:1])
            above = keep(has[1], corners[1:2])
            ix = lax.broadcasted_iota(jnp.int32, c.shape, 0)
            xl = jnp.where(ix == 0, below, pltpu.roll(c, 1, 0))
            xr = jnp.where(ix == nx - 1, above, pltpu.roll(c, nx - 1, 0))
            numer, denom = z_flux(c)
            numer = numer + src
            denom = denom + 1.0
            for other in (far, near, xl, xr):
                f, mu = flux(other - c)
                numer = numer + f
                denom = denom + mu
            pe2[pl.ds(2 * rows + row, nx, stride=rows), :] = c
            pe2[pl.ds(rows + row, 1), :] = below
            pe2[pl.ds((nx + 2) * rows + row, 1), :] = above
            q2[pl.ds(rows + row, nx, stride=rows), :] = keep(flag, finish(c, numer, denom))

        def sweep1(x, planes, flag=None):
            def store(u, k, v):
                q[x + u + 1, pl.ds(TOP + k * STRIP, STRIP), :] = v if flag is None else keep(flag, v)

            sweep(pe, x + 2, planes, ends, fx1, mx1, fy1, my1, sb.at[pl.ds(x + 1, planes)], store)

        kk = both(kern[...])

        def sweep2(x, planes):
            def store(u, k, v):
                ob[x + u + UNIT, pl.ds(k * STRIP, STRIP), :] = v

            sweep(q, x + 1, planes, whole, fx2, mx2, fy2, my2, sb.at[pl.ds(x + 1, planes)], store)

        def surface(x, planes):
            nt = (((1,), (1,)), ((), ()))
            for u in range(planes):
                v = ob[x + u + UNIT]
                hi = v.astype(jnp.bfloat16)
                lo = (v - hi.astype(jnp.float32)).astype(jnp.bfloat16)
                a = lax.dot_general(kk, hi, nt, preferred_element_type=jnp.float32)
                b = lax.dot_general(kk, lo, nt, preferred_element_type=jnp.float32)
                table[x + u + UNIT] = (a[8:16] + b[0:8]) + a[0:8]

        n_unit = nx // UNIT
        qfirst.wait()
        arrive(0)
        first_x(pe, 0, ends, fx1, mx1)
        sweep1(-1, 1, has[0])
        sweep1(0, 1)
        first_x(q, 0, whole, fx2, mx2)
        arrive(1)
        sweep1(1, UNIT)

        def body(b, _):
            @pl.when(b + AHEAD <= n_unit)
            def _():
                fetch(b + AHEAD - 1)

            @pl.when(b < n_unit - 1)
            def _():
                arrive(b + 1)

            surface((b - 2) * UNIT, UNIT)
            sweep2((b - 1) * UNIT, UNIT)
            sweep1(b * UNIT + 1, UNIT)
            ocopy(b - 1).start()
            return 0

        lax.fori_loop(1, n_unit, body, 0)

        @pl.when(jnp.logical_not(has[1]))
        def _():
            q[nx + 1] = jnp.zeros_like(q[nx + 1])

        surface(nx - 2 * UNIT, UNIT)
        sweep2(nx - UNIT, UNIT)
        ocopy(n_unit - 1).start()
        surface(nx - UNIT, UNIT)

        flat = table.reshape((nx + UNIT) * 8, ny)
        for c in range(3):
            hi, lo = split(flat[pl.ds(UNIT * 8 + c, nx, stride=8), :])
            parts[pl.ds(c * nx, nx), pl.ds(0, ny)] = hi
            parts[pl.ds(c * nx, nx), pl.ds(ny, ny)] = lo
        asked = requests[...]

        share = n_track // 4

        def rcopy(n):
            part = pl.ds(n * share, share)
            return pltpu.make_async_copy(reply.at[part], reply_out.at[part], rsem.at[n])

        def answer(j, values):
            for c in range(3):
                reply[j // per, pl.ds(c * per + j % per, 1), :] = values[c]
            if (j + 1) % (share * per) == 0:
                rcopy(j // (share * per)).start()

        look_up_all(parts[...], asked & (ny - 1), lax.shift_right_logical(asked, int(math.log2(ny))), nx, ny, answer)
        for n in range(4):
            rcopy(n).wait()
        for c in range(n_chunk):
            ocopy(c).wait()

    f32 = jnp.float32
    vm = pl.BlockSpec(memory_space=pltpu.VMEM)
    hbm = pl.BlockSpec(memory_space=pltpu.HBM)
    plane = pltpu.VMEM((ny, nz), f32)
    edge = pltpu.VMEM((UNIT, rows, nz), f32)
    return pl.pallas_call(
        kernel,
        out_shape=(
            jax.ShapeDtypeStruct((nx, ny, nz), f32),
            jax.ShapeDtypeStruct((n_track, 3 * per, 128), f32),
        ),
        in_specs=[hbm, hbm] + [vm] * 8 + [hbm],
        out_specs=(hbm, hbm),
        scratch_shapes=[
            pltpu.VMEM((n_track, 3 * per, 128), f32), pltpu.SemaphoreType.DMA((4,)),
            pltpu.VMEM((nx + UNIT, 8, ny), f32), pltpu.VMEM((3 * nx, 2 * ny), jnp.bfloat16),
            pltpu.VMEM((nx + 4, rows, nz), f32), pltpu.VMEM((nx + 2, rows, nz), f32),
            pltpu.VMEM((nx + 2, ny, nz), f32), pltpu.VMEM((nx + UNIT, ny, nz), f32),
            plane, plane, plane, plane, edge, edge, edge, edge,
            pltpu.SemaphoreType.DMA((2, nx // chunk)), pltpu.SemaphoreType.DMA((nx // chunk,)),
            pltpu.SemaphoreType.DMA((nx // chunk,)), pltpu.SemaphoreType.DMA((nx // chunk + 1,)),
        ],
        compiler_params=pltpu.CompilerParams(vmem_limit_bytes=LARGE),
        cost_estimate=pl.CostEstimate(flops=nx * ny * nz * 100, bytes_accessed=nx * ny * nz * 12, transcendentals=nx * ny * nz * 10),
        name="relax",
    )


def pack_call(nx, ny, nz):
    def kernel(p_hbm, s_hbm, head_a, head_b, track_lo, track_hi, p_lo, p_hi, s_lo, s_hi, sem):
        odd = place()[4]
        copies = []
        for i, (out, low) in enumerate(((head_a, odd), (head_b, 1 - odd))):
            at_p = jnp.where(low > 0, 0, nx - 2)
            at_s = jnp.where(low > 0, 0, nx - 1)
            copies += [
                pltpu.make_async_copy(p_hbm.at[at_p], out.at[pl.ds(0, ny)], sem.at[3 * i]),
                pltpu.make_async_copy(p_hbm.at[at_p + 1], out.at[pl.ds(ny, ny)], sem.at[3 * i + 1]),
                pltpu.make_async_copy(s_hbm.at[at_s], out.at[pl.ds(2 * ny, ny)], sem.at[3 * i + 2]),
            ]
        rows = [(p_hbm, 0, p_lo), (p_hbm, ny - 8, p_hi), (s_hbm, 0, s_lo), (s_hbm, ny - 8, s_hi)]
        copies += [
            pltpu.make_async_copy(src.at[:, pl.ds(at, 8)], dst, sem.at[6 + i])
            for i, (src, at, dst) in enumerate(rows)
        ]
        for copy in copies:
            copy.start()
        head_a[pl.ds(3 * ny, 8), :] = jnp.zeros((8, nz), F32)
        head_b[pl.ds(3 * ny, 8), :] = jnp.zeros((8, nz), F32)
        for copy in copies[6:]:
            copy.wait()
        for out, p_ref, s_ref, order in ((track_lo, p_lo, s_lo, (0, 1)), (track_hi, p_hi, s_hi, (7, 6))):
            p2 = p_ref.reshape(nx * 8, nz)
            s2 = s_ref.reshape(nx * 8, nz)
            out[pl.ds(0, nx), :] = p2[pl.ds(order[0], nx, stride=8), :]
            out[pl.ds(nx, nx), :] = p2[pl.ds(order[1], nx, stride=8), :]
            out[pl.ds(2 * nx, nx), :] = s2[pl.ds(order[0], nx, stride=8), :]
            out[pl.ds(3 * nx, 8), :] = jnp.zeros((8, nz), F32)
        for copy in copies[:6]:
            copy.wait()

    head = jax.ShapeDtypeStruct((3 * ny + 8, nz), F32)
    track = jax.ShapeDtypeStruct((3 * nx + 8, nz), F32)
    eight = pltpu.VMEM((nx, 8, nz), F32)
    return pl.pallas_call(
        kernel,
        out_shape=(head, head, track, track),
        in_specs=[HBM, HBM],
        out_specs=(VM,) * 4,
        scratch_shapes=[eight] * 4 + [pltpu.SemaphoreType.DMA((10,))],
        compiler_params=pltpu.CompilerParams(vmem_limit_bytes=LARGE),
        cost_estimate=cost(10**6, 4 * 2**20),
        name="pack",
    )


def ends_call(ny, n_tiles):
    def kernel(m_ref, a_in, b_in, head_a, head_b):
        flags = place()
        for out, low in ((head_a, flags[4]), (head_b, 1 - flags[4])):
            for c in range(3):
                first = m_ref[pl.ds(c * n_tiles, 1), :]
                last = m_ref[pl.ds((c + 1) * n_tiles - 1, 1), :]
                out[pl.ds(3 * ny + c, 1), :] = jnp.where(low > 0, first, last)

    head = jax.ShapeDtypeStruct((3 * ny + 8, LANES), F32)
    return pl.pallas_call(
        kernel, out_shape=(head, head), in_specs=[VM, VM, VM], out_specs=(VM, VM),
        input_output_aliases={1: 0, 2: 1},
        compiler_params=pltpu.CompilerParams(vmem_limit_bytes=SMALL),
        cost_estimate=cost(10**5, 10**5), name="ends",
    )


def corner_call(nx, ny, nz):
    def kernel(lo_in, hi_in, from_a, from_b, lo, hi):
        odd = place()[4] > 0
        for src, dst, row in ((lo_in, lo, 0), (hi_in, hi, ny - 1)):
            dst[pl.ds(0, 3 * nx), :] = src[pl.ds(0, 3 * nx), :]
            dst[pl.ds(3 * nx, 8), :] = jnp.zeros((8, nz), F32)
            below = pl.ds(ny + row, 1)
            above = pl.ds(row, 1)
            dst[pl.ds(3 * nx, 1), :] = jnp.where(odd, from_a[below, :], from_b[below, :])
            dst[pl.ds(3 * nx + 1, 1), :] = jnp.where(odd, from_b[above, :], from_a[above, :])

    track = jax.ShapeDtypeStruct((3 * nx + 8, nz), F32)
    return pl.pallas_call(
        kernel, out_shape=(track, track), in_specs=[VM] * 4, out_specs=(VM, VM),
        compiler_params=pltpu.CompilerParams(vmem_limit_bytes=SMALL),
        cost_estimate=cost(10**5, 2**20), name="corners",
    )


def request_call(n_track, n_tiles, cells, width, cap):
    slot_rows = n_track * cap // LANES

    def kernel(foot, index, profile, requests, slots, target):
        fp = foot[...]
        owner = lax.shift_right_logical(fp, int(math.log2(cells)))
        cell = fp & (cells - 1)
        marks = [(owner == o).astype(F32) for o in range(n_track)]
        stacked = jnp.concatenate(marks, axis=0).astype(BF16)
        row = lax.broadcasted_iota(jnp.int32, (LANES, LANES), 0)
        col = lax.broadcasted_iota(jnp.int32, (LANES, LANES), 1)
        within = mm(stacked, (row < col).astype(F32).astype(BF16))
        totals = mm(stacked, jnp.ones((LANES, LANES), BF16)).astype(BF16)
        t_row = lax.broadcasted_iota(jnp.int32, (n_tiles, n_tiles), 0)
        t_col = lax.broadcasted_iota(jnp.int32, (n_tiles, n_tiles), 1)
        lower = (t_col < t_row).astype(F32).astype(BF16)
        rank = jnp.zeros((n_tiles, LANES), F32)
        for o in range(n_track):
            part = slice(o * n_tiles, (o + 1) * n_tiles)
            rank = rank + marks[o] * (within[part] + mm(lower, totals[part]))
        slot = owner * cap + rank.astype(jnp.int32)
        slots[...] = slot
        at_row = lax.shift_right_logical(slot, int(math.log2(LANES)))
        at_lane = slot & (LANES - 1)
        high = lax.shift_right_logical(cell, int(math.log2(width))).astype(F32)
        low = (cell & (width - 1)).astype(F32)
        rows = lax.broadcasted_iota(jnp.int32, (slot_rows, LANES), 0)
        found = jnp.zeros((2 * slot_rows, LANES), F32)
        row_b = row.astype(F32).astype(BF16)
        lane_b = at_lane.astype(F32).astype(BF16)
        for k in range(0, n_tiles, 2):
            values = []
            lanes = []
            for i in (k, k + 1):
                here = rows == at_row[i : i + 1]
                parts = [jnp.where(here, v[i : i + 1], 0.0) for v in (high, low)]
                values.append(jnp.concatenate(parts, axis=0).astype(BF16))
                lanes.append(jnp.where(row_b == lane_b[i : i + 1], jnp.array(1, BF16), jnp.array(0, BF16)))
            found = found + mm_nt(jnp.concatenate(values, axis=1), jnp.concatenate(lanes, axis=1))
        requests[...] = found[:slot_rows] * float(width) + found[slot_rows:]
        spread = jnp.broadcast_to(profile[...], (n_tiles, profile.shape[1]))
        temp = jnp.take_along_axis(spread, index[...], axis=1)
        target[...] = 0.05 + jnp.maximum(1.0 - temp, 0.0)

    tiles = (n_tiles, LANES)
    return pl.pallas_call(
        kernel,
        out_shape=(
            jax.ShapeDtypeStruct((slot_rows, LANES), F32),
            jax.ShapeDtypeStruct(tiles, jnp.int32),
            jax.ShapeDtypeStruct(tiles, F32),
        ),
        in_specs=[VM] * 3,
        out_specs=(VM,) * 3,
        compiler_params=pltpu.CompilerParams(vmem_limit_bytes=SMALL),
        cost_estimate=cost(10**8, 2**20),
        name="requests",
    )


def look_up(table, lane, row, rows, width):
    n = lane.shape[1]
    lanes = lax.broadcasted_iota(jnp.int32, (width, n), 0).astype(F32).astype(BF16)
    here = jnp.where(lanes == lane.astype(F32).astype(BF16), jnp.array(1, BF16), jnp.array(0, BF16))
    got = mm(table, jnp.concatenate([here, here], axis=0))
    mine = lax.broadcasted_iota(jnp.int32, (rows, n), 0) == row
    return [
        jnp.sum(jnp.where(mine, got[c * rows : (c + 1) * rows], 0.0), axis=0, keepdims=True) for c in range(3)
    ]


def look_up_all(table, lane, row, rows, width, store):
    for j in range(0, lane.shape[0], 2):
        pair = [jnp.concatenate([v[j : j + 1], v[j + 1 : j + 2]], axis=1) for v in (lane, row)]
        values = look_up(table, pair[0], pair[1], rows, width)
        for i in range(2):
            store(j + i, [v[:, i * LANES : (i + 1) * LANES] for v in values])


def llb(m, field, target):
    sq = m[0] * m[0] + m[1] * m[1] + m[2] * m[2]
    pull = 0.5 * (1.0 - sq / target)
    h = [field[c] + pull * m[c] for c in range(3)]

    def cross(a, b):
        return [a[(c + 1) % 3] * b[(c + 2) % 3] - a[(c + 2) % 3] * b[(c + 1) % 3] for c in range(3)]

    turn = cross(m, h)
    damp = cross(m, turn)
    along = m[0] * h[0] + m[1] * h[1] + m[2] * h[2]
    return [m[c] + 0.1 * (0.3 * along * m[c] - turn[c] - 0.5 * damp[c]) for c in range(3)]


def fold(by_hi, by_lo):
    return (by_hi[8:16] + by_lo[0:8]) + by_hi[0:8]


def tile_major(m_ref, tiles_ref, n_tiles):
    tiles_ref[...] = jnp.zeros_like(tiles_ref)
    flat = tiles_ref.reshape((n_tiles + 2) * 8, LANES)
    for c in range(3):
        flat[pl.ds(8 + c, n_tiles, stride=8), :] = m_ref[pl.ds(c * n_tiles, n_tiles), :]


def exchange(tiles_ref, own, nxt, k):
    here = jnp.concatenate([both(tiles_ref[k + 1]), both(tiles_ref[k])], axis=1)
    high = both(tiles_ref[k + 2])
    own_hi, own_lo = split(own)
    nxt_hi, nxt_lo = split(nxt)
    pairs = [jnp.concatenate(v, axis=1) for v in ((own_hi, nxt_hi), (own_lo, nxt_lo))]
    before = mm_nt(here, jnp.concatenate(pairs, axis=0))
    field = fold(before[:, :LANES], before[:, LANES:])
    only_hi = jnp.where(lax.broadcasted_iota(jnp.int32, high.shape, 0) < 8, high.astype(F32), 0.0).astype(BF16)
    after = mm(jnp.concatenate([high, only_hi], axis=1), jnp.concatenate([nxt_hi, nxt_lo], axis=0))
    return field + (after[0:8] + after[8:16])


def first_call(n_tiles, ny, start, count):
    step = 4
    chunks = count // step

    def kernel(own_hbm, nxt_hbm, m_ref, from_a, from_b, ex, own, nxt, tiles, sem):
        def copies(c):
            part = pl.ds(c * step, step)
            return [
                pltpu.make_async_copy(own_hbm.at[pl.ds(start + c * step, step)], own.at[part], sem.at[0, c]),
                pltpu.make_async_copy(nxt_hbm.at[pl.ds(start + c * step, step)], nxt.at[part], sem.at[1, c]),
            ]

        for c in range(chunks):
            for copy in copies(c):
                copy.start()
        tile_major(m_ref, tiles, n_tiles)
        flags = place()
        odd = flags[4] > 0
        by_a = from_a[pl.ds(3 * ny, 8), :]
        by_b = from_b[pl.ds(3 * ny, 8), :]
        tiles[0] = jnp.where(flags[0] > 0, jnp.where(odd, by_a, by_b), 0.0)
        tiles[n_tiles + 1] = jnp.where(flags[1] > 0, jnp.where(odd, by_b, by_a), 0.0)
        for c in range(chunks):
            for copy in copies(c):
                copy.wait()
            for k in range(c * step, (c + 1) * step):
                field = exchange(tiles, own[k], nxt[k], start + k)
                for n in range(3):
                    ex[pl.ds(n * count + k, 1), :] = field[n : n + 1]

    return pl.pallas_call(
        kernel,
        out_shape=jax.ShapeDtypeStruct((3 * count, LANES), F32),
        in_specs=[HBM, HBM, VM, VM, VM],
        out_specs=VM,
        scratch_shapes=[
            pltpu.VMEM((count, LANES, LANES), F32),
            pltpu.VMEM((count, LANES, LANES), F32),
            pltpu.VMEM((n_tiles + 2, 8, LANES), F32),
            pltpu.SemaphoreType.DMA((2, chunks)),
        ],
        compiler_params=pltpu.CompilerParams(vmem_limit_bytes=LARGE),
        cost_estimate=cost(1, 1),
        name="couple_first",
    )


def section_call(n_tiles, n_track, cap):
    per = cap // LANES
    slot_rows = n_track * per

    def kernel(answers, slots, m_ref, ex_a, ex_b, target, applied, m_out, edge_a, edge_b, parts):
        for c in range(3):
            rows = jnp.concatenate([answers[o, pl.ds(c * per, per), :] for o in range(n_track)], axis=0)
            hi, lo = split(rows)
            parts[pl.ds(c * slot_rows, slot_rows), pl.ds(0, LANES)] = hi
            parts[pl.ds(c * slot_rows, slot_rows), pl.ds(LANES, LANES)] = lo
        table = parts[...]
        slot = slots[...]
        at_row = lax.shift_right_logical(slot, int(math.log2(LANES)))
        at_lane = slot & (LANES - 1)

        def store(k, values):
            for c in range(3):
                applied[pl.ds(c * n_tiles + k, 1), :] = values[c]

        look_up_all(table, at_lane, at_row, slot_rows, LANES, store)
        part = [pl.ds(c * n_tiles, n_tiles) for c in range(3)]
        m = [m_ref[part[c], :] for c in range(3)]
        half = n_tiles // 2
        ex = [
            jnp.concatenate([ref[pl.ds(c * half, half), :] for ref in (ex_a, ex_b)], axis=0) for c in range(3)
        ]
        m = llb(m, [applied[part[c], :] + ex[c] for c in range(3)], target[...])
        odd = place()[4] > 0
        edge_a[...] = jnp.zeros((8, LANES), F32)
        edge_b[...] = jnp.zeros((8, LANES), F32)
        for c in range(3):
            m_out[part[c], :] = m[c]
            edge_a[pl.ds(c, 1), :] = jnp.where(odd, m[c][0:1], m[c][n_tiles - 1 :])
            edge_b[pl.ds(c, 1), :] = jnp.where(odd, m[c][n_tiles - 1 :], m[c][0:1])

    grains = jax.ShapeDtypeStruct((3 * n_tiles, LANES), F32)
    edge = jax.ShapeDtypeStruct((8, LANES), F32)
    return pl.pallas_call(
        kernel,
        out_shape=(grains, grains, edge, edge),
        in_specs=[VM] * 6,
        out_specs=(VM,) * 4,
        scratch_shapes=[pltpu.VMEM((3 * slot_rows, 2 * LANES), BF16)],
        compiler_params=pltpu.CompilerParams(vmem_limit_bytes=SMALL),
        cost_estimate=cost(10**9, 2**20),
        name="section_first",
    )


def second_call(n_tiles):
    def kernel(own, nxt, m_ref, ex, tiles):
        tile_major(m_ref, tiles, n_tiles)
        for k in range(n_tiles):
            field = exchange(tiles, own[k], nxt[k], k)
            for n in range(3):
                ex[pl.ds(n * n_tiles + k, 1), :] = field[n : n + 1]

    return pl.pallas_call(
        kernel,
        out_shape=jax.ShapeDtypeStruct((3 * n_tiles, LANES), F32),
        in_specs=[VM] * 3,
        out_specs=VM,
        scratch_shapes=[pltpu.VMEM((n_tiles + 2, 8, LANES), F32)],
        compiler_params=pltpu.CompilerParams(vmem_limit_bytes=SMALL),
        cost_estimate=cost(10**9, 4 * 2**20),
        name="couple_second",
    )


def last_call(n_tiles):
    def kernel(m_ref, ex, applied, target, from_a, from_b, nxt, out):
        flags = place()
        odd = flags[4] > 0
        below = jnp.where(odd, from_a[...], from_b[...])
        above = jnp.where(odd, from_b[...], from_a[...])
        low = both(jnp.where(flags[0] > 0, below, 0.0))
        high = both(jnp.where(flags[1] > 0, above, 0.0))
        hi, lo = split(nxt[0])
        first = fold(mm_nt(low, hi), mm_nt(low, lo))
        hi, lo = split(nxt[n_tiles - 1])
        last = fold(mm(high, hi), mm(high, lo))
        at = lax.broadcasted_iota(jnp.int32, (n_tiles, LANES), 0)
        field = []
        m = []
        for c in range(3):
            part = pl.ds(c * n_tiles, n_tiles)
            extra = jnp.where(at == 0, first[c : c + 1], 0.0) + jnp.where(at == n_tiles - 1, last[c : c + 1], 0.0)
            field.append(applied[part, :] + (ex[part, :] + extra))
            m.append(m_ref[part, :])
        m = llb(m, field, target[...])
        for c in range(3):
            out[pl.ds(c * n_tiles, n_tiles), :] = m[c]

    return pl.pallas_call(
        kernel,
        out_shape=jax.ShapeDtypeStruct((3 * n_tiles, LANES), F32),
        in_specs=[VM] * 7,
        out_specs=VM,
        compiler_params=pltpu.CompilerParams(vmem_limit_bytes=SMALL),
        cost_estimate=cost(10**7, 2**20),
        name="section_last",
    )


def shifted(v, axis, by):
    n = lax.axis_size(axis)
    return lax.ppermute(v, axis, [(i, (i + by) % n) for i in range(n)])


def traded(to_a, to_b, axis):
    n = lax.axis_size(axis)
    first = [(i, i ^ 1) for i in range(n)]
    second = [(i, (i + 1) % n if i % 2 else (i - 1) % n) for i in range(n)]
    return lax.ppermute(to_a, axis, first), lax.ppermute(to_b, axis, second)


def cells_call(rows):
    def kernel(asked, ex, cells):
        cells[...] = asked[...].astype(jnp.int32)

    return pl.pallas_call(
        kernel, out_shape=jax.ShapeDtypeStruct((rows, LANES), jnp.int32), in_specs=[VM, ANY], out_specs=VM,
        compiler_params=pltpu.CompilerParams(vmem_limit_bytes=SMALL),
        cost_estimate=cost(10**9, 4 * 2**20), name="cells",
    )


def per_device(
    potential, source, depth_kernel, magnet, footprint, temp_index, temp_profile, self_tiles, next_tiles
):
    nx, ny, nz = potential.shape
    n_track = lax.axis_size("track")
    n_tiles = self_tiles.shape[1]
    grains = footprint.shape[1]
    cap = 2 * grains // n_track
    state = magnet.reshape(3 * n_tiles, LANES)

    head_a, head_b, track_lo, track_hi = pack_call(nx, ny, nz)(potential, source)
    head_a, head_b = ends_call(ny, n_tiles)(state, head_a, head_b)
    from_a, from_b = traded(head_a, head_b, "head")
    requests, slots, target = request_call(n_track, n_tiles, nx * ny, ny, cap)(
        footprint.reshape(n_tiles, LANES), temp_index.reshape(n_tiles, LANES), temp_profile[None, :]
    )
    track_lo, track_hi = corner_call(nx, ny, nz)(track_lo, track_hi, from_a, from_b)
    left = shifted(track_hi, "track", 1)
    right = shifted(track_lo, "track", -1)
    asked = lax.all_to_all(requests.reshape(n_track, cap // LANES, LANES), "track", 0, 0)

    kern = jnp.pad(depth_kernel, ((0, 5), (0, 0)))
    half = n_tiles // 2
    couplings = (self_tiles[0], next_tiles[0], state, from_a, from_b)
    q_inner, token = inner_call(nx, ny, nz)(potential, source, from_a, from_b)
    asked = cells_call(n_track * cap // LANES)(asked.reshape(n_track * cap // LANES, LANES), token)
    relaxed, reply = relax_call(nx, ny, nz, n_track, cap)(
        potential, source, from_a, from_b, left, right, track_lo, track_hi, kern,
        asked, q_inner,
    )
    answers = lax.all_to_all(reply, "track", 0, 0)
    ex_a = first_call(n_tiles, ny, 0, half)(*couplings)
    ex_b = first_call(n_tiles, ny, half, n_tiles - half)(*couplings)
    applied, state, edge_a, edge_b = section_call(n_tiles, n_track, cap)(
        answers, slots, state, ex_a, ex_b, target
    )
    tile_a, tile_b = traded(edge_a, edge_b, "head")
    ex = second_call(n_tiles)(self_tiles[0], next_tiles[0], state)
    state = last_call(n_tiles)(
        state, ex, applied, target, tile_a, tile_b, next_tiles[0]
    )
    return relaxed, state.reshape(3, 1, grains)


def solution(mesh):
    in_specs = (
        P("head", "track", None),
        P("head", "track", None),
        P(),
        P(None, "track", "head"),
        P("track", "head"),
        P("track", "head"),
        P(),
        P("track", "head", None, None),
        P("track", "head", None, None),
    )
    out_specs = (P("head", "track", None), P(None, "track", "head"))
    return jax.shard_map(
        per_device, mesh=mesh, in_specs=in_specs, out_specs=out_specs, check_vma=False
    )
```
